512 devices in a mesh: sweep: 16 (over x, y_lo), azim: 32 (over y_hi, z, core).
Axes of the slice: x: 4, y: 8 (y_hi: 2, y_lo: 4; y = y_hi * 4 + y_lo), z: 8, core: 2. Of those that a mesh axis runs over, the one named last changes fastest.
Arguments:
- latents: bfloat16 [32, 8, 1024, 512], P('sweep', None, 'azim'), may hold values from -6 to 6
- cotangent: bfloat16 [32, 8, 1024, 512], P('sweep', None, 'azim'), may hold values from -6 to 6
- conv_kernel: float32 [9, 512], replicated, may hold values from -2 to 2
- conv_bias: float32 [512], replicated, may hold values from -3 to 3
- norm_gain: float32 [512], replicated, may hold values from 0.25 to 1.75
- w_query: bfloat16 [512, 256], replicated, may hold values from -2 to 2
- w_key: bfloat16 [512, 256], replicated, may hold values from -2 to 2
- w_value: bfloat16 [512, 256], replicated, may hold values from -0.25 to 0.25
- w_output: bfloat16 [512, 256], replicated, may hold values from -0.375 to 0.375
Outputs:
- grad_latents: float32 [32, 8, 1024, 512], P('sweep', None, 'azim')
- grad_kernel: float32 [9, 512], replicated
- grad_bias: float32 [512], replicated
- grad_gain: float32 [512], replicated
- grad_query: float32 [512, 256], P('azim')
- grad_key: float32 [512, 256], P('azim')
- grad_value: float32 [512, 256], P('azim')
- grad_output: float32 [512, 256], P('azim')
The draws below stay inside these ranges and needn't reach their ends.
All inputs are finite; a program needn't handle non-finite values.
Results may differ from the reference program's by a relative error of at most 0.01.
The reference program's roundings to bfloat16 on the way count: a program that leaves them out, or rounds other values in their place, can miss the bound.
Values may be sent and summed in bfloat16 or wider, within the bound.
No kernel may reach another device: no remote copies, remote signals or barrier semaphores. Data moves between devices by JAX's collectives and lax.ppermute only.
A program may use at most 64 MiB of HBM per device.

```python
import math
import jax
import jax.numpy as jnp
from jax import lax

C = 512
HEADS = 4
DH = 64
H = 8
SWEEPS = 32
W = 1024
HD = 256
N_AZIM = 32


def projection_draw(key, salt):
    base = jax.random.normal(jax.random.fold_in(key, salt), (C, HEADS * DH), jnp.float32)
    base = jnp.clip(base, -4.0, 4.0) * C ** (-0.5)
    head_scale = jax.random.uniform(jax.random.fold_in(key, 7), (HEADS,), jnp.float32, 0.8, 1.25)
    columns = jnp.repeat(head_scale, DH)
    return jnp.clip(base * columns, -2.0, 2.0).astype(jnp.bfloat16)


def draw_w_query(key, part):
    return projection_draw(key, 11)


def draw_w_key(key, part):
    return projection_draw(key, 13)


def with_spikes(values, key, source, target, parts, factor):
    def block_of(dim):
        return (jnp.arange(values.shape[dim]) // (values.shape[dim] // parts)).reshape((-1,) + (1,) * (values.ndim - 1 - dim))

    one_side = jax.random.permutation(key, parts)[block_of(target)]
    second = (block_of(target) + parts // 2) % parts
    return jnp.where((block_of(source) == one_side) | (block_of(source) == second), factor * values, values)


def block_levels(stream_key, dims, split, least, largest):
    gain = 1.0
    for axis_at, parts in split:
        heights = jax.random.uniform(jax.random.fold_in(jax.random.fold_in(stream_key, 6), axis_at), (parts,), jnp.float32, least / len(split), largest / len(split))
        gain = gain * jnp.repeat(jnp.exp(heights), dims[axis_at] // parts).reshape((-1,) + (1,) * (len(dims) - 1 - axis_at))
    return gain


def gaussian(own_key, dims, spread, reach, pieces=(), kind=jnp.bfloat16):
    level = block_levels(own_key, dims, pieces, -0.22, 0.18) if pieces else 1.0
    entries = jax.random.normal(own_key, dims, jnp.float32) * spread * level
    return jnp.minimum(jnp.maximum(entries, -reach), reach).astype(kind)


def heavy_noise(rng, extent, scale, reach, shards, heavy, kind=jnp.bfloat16):
    values = scale * jax.random.normal(rng, extent, jnp.float32)
    if shards:
        values = values * block_levels(rng, extent, shards, -0.22, 0.18)
    return jnp.clip(with_spikes(values, jax.random.fold_in(rng, 3), *heavy), -reach, reach).astype(kind)


def setup_inputs(seed: int = 0) -> dict:
    key_list = jax.random.split(jax.random.key(seed), 10)
    return {
        "latents": gaussian(key_list[0], (SWEEPS, H, W, C), 1.0, 6.0, ((0, 16), (2, 32))),
        "cotangent": heavy_noise(key_list[1], (SWEEPS, H, W, C), 1.0, 6.0, ((0, 16), (2, 32)), (2, 3, 32, 2.75)),
        "conv_kernel": gaussian(key_list[2], (9, C), 0.35, 2.0, (), jnp.float32),
        "conv_bias": gaussian(key_list[3], (C,), 0.5, 3.0, (), jnp.float32),
        "norm_gain": jnp.clip(1.0 + 0.15 * jax.random.normal(key_list[4], (C,), jnp.float32), 0.25, 1.75),
        "w_query": draw_w_query(jax.random.fold_in(key_list[9], 71), 0),
        "w_key": draw_w_key(jax.random.fold_in(key_list[9], 71), 0),
        "w_value": gaussian(key_list[7], (C, HD), C ** -0.5, 0.25),
        "w_output": gaussian(key_list[8], (C, HD), HD ** -0.5, 0.375),
    }


EPS = 1e-06

def silu_slope(value):
    sigmoid_val = jax.nn.sigmoid(value)
    return sigmoid_val * (1.0 + value * (1.0 - sigmoid_val))

def frame_sweep(field):
    padded = jnp.pad(field, ((1, 1), (0, 0), (0, 0)))
    return jnp.concatenate([padded[:, -1:], padded, padded[:, :1]], axis=1)

def forward_sweep(latent_one, conv_kernel, conv_bias):
    height, width = (latent_one.shape[0], latent_one.shape[1])
    framed = frame_sweep(jax.nn.silu(latent_one.astype(jnp.float32)))
    conv_sum = jnp.zeros(latent_one.shape, jnp.float32)
    for row_tap in range(3):
        for col_tap in range(3):
            conv_sum = conv_sum + conv_kernel[3 * row_tap + col_tap] * framed[row_tap:row_tap + height, col_tap:col_tap + width]
    return (latent_one.astype(jnp.float32) + conv_sum + conv_bias).astype(jnp.bfloat16)

def attend(y_block, cot_block, w_query, w_key, w_value, w_output, norm_gain):
    sweeps, pixels, channels = y_block.shape
    heads = w_query.shape[1] // DH
    scale = 1.0 / math.sqrt(DH)
    y_float = y_block.astype(jnp.float32)
    root = jnp.sqrt(lax.optimization_barrier(jnp.mean(y_float * y_float, axis=-1, keepdims=True)) + EPS)
    inverse = 1.0 / root
    normed = (y_float * inverse * norm_gain).astype(jnp.bfloat16)
    rows = normed.reshape(sweeps * pixels, channels)
    query = jnp.dot(rows, w_query, preferred_element_type=jnp.float32).astype(jnp.bfloat16)
    key = jnp.dot(rows, w_key, preferred_element_type=jnp.float32).astype(jnp.bfloat16)
    value = jnp.dot(rows, w_value, preferred_element_type=jnp.float32).astype(jnp.bfloat16)
    query4 = query.reshape(sweeps, pixels, heads, DH).astype(jnp.float32)
    key4 = key.reshape(sweeps, pixels, heads, DH).astype(jnp.float32)
    value4 = value.reshape(sweeps, pixels, heads, DH).astype(jnp.float32)
    scores = jnp.einsum('tphd,uphd->phtu', query4, key4) * scale
    row_max = lax.optimization_barrier(jnp.max(scores, axis=-1, keepdims=True))
    expon = jnp.exp(scores - row_max)
    probs = expon / lax.optimization_barrier(jnp.sum(expon, axis=-1, keepdims=True))
    probs_low = probs.astype(jnp.bfloat16)
    attended = jnp.einsum('phtu,uphd->tphd', probs_low.astype(jnp.float32), value4).astype(jnp.bfloat16)
    attended_rows = attended.reshape(sweeps * pixels, heads * DH)
    cot_rows = cot_block.reshape(sweeps * pixels, channels)
    grad_output = jnp.dot(cot_rows.T, attended_rows, preferred_element_type=jnp.float32)
    grad_attended = jnp.dot(cot_rows, w_output, preferred_element_type=jnp.float32).astype(jnp.bfloat16)
    grad_att4 = grad_attended.reshape(sweeps, pixels, heads, DH).astype(jnp.float32)
    grad_probs = jnp.einsum('tphd,uphd->phtu', grad_att4, value4)
    grad_scores = (probs * (grad_probs - lax.optimization_barrier(jnp.sum(probs * grad_probs, axis=-1, keepdims=True))) * scale).astype(jnp.bfloat16)
    grad_v = jnp.einsum('phtu,tphd->uphd', probs_low.astype(jnp.float32), grad_att4).astype(jnp.bfloat16)
    grad_q = jnp.einsum('phtu,uphd->tphd', grad_scores.astype(jnp.float32), key4).astype(jnp.bfloat16)
    grad_k = jnp.einsum('phtu,tphd->uphd', grad_scores.astype(jnp.float32), query4).astype(jnp.bfloat16)
    grad_q = grad_q.reshape(sweeps * pixels, heads * DH)
    grad_k = grad_k.reshape(sweeps * pixels, heads * DH)
    grad_v = grad_v.reshape(sweeps * pixels, heads * DH)
    grad_query = jnp.dot(rows.T, grad_q, preferred_element_type=jnp.float32)
    grad_key = jnp.dot(rows.T, grad_k, preferred_element_type=jnp.float32)
    grad_value = jnp.dot(rows.T, grad_v, preferred_element_type=jnp.float32)
    grad_normed = jnp.dot(jnp.concatenate([grad_q, grad_k, grad_v], axis=-1), jnp.concatenate([w_query, w_key, w_value], axis=-1).T, preferred_element_type=jnp.float32)
    grad_normed = grad_normed.reshape(sweeps, pixels, channels)
    grad_gain = lax.optimization_barrier(jnp.sum(grad_normed * y_float * inverse, axis=(0, 1)))
    gained = grad_normed * norm_gain
    grad_attn = (inverse * (gained - y_float * lax.optimization_barrier(jnp.mean(gained * y_float, axis=-1, keepdims=True)) * inverse * inverse)).astype(jnp.bfloat16)
    return (grad_attn, grad_query, grad_key, grad_value, grad_output, grad_gain)

def reference(latents, cotangent, conv_kernel, conv_bias, norm_gain, w_query, w_key, w_value, w_output):
    sweeps, height, width, channels = latents.shape
    inner = w_query.shape[1]
    y_all = lax.map(lambda one: forward_sweep(one, conv_kernel, conv_bias), latents)
    blocks = N_AZIM
    block_pixels = height * width // blocks
    y_blocks = y_all.reshape(sweeps, blocks, block_pixels, channels).transpose(1, 0, 2, 3)
    cot_blocks = cotangent.reshape(sweeps, blocks, block_pixels, channels).transpose(1, 0, 2, 3)

    def step(carry, item):
        result = attend(item[0], item[1], w_query, w_key, w_value, w_output, norm_gain)
        carry = tuple((carry[idx] + result[idx + 1] for idx in range(5)))
        return (carry, result[0])
    zero_mat = jnp.zeros((channels, inner), jnp.float32)
    init = (zero_mat, zero_mat, zero_mat, zero_mat, jnp.zeros((channels,), jnp.float32))
    sums, grad_attn = lax.scan(step, init, (y_blocks, cot_blocks))
    grad_attn = grad_attn.transpose(1, 0, 2, 3).reshape(sweeps, height, width, channels)

    def backward_sweep(item):
        latent_one, cot_one, attn_one = item
        grad_y = cot_one.astype(jnp.float32) + attn_one.astype(jnp.float32)
        framed_act = frame_sweep(jax.nn.silu(latent_one.astype(jnp.float32)))
        framed_grad = frame_sweep(grad_y)
        grad_act = jnp.zeros(grad_y.shape, jnp.float32)
        taps = []
        for row_tap in range(3):
            for col_tap in range(3):
                weight = conv_kernel[3 * row_tap + col_tap]
                grad_act = grad_act + weight * framed_grad[2 - row_tap:2 - row_tap + height, 2 - col_tap:2 - col_tap + width]
                taps.append(lax.optimization_barrier(jnp.sum(grad_y * framed_act[row_tap:row_tap + height, col_tap:col_tap + width], axis=(0, 1))))
        latent_float = latent_one.astype(jnp.float32)
        grad_lat = grad_y + grad_act * silu_slope(latent_float)
        return (grad_lat, jnp.stack(taps), lax.optimization_barrier(jnp.sum(grad_y, axis=(0, 1))))
    grad_latents, tap_terms, bias_terms = lax.map(backward_sweep, (latents, cotangent, grad_attn))
    predivide = 1.0 / math.sqrt(sweeps * height * width)
    grad_kernel = lax.optimization_barrier(jnp.sum(tap_terms, axis=0)) * predivide
    grad_bias = lax.optimization_barrier(jnp.sum(bias_terms, axis=0)) * predivide
    return (grad_latents, grad_kernel, grad_bias, sums[4] * predivide, sums[0] * predivide, sums[1] * predivide, sums[2] * predivide, sums[3] * predivide)
```

```python
import functools
import math

import jax
import jax.numpy as jnp
from jax import lax
from jax.experimental import pallas as pl
from jax.experimental.pallas import tpu as pltpu
from jax.sharding import PartitionSpec as P

DH = 64
EPS = 1e-06
F32 = jnp.float32
BF16 = jnp.bfloat16
MASKED = -1e30

SL, H, WL, C = 2, 8, 32, 512
GROUPS = 16
PX = 16
HD = 256
LANES = 128
PARTS = C // LANES


def params(mib):
    return pltpu.CompilerParams(vmem_limit_bytes=mib * 1024 * 1024)


def call(kernel, outs, mib, flops=0, moved=0, scratch=(), smem=0):
    vmem = pl.BlockSpec(memory_space=pltpu.VMEM)

    def run(*args):
        specs = [pl.BlockSpec(memory_space=pltpu.SMEM)] * smem + [vmem] * (len(args) - smem)
        return pl.pallas_call(
            kernel,
            out_shape=outs,
            in_specs=specs,
            out_specs=jax.tree.map(lambda _: vmem, outs),
            scratch_shapes=list(scratch),
            compiler_params=params(mib),
            cost_estimate=pl.CostEstimate(
                flops=flops, bytes_accessed=moved, transcendentals=0
            ),
        )(*args)

    return run


def struct(shape, dtype):
    return jax.ShapeDtypeStruct(shape, dtype)


def silu(value):
    return value / (1.0 + jnp.exp(-value))


def nt(left, right):
    return lax.dot_general(left, right, (((1,), (1,)), ((), ())), preferred_element_type=F32)


def tn(left, right):
    return lax.dot_general(left, right, (((0,), (0,)), ((), ())), preferred_element_type=F32)


def nn(left, right):
    return lax.dot_general(left, right, (((1,), (0,)), ((), ())), preferred_element_type=F32)


def lanes_of(part):
    return pl.ds(pl.multiple_of(part * LANES, LANES), LANES)


def row_index(rows):
    return lax.broadcasted_iota(jnp.int32, (rows, LANES), 0)


def row_shifts(value):
    at = lax.broadcasted_iota(jnp.int32, value.shape, 0)
    below = jnp.where(at == 0, 0.0, pltpu.roll(value, 1, 0))
    above = jnp.where(at == H - 1, 0.0, pltpu.roll(value, H - 1, 0))
    return below, value, above


def forward_kernel(lat, cot, left, right, taps, bias, out, edge_l, edge_r):
    for s in range(SL):
        shifted = row_shifts(silu(left[0, s].astype(F32)))
        edge_l[s] = sum(taps[3 * a : 3 * a + 1, :] * shifted[a] for a in range(3))
        shifted = row_shifts(silu(right[0, s].astype(F32)))
        edge_r[s] = sum(taps[3 * a + 2 : 3 * a + 3, :] * shifted[a] for a in range(3))
    rows = row_index(WL)

    @pl.loop(0, SL * PARTS)
    def _(step):
        s = step // PARTS
        here = lanes_of(step % PARTS)
        tap = [taps[t : t + 1, here] for t in range(9)]
        base = bias[:, here]
        values = [lat[s, h, :, here].astype(F32) for h in range(H)]
        acts = [silu(v) for v in values]
        for h in range(H):
            cols = []
            for b in range(3):
                terms = [
                    tap[3 * a + b] * acts[h + a - 1] for a in range(3) if 0 <= h + a - 1 < H
                ]
                cols.append(functools.reduce(jnp.add, terms))
            from_left = jnp.where(
                rows == 0, edge_l[s, h : h + 1, here], pltpu.roll(cols[0], 1, 0)
            )
            from_right = jnp.where(
                rows == WL - 1, edge_r[s, h : h + 1, here], pltpu.roll(cols[2], WL - 1, 0)
            )
            y = (values[h] + (cols[1] + from_left + from_right) + base).astype(BF16)
            out[2 * h, 0, s, :, here] = y[:PX]
            out[2 * h + 1, 0, s, :, here] = y[PX:]
            moved = cot[s, h, :, here]
            out[2 * h, 1, s, :, here] = moved[:PX]
            out[2 * h + 1, 1, s, :, here] = moved[PX:]


def pair_up(first, second):
    low = lax.broadcasted_iota(jnp.int32, first.shape, 1) < 4
    return (
        jnp.where(low, first, pltpu.roll(second, 4, 1)),
        jnp.where(low, pltpu.roll(first, 4, 1), second),
    )


def attend_kernel(
    recv, w_query, w_key, w_value, w_output, gain,
    out, normed, stacked, attended, cot, gain_sum,
    y_rows, inv_rows, qkv, gatt, gnorm,
):
    rows_each = GROUPS * 8
    scale = 1.0 / math.sqrt(DH)
    for tile in range(2):
        y_two = [
            recv[:, 0, s].astype(F32)[:, 8 * tile : 8 * tile + 8, :] for s in range(SL)
        ]
        cot_two = [
            recv[:, 1, s].astype(F32)[:, 8 * tile : 8 * tile + 8, :] for s in range(SL)
        ]
        for half, (y, c) in enumerate(zip(pair_up(*y_two), pair_up(*cot_two))):
            at = pl.ds((2 * tile + half) * rows_each, rows_each)
            y = y.reshape(rows_each, C)
            inverse = lax.rsqrt(jnp.sum(y * y, axis=-1, keepdims=True) * (1.0 / C) + EPS)
            y_rows[at, :] = y
            inv_rows[at, :] = jnp.broadcast_to(inverse, (rows_each, LANES))
            normed[at, :] = (y * inverse * gain[...]).astype(BF16)
            cot[at, :] = c.reshape(rows_each, C).astype(BF16)
    for index, weight in enumerate((w_query, w_key, w_value)):
        qkv[:, index * HD : (index + 1) * HD] = nn(normed[...], weight[...]).astype(BF16)
    gatt[...] = nn(cot[...], w_output[...]).astype(BF16)

    square = (rows_each, rows_each)
    same = (lax.broadcasted_iota(jnp.int32, square, 0) % 4) == (
        lax.broadcasted_iota(jnp.int32, square, 1) % 4
    )
    lane = lax.broadcasted_iota(jnp.int32, (rows_each, LANES), 1)

    def split(value):
        zero = jnp.zeros_like(value)
        return jnp.concatenate(
            [jnp.where(lane < DH, value, zero), jnp.where(lane >= DH, value, zero)], axis=0
        )

    for group in range(4):
        at = pl.ds(group * rows_each, rows_each)
        for pair in range(2):
            def part(index):
                return qkv[at, pl.ds(index * HD + pair * LANES, LANES)]

            lanes = pl.ds(pair * LANES, LANES)
            query, key, value = part(0), part(1), part(2)
            grad_att = gatt[at, lanes]
            key2, value2 = split(key), split(value)
            scores = nt(query, key2)
            grad_probs = nt(grad_att, value2)
            lows, grads = [], []
            for head in range(2):
                cut = slice(head * rows_each, (head + 1) * rows_each)
                score = jnp.where(same, scores[:, cut] * scale, MASKED)
                expon = jnp.exp(score - jnp.max(score, axis=-1, keepdims=True))
                probs = expon * (1.0 / jnp.sum(expon, axis=-1, keepdims=True))
                gp = grad_probs[:, cut]
                weighted = probs * gp
                total = jnp.sum(weighted, axis=-1, keepdims=True)
                lows.append(probs.astype(BF16))
                grads.append(((weighted - probs * total) * scale).astype(BF16))
            attended[at, lanes] = nn(jnp.concatenate(lows, axis=1), value2).astype(BF16)
            grad_q = nn(jnp.concatenate(grads, axis=1), key2)
            grad_k = tn(jnp.concatenate(grads, axis=0), split(query))
            grad_v = tn(jnp.concatenate(lows, axis=0), split(grad_att))
            for index, grad in enumerate((grad_q, grad_k, grad_v)):
                stacked[at, pl.ds(index * HD + pair * LANES, LANES)] = grad.astype(BF16)

    gnorm[...] = (
        nt(stacked[:, :HD], w_query[...])
        + nt(stacked[:, HD : 2 * HD], w_key[...])
        + nt(stacked[:, 2 * HD :], w_value[...])
    )
    total = jnp.zeros((8, C), F32)
    for tile in range(2):
        halves = []
        for half in range(2):
            at = pl.ds((2 * tile + half) * rows_each, rows_each)
            y = y_rows[at, :]
            inverse = inv_rows[at, :][:, :1]
            grad = gnorm[at, :]
            total = total + jnp.sum((grad * y * inverse).reshape(GROUPS, 8, C), axis=0)
            gained = grad * gain[...]
            mean = jnp.sum(gained * y, axis=-1, keepdims=True) * (1.0 / C)
            result = inverse * (gained - y * (mean * inverse * inverse))
            halves.append(result.reshape(GROUPS, 8, C))
        for s, whole in enumerate(pair_up(*halves)):
            out[:, s, 8 * tile : 8 * tile + 8, :] = whole.astype(BF16)
    gain_sum[...] = jnp.sum(total, axis=0, keepdims=True)


def weights_kernel(predivide, core, normed, stacked, attended, cot, out):
    mine = core[0]
    for m in range(4):
        if m < 3:
            whole = tn(normed[...], stacked[:, m * HD : (m + 1) * HD])
        else:
            whole = tn(cot[...], attended[...])
        tiles = (whole * predivide).reshape(16, 2, 2, 8, HD)
        for which in range(2):
            slot = (mine + which) % 2
            for high in range(2):
                for side in range(2):
                    piece = tiles[:, which, high, :, side * LANES : (side + 1) * LANES]
                    out[slot, 4 * m + 2 * high + side] = piece.reshape(LANES, LANES).astype(BF16)


def taps_kernel(predivide, lat, left, right, cot, ret, gain_sum, kept, got, out, edge_l, edge_r, tiles):
    tiles[...] = jnp.zeros_like(tiles)
    for s in range(SL):
        edge_l[s] = silu(left[0, s].astype(F32))
        edge_r[s] = silu(right[0, s].astype(F32))
    rows = row_index(WL)

    @pl.loop(0, PARTS)
    def _(part):
        here = lanes_of(part)
        sums = [jnp.zeros((8, LANES), F32) for _ in range(10)]
        for s in range(SL):
            grads, cols = [], []
            for h in range(H):
                back = jnp.concatenate(
                    [ret[2 * h, s, :, here].astype(F32), ret[2 * h + 1, s, :, here].astype(F32)],
                    axis=0,
                )
                grads.append(cot[s, h, :, here].astype(F32) + back)
                act = silu(lat[s, h, :, here].astype(F32))
                cols.append(
                    (
                        jnp.where(rows == 0, edge_l[s, h : h + 1, here], pltpu.roll(act, 1, 0)),
                        act,
                        jnp.where(
                            rows == WL - 1, edge_r[s, h : h + 1, here], pltpu.roll(act, WL - 1, 0)
                        ),
                    )
                )
            for h in range(H):
                for a in range(3):
                    if 0 <= h + a - 1 < H:
                        for b in range(3):
                            term = (grads[h] * cols[h + a - 1][b]).reshape(4, 8, LANES)
                            sums[3 * a + b] = sums[3 * a + b] + jnp.sum(term, axis=0)
                sums[9] = sums[9] + jnp.sum(grads[h].reshape(4, 8, LANES), axis=0)
        for r in range(10):
            tiles[4 * part + r // 3, pl.ds(r % 3, 1), :] = jnp.sum(sums[r], axis=0, keepdims=True)
        tiles[4 * part + 3, pl.ds(1, 1), :] = gain_sum[:, here]

    whole = tiles[...] * predivide
    high = whole.astype(BF16).astype(F32)
    out[:, LANES:, :] = jnp.concatenate([high, whole - high], axis=1).astype(BF16)
    out[:, :LANES, :] = (kept[0].astype(F32) + got[...].astype(F32)).astype(BF16)


def latents_kernel(lat, cot, ret, left, right, back_l, back_r, taps, out, edge_l, edge_r):
    for s in range(SL):
        below, here, above = row_shifts(left[1, s].astype(F32) + back_l[s].astype(F32))
        edge_l[s] = taps[2:3, :] * above + taps[5:6, :] * here + taps[8:9, :] * below
        below, here, above = row_shifts(right[1, s].astype(F32) + back_r[s].astype(F32))
        edge_r[s] = taps[0:1, :] * above + taps[3:4, :] * here + taps[6:7, :] * below
    rows = row_index(WL)

    @pl.loop(0, SL * PARTS)
    def _(step):
        s = step // PARTS
        here = lanes_of(step % PARTS)
        tap = [taps[t : t + 1, here] for t in range(9)]
        grads = []
        for h in range(H):
            back = jnp.concatenate(
                [ret[2 * h, s, :, here].astype(F32), ret[2 * h + 1, s, :, here].astype(F32)],
                axis=0,
            )
            grads.append(cot[s, h, :, here].astype(F32) + back)
        for h in range(H):
            cols = []
            for b in range(3):
                terms = [
                    tap[3 * a + b] * grads[h - a + 1] for a in range(3) if 0 <= h - a + 1 < H
                ]
                cols.append(functools.reduce(jnp.add, terms))
            from_left = jnp.where(
                rows == 0, edge_l[s, h : h + 1, here], pltpu.roll(cols[2], 1, 0)
            )
            from_right = jnp.where(
                rows == WL - 1, edge_r[s, h : h + 1, here], pltpu.roll(cols[0], WL - 1, 0)
            )
            total = cols[1] + from_left + from_right
            value = lat[s, h, :, here].astype(F32)
            sig = 1.0 / (1.0 + jnp.exp(-value))
            out[s, h, :, here] = grads[h] + total * (sig * (1.0 + value * (1.0 - sig)))


def second_kernel(core, recv, out):
    total = jnp.sum(recv[...].astype(F32), axis=0)
    weights = total[:LANES].reshape(16, 8, LANES)
    taps = total[LANES : LANES + 8] + total[LANES + 8 :]
    high = taps.astype(BF16).astype(F32)
    low = taps - high
    at = lax.broadcasted_iota(jnp.int32, (8, LANES), 0)
    both = jnp.where(at < 4, high, pltpu.roll(low, 4, 0))
    for which in range(2):
        own = jnp.where(core[0] == which, 1.0, 0.0)
        for z in range(16):
            out[2 * z + which] = jnp.concatenate([weights[z] * own, both], axis=0).astype(BF16)


def third_kernel(recv, out):
    total = jnp.sum(recv[...].astype(F32), axis=0)
    both = total[8:]
    taps = both + pltpu.roll(both, 4, 0)
    result = jnp.concatenate([total[:8], taps], axis=0)
    for s in range(GROUPS):
        out[s] = result


def unpack_kernel(recv, kernel_out, bias_out, gain_out, *outs):
    for part in range(PARTS):
        here = slice(part * LANES, (part + 1) * LANES)
        for r in range(11):
            row = recv[4 * part + r // 3, 8 + r % 3 : 9 + r % 3, :]
            if r < 9:
                kernel_out[r : r + 1, here] = row
            elif r == 9:
                bias_out[:, here] = row
            else:
                gain_out[:, here] = row
    for m in range(4):
        for high in range(2):
            for side in range(2):
                outs[m][8 * high : 8 * high + 8, side * LANES : (side + 1) * LANES] = recv[
                    4 * m + 2 * high + side, :8, :
                ]


def on_device(
    latents, cotangent, conv_kernel, conv_bias, norm_gain, w_query, w_key, w_value, w_output
):
    strips = lax.axis_size("azim")
    groups = lax.axis_size("sweep")
    up = [(i, (i + 1) % strips) for i in range(strips)]
    down = [(j, i) for i, j in up]
    pair = [(i, i ^ 1) for i in range(strips)]
    core = (lax.axis_index("azim") % 2).astype(jnp.int32).reshape(1)
    predivide = 1.0 / math.sqrt(SL * groups * H * WL * strips)
    bias_row = conv_bias.reshape(1, C)
    gain_row = norm_gain.reshape(1, C)
    edge = pltpu.VMEM((SL, H, C), F32)

    last = jnp.stack([latents[:, :, WL - 1, :], cotangent[:, :, WL - 1, :]])
    first = jnp.stack([latents[:, :, 0, :], cotangent[:, :, 0, :]])
    left = lax.ppermute(last, "azim", up)
    right = lax.ppermute(first, "azim", down)

    sent = call(
        forward_kernel,
        struct((GROUPS, 2, SL, PX, C), BF16),
        16,
        flops=10_000_000,
        moved=2_000_000,
        scratch=[edge, edge],
    )(latents, cotangent, left, right, conv_kernel, bias_row)
    recv = lax.all_to_all(sent, "sweep", split_axis=0, concat_axis=0, tiled=True)

    rows = GROUPS * SL * PX
    grad_attn, normed, stacked, attended, cot_rows, gain_sum = call(
        attend_kernel,
        (
            struct((GROUPS, SL, PX, C), BF16),
            struct((rows, C), BF16),
            struct((rows, 3 * HD), BF16),
            struct((rows, HD), BF16),
            struct((rows, C), BF16),
            struct((1, C), F32),
        ),
        32,
        flops=2_000_000_000,
        moved=6_000_000,
        scratch=[
            pltpu.VMEM((rows, C), F32),
            pltpu.VMEM((rows, LANES), F32),
            pltpu.VMEM((rows, 3 * HD), BF16),
            pltpu.VMEM((rows, HD), BF16),
            pltpu.VMEM((rows, C), F32),
        ],
    )(recv, w_query, w_key, w_value, w_output, gain_row)
    ret = lax.all_to_all(grad_attn, "sweep", split_axis=0, concat_axis=0, tiled=True)

    halves = call(
        functools.partial(weights_kernel, predivide),
        struct((2, GROUPS, LANES, LANES), BF16),
        24,
        flops=600_000_000,
        moved=4_000_000,
        smem=1,
    )(core, normed, stacked, attended, cot_rows)
    got = lax.ppermute(halves[1], "azim", pair)

    back_last = ret[1::2, :, PX - 1, :].transpose(1, 0, 2)
    back_first = ret[0::2, :, 0, :].transpose(1, 0, 2)
    back_l = lax.ppermute(back_last, "azim", up)
    back_r = lax.ppermute(back_first, "azim", down)

    first_sent = call(
        functools.partial(taps_kernel, predivide),
        struct((GROUPS, LANES + 16, LANES), BF16),
        16,
        flops=10_000_000,
        moved=3_000_000,
        scratch=[edge, edge, pltpu.VMEM((GROUPS, 8, LANES), F32)],
    )(latents, left, right, cotangent, ret, gain_sum, halves, got)
    first_recv = lax.all_to_all(first_sent, "sweep", split_axis=0, concat_axis=0, tiled=True)

    grad_latents = call(
        latents_kernel,
        struct((SL, H, WL, C), F32),
        16,
        flops=10_000_000,
        moved=4_000_000,
        scratch=[edge, edge],
    )(latents, cotangent, ret, left, right, back_l, back_r, conv_kernel)

    second_sent = call(
        second_kernel, struct((strips, 16, LANES), BF16), 16, moved=1_000_000, smem=1
    )(core, first_recv)
    second_recv = lax.all_to_all(second_sent, "azim", split_axis=0, concat_axis=0, tiled=True)
    third_sent = call(third_kernel, struct((GROUPS, 16, LANES), F32), 16, moved=300_000)(
        second_recv
    )
    third_recv = lax.all_to_all(third_sent, "sweep", split_axis=0, concat_axis=0, tiled=True)
    share = struct((C // strips, HD), F32)
    line = struct((1, C), F32)
    grad_kernel, grad_bias, grad_gain, *shares = call(
        unpack_kernel,
        (struct((9, C), F32), line, line, share, share, share, share),
        16,
        moved=300_000,
    )(third_recv)
    return (
        grad_latents,
        grad_kernel,
        grad_bias.reshape(C),
        grad_gain.reshape(C),
        shares[0],
        shares[1],
        shares[2],
        shares[3],
    )


def solution(mesh):
    image = P("sweep", None, "azim", None)
    share = P("azim", None)
    return jax.shard_map(
        on_device,
        mesh=mesh,
        in_specs=(image, image, P(), P(), P(), P(), P(), P(), P()),
        out_specs=(image, P(), P(), P(), share, share, share, share),
        check_vma=False,
    )
```

```python
import functools
import math

import jax
import jax.numpy as jnp
from jax import lax
from jax.experimental import pallas as pl
from jax.experimental.pallas import tpu as pltpu
from jax.sharding import PartitionSpec as P

DH = 64
EPS = 1e-06
F32 = jnp.float32
BF16 = jnp.bfloat16
MASKED = -1e30

SL, H, WL, C = 2, 8, 32, 512
GROUPS = 16
PX = 16
HD = 256
LANES = 128
PARTS = C // LANES


def params(mib):
    return pltpu.CompilerParams(vmem_limit_bytes=mib * 1024 * 1024)


def call(kernel, outs, mib, flops=0, moved=0, scratch=(), smem=0):
    vmem = pl.BlockSpec(memory_space=pltpu.VMEM)

    def run(*args):
        specs = [pl.BlockSpec(memory_space=pltpu.SMEM)] * smem + [vmem] * (len(args) - smem)
        return pl.pallas_call(
            kernel,
            out_shape=outs,
            in_specs=specs,
            out_specs=jax.tree.map(lambda _: vmem, outs),
            scratch_shapes=list(scratch),
            compiler_params=params(mib),
            cost_estimate=pl.CostEstimate(
                flops=flops, bytes_accessed=moved, transcendentals=0
            ),
        )(*args)

    return run


def struct(shape, dtype):
    return jax.ShapeDtypeStruct(shape, dtype)


def silu(value):
    return value / (1.0 + jnp.exp(-value))


def nt(left, right):
    return lax.dot_general(left, right, (((1,), (1,)), ((), ())), preferred_element_type=F32)


def tn(left, right):
    return lax.dot_general(left, right, (((0,), (0,)), ((), ())), preferred_element_type=F32)


def nn(left, right):
    return lax.dot_general(left, right, (((1,), (0,)), ((), ())), preferred_element_type=F32)


def lanes_of(part):
    return pl.ds(pl.multiple_of(part * LANES, LANES), LANES)


def row_index(rows):
    return lax.broadcasted_iota(jnp.int32, (rows, LANES), 0)


def row_shifts(value):
    at = lax.broadcasted_iota(jnp.int32, value.shape, 0)
    below = jnp.where(at == 0, 0.0, pltpu.roll(value, 1, 0))
    above = jnp.where(at == H - 1, 0.0, pltpu.roll(value, H - 1, 0))
    return below, value, above


def start_kernel(lat, cot, packed, first, last, edges):
    for which, ref in enumerate((lat, cot)):
        for s in range(SL):
            for h in range(H):
                edges[0, which, s, h : h + 1, :] = ref[s, h, :PX, :].astype(F32)[:1]
                edges[1, which, s, h : h + 1, :] = ref[s, h, PX:, :].astype(F32)[PX - 1 :]
    first[...] = edges[0].astype(BF16)
    last[...] = edges[1].astype(BF16)
    for s in range(SL):
        for h in range(H):
            packed[2 * h, s] = cot[s, h, :PX, :]
            packed[2 * h + 1, s] = cot[s, h, PX:, :]


def forward_kernel(lat, left, right, taps, bias, out, edge_l, edge_r):
    for s in range(SL):
        shifted = row_shifts(silu(left[0, s].astype(F32)))
        edge_l[s] = sum(taps[3 * a : 3 * a + 1, :] * shifted[a] for a in range(3))
        shifted = row_shifts(silu(right[0, s].astype(F32)))
        edge_r[s] = sum(taps[3 * a + 2 : 3 * a + 3, :] * shifted[a] for a in range(3))
    rows = row_index(WL)

    @pl.loop(0, SL * PARTS)
    def _(step):
        s = step // PARTS
        here = lanes_of(step % PARTS)
        tap = [taps[t : t + 1, here] for t in range(9)]
        base = bias[:, here]
        values = [lat[s, h, :, here].astype(F32) for h in range(H)]
        acts = [silu(v) for v in values]
        for h in range(H):
            cols = []
            for b in range(3):
                terms = [
                    tap[3 * a + b] * acts[h + a - 1] for a in range(3) if 0 <= h + a - 1 < H
                ]
                cols.append(functools.reduce(jnp.add, terms))
            from_left = jnp.where(
                rows == 0, edge_l[s, h : h + 1, here], pltpu.roll(cols[0], 1, 0)
            )
            from_right = jnp.where(
                rows == WL - 1, edge_r[s, h : h + 1, here], pltpu.roll(cols[2], WL - 1, 0)
            )
            y = (values[h] + (cols[1] + from_left + from_right) + base).astype(BF16)
            out[2 * h, s, :, here] = y[:PX]
            out[2 * h + 1, s, :, here] = y[PX:]


def pair_up(first, second):
    low = lax.broadcasted_iota(jnp.int32, first.shape, 1) < 4
    return (
        jnp.where(low, first, pltpu.roll(second, 4, 1)),
        jnp.where(low, pltpu.roll(first, 4, 1), second),
    )


def attend_kernel(
    predivide, core, recv, recv_cot, w_query, w_key, w_value, w_output, gain,
    out, halves, gain_sum,
    normed, stacked, attended, cot, y_rows, inv_rows, qkv, gatt, gnorm,
):
    rows_each = GROUPS * 8
    scale = 1.0 / math.sqrt(DH)
    for tile in range(2):
        y_two = [
            recv[:, s].astype(F32)[:, 8 * tile : 8 * tile + 8, :] for s in range(SL)
        ]
        cot_two = [
            recv_cot[:, s].astype(F32)[:, 8 * tile : 8 * tile + 8, :] for s in range(SL)
        ]
        for half, (y, c) in enumerate(zip(pair_up(*y_two), pair_up(*cot_two))):
            at = pl.ds((2 * tile + half) * rows_each, rows_each)
            y = y.reshape(rows_each, C)
            inverse = lax.rsqrt(jnp.sum(y * y, axis=-1, keepdims=True) * (1.0 / C) + EPS)
            y_rows[at, :] = y
            inv_rows[at, :] = jnp.broadcast_to(inverse, (rows_each, LANES))
            normed[at, :] = (y * inverse * gain[...]).astype(BF16)
            cot[at, :] = c.reshape(rows_each, C).astype(BF16)
    for index, weight in enumerate((w_query, w_key, w_value)):
        qkv[:, index * HD : (index + 1) * HD] = nn(normed[...], weight[...]).astype(BF16)
    gatt[...] = nn(cot[...], w_output[...]).astype(BF16)

    square = (rows_each, rows_each)
    same = (lax.broadcasted_iota(jnp.int32, square, 0) % 4) == (
        lax.broadcasted_iota(jnp.int32, square, 1) % 4
    )
    lane = lax.broadcasted_iota(jnp.int32, (rows_each, LANES), 1)

    def split(value):
        zero = jnp.zeros_like(value)
        return jnp.concatenate(
            [jnp.where(lane < DH, value, zero), jnp.where(lane >= DH, value, zero)], axis=0
        )

    for group in range(4):
        at = pl.ds(group * rows_each, rows_each)
        for pair in range(2):
            def part(index):
                return qkv[at, pl.ds(index * HD + pair * LANES, LANES)]

            lanes = pl.ds(pair * LANES, LANES)
            query, key, value = part(0), part(1), part(2)
            grad_att = gatt[at, lanes]
            key2, value2 = split(key), split(value)
            scores = nt(query, key2)
            grad_probs = nt(grad_att, value2)
            lows, grads = [], []
            for head in range(2):
                cut = slice(head * rows_each, (head + 1) * rows_each)
                score = jnp.where(same, scores[:, cut] * scale, MASKED)
                expon = jnp.exp(score - jnp.max(score, axis=-1, keepdims=True))
                probs = expon * (1.0 / jnp.sum(expon, axis=-1, keepdims=True))
                gp = grad_probs[:, cut]
                weighted = probs * gp
                total = jnp.sum(weighted, axis=-1, keepdims=True)
                lows.append(probs.astype(BF16))
                grads.append(((weighted - probs * total) * scale).astype(BF16))
            attended[at, lanes] = nn(jnp.concatenate(lows, axis=1), value2).astype(BF16)
            grad_q = nn(jnp.concatenate(grads, axis=1), key2)
            grad_k = tn(jnp.concatenate(grads, axis=0), split(query))
            grad_v = tn(jnp.concatenate(lows, axis=0), split(grad_att))
            for index, grad in enumerate((grad_q, grad_k, grad_v)):
                stacked[at, pl.ds(index * HD + pair * LANES, LANES)] = grad.astype(BF16)

    gnorm[...] = (
        nt(stacked[:, :HD], w_query[...])
        + nt(stacked[:, HD : 2 * HD], w_key[...])
        + nt(stacked[:, 2 * HD :], w_value[...])
    )
    total = jnp.zeros((8, C), F32)
    for tile in range(2):
        results = []
        for half in range(2):
            at = pl.ds((2 * tile + half) * rows_each, rows_each)
            y = y_rows[at, :]
            inverse = inv_rows[at, :][:, :1]
            grad = gnorm[at, :]
            total = total + jnp.sum((grad * y * inverse).reshape(GROUPS, 8, C), axis=0)
            gained = grad * gain[...]
            mean = jnp.sum(gained * y, axis=-1, keepdims=True) * (1.0 / C)
            result = inverse * (gained - y * (mean * inverse * inverse))
            results.append(result.reshape(GROUPS, 8, C))
        for s, whole in enumerate(pair_up(*results)):
            out[:, s, 8 * tile : 8 * tile + 8, :] = whole.astype(BF16)
    gain_sum[...] = jnp.sum(total, axis=0, keepdims=True)

    mine = core[0]
    for m in range(4):
        if m < 3:
            whole = tn(normed[...], stacked[:, m * HD : (m + 1) * HD])
        else:
            whole = tn(cot[...], attended[...])
        tiles = (whole * predivide).reshape(16, 2, 2, 8, HD)
        for which in range(2):
            slot = (mine + which) % 2
            for high in range(2):
                for side in range(2):
                    piece = tiles[:, which, high, :, side * LANES : (side + 1) * LANES]
                    halves[slot, 4 * m + 2 * high + side] = piece.reshape(LANES, LANES).astype(BF16)


def taps_kernel(
    predivide, lat, left, right, cot, ret, gain_sum, kept, got,
    out, first, last, edge_l, edge_r, tiles, edges,
):
    tiles[...] = jnp.zeros_like(tiles)
    for s in range(SL):
        edge_l[s] = silu(left[0, s].astype(F32))
        edge_r[s] = silu(right[0, s].astype(F32))
    rows = row_index(WL)

    @pl.loop(0, PARTS)
    def _(part):
        here = lanes_of(part)
        sums = [jnp.zeros((8, LANES), F32) for _ in range(10)]
        for s in range(SL):
            grads, cols = [], []
            for h in range(H):
                back = jnp.concatenate(
                    [ret[2 * h, s, :, here].astype(F32), ret[2 * h + 1, s, :, here].astype(F32)],
                    axis=0,
                )
                grads.append(cot[s, h, :, here].astype(F32) + back)
                act = silu(lat[s, h, :, here].astype(F32))
                cols.append(
                    (
                        jnp.where(rows == 0, edge_l[s, h : h + 1, here], pltpu.roll(act, 1, 0)),
                        act,
                        jnp.where(
                            rows == WL - 1, edge_r[s, h : h + 1, here], pltpu.roll(act, WL - 1, 0)
                        ),
                    )
                )
            for h in range(H):
                for a in range(3):
                    if 0 <= h + a - 1 < H:
                        for b in range(3):
                            term = (grads[h] * cols[h + a - 1][b]).reshape(4, 8, LANES)
                            sums[3 * a + b] = sums[3 * a + b] + jnp.sum(term, axis=0)
                sums[9] = sums[9] + jnp.sum(grads[h].reshape(4, 8, LANES), axis=0)
        for r in range(10):
            tiles[4 * part + r // 3, pl.ds(r % 3, 1), :] = jnp.sum(sums[r], axis=0, keepdims=True)
        tiles[4 * part + 3, pl.ds(1, 1), :] = gain_sum[:, here]

    for s in range(SL):
        for h in range(H):
            edges[0, s, h : h + 1, :] = ret[2 * h, s].astype(F32)[:1]
            edges[1, s, h : h + 1, :] = ret[2 * h + 1, s].astype(F32)[PX - 1 :]
    first[...] = edges[0].astype(BF16)
    last[...] = edges[1].astype(BF16)
    whole = tiles[...] * predivide
    high = whole.astype(BF16).astype(F32)
    out[:, LANES:, :] = jnp.concatenate([high, whole - high], axis=1).astype(BF16)
    out[:, :LANES, :] = (kept[0].astype(F32) + got[...].astype(F32)).astype(BF16)


def latents_kernel(lat, cot, ret, left, right, back_l, back_r, taps, out, edge_l, edge_r):
    for s in range(SL):
        below, here, above = row_shifts(left[1, s].astype(F32) + back_l[s].astype(F32))
        edge_l[s] = taps[2:3, :] * above + taps[5:6, :] * here + taps[8:9, :] * below
        below, here, above = row_shifts(right[1, s].astype(F32) + back_r[s].astype(F32))
        edge_r[s] = taps[0:1, :] * above + taps[3:4, :] * here + taps[6:7, :] * below
    rows = row_index(WL)

    @pl.loop(0, SL * PARTS)
    def _(step):
        s = step // PARTS
        here = lanes_of(step % PARTS)
        tap = [taps[t : t + 1, here] for t in range(9)]
        grads = []
        for h in range(H):
            back = jnp.concatenate(
                [ret[2 * h, s, :, here].astype(F32), ret[2 * h + 1, s, :, here].astype(F32)],
                axis=0,
            )
            grads.append(cot[s, h, :, here].astype(F32) + back)
        for h in range(H):
            cols = []
            for b in range(3):
                terms = [
                    tap[3 * a + b] * grads[h - a + 1] for a in range(3) if 0 <= h - a + 1 < H
                ]
                cols.append(functools.reduce(jnp.add, terms))
            from_left = jnp.where(
                rows == 0, edge_l[s, h : h + 1, here], pltpu.roll(cols[2], 1, 0)
            )
            from_right = jnp.where(
                rows == WL - 1, edge_r[s, h : h + 1, here], pltpu.roll(cols[0], WL - 1, 0)
            )
            total = cols[1] + from_left + from_right
            value = lat[s, h, :, here].astype(F32)
            sig = 1.0 / (1.0 + jnp.exp(-value))
            out[s, h, :, here] = grads[h] + total * (sig * (1.0 + value * (1.0 - sig)))


def second_kernel(core, recv, out):
    total = jnp.sum(recv[...].astype(F32), axis=0)
    weights = total[:LANES].reshape(16, 8, LANES)
    taps = total[LANES : LANES + 8] + total[LANES + 8 :]
    high = taps.astype(BF16).astype(F32)
    low = taps - high
    at = lax.broadcasted_iota(jnp.int32, (8, LANES), 0)
    both = jnp.where(at < 4, high, pltpu.roll(low, 4, 0))
    for which in range(2):
        own = jnp.where(core[0] == which, 1.0, 0.0)
        for z in range(16):
            out[2 * z + which] = jnp.concatenate([weights[z] * own, both], axis=0).astype(BF16)


def third_kernel(recv, out):
    total = jnp.sum(recv[...].astype(F32), axis=0)
    both = total[8:]
    taps = both + pltpu.roll(both, 4, 0)
    result = jnp.concatenate([total[:8], taps], axis=0)
    for s in range(GROUPS):
        out[s] = result


def unpack_kernel(recv, kernel_out, bias_out, gain_out, *outs):
    for part in range(PARTS):
        here = slice(part * LANES, (part + 1) * LANES)
        for r in range(11):
            row = recv[4 * part + r // 3, 8 + r % 3 : 9 + r % 3, :]
            if r < 9:
                kernel_out[r : r + 1, here] = row
            elif r == 9:
                bias_out[:, here] = row
            else:
                gain_out[:, here] = row
    for m in range(4):
        for high in range(2):
            for side in range(2):
                outs[m][8 * high : 8 * high + 8, side * LANES : (side + 1) * LANES] = recv[
                    4 * m + 2 * high + side, :8, :
                ]


def on_device(
    latents, cotangent, conv_kernel, conv_bias, norm_gain, w_query, w_key, w_value, w_output
):
    strips = lax.axis_size("azim")
    groups = lax.axis_size("sweep")
    up = [(i, (i + 1) % strips) for i in range(strips)]
    down = [(j, i) for i, j in up]
    pair = [(i, i ^ 1) for i in range(strips)]
    core = (lax.axis_index("azim") % 2).astype(jnp.int32).reshape(1)
    predivide = 1.0 / math.sqrt(SL * groups * H * WL * strips)
    bias_row = conv_bias.reshape(1, C)
    gain_row = norm_gain.reshape(1, C)
    edge = pltpu.VMEM((SL, H, C), F32)

    both_edges = struct((2, SL, H, C), BF16)
    cot_sent, first, last = call(
        start_kernel,
        (struct((GROUPS, SL, PX, C), BF16), both_edges, both_edges),
        16,
        moved=1_500_000,
        scratch=[pltpu.VMEM((2, 2, SL, H, C), F32)],
    )(latents, cotangent)
    left = lax.ppermute(last, "azim", up)
    right = lax.ppermute(first, "azim", down)
    recv_cot = lax.all_to_all(cot_sent, "sweep", split_axis=0, concat_axis=0, tiled=True)

    y_sent = call(
        forward_kernel,
        struct((GROUPS, SL, PX, C), BF16),
        16,
        flops=10_000_000,
        moved=1_000_000,
        scratch=[edge, edge],
    )(latents, left, right, conv_kernel, bias_row)
    recv = lax.all_to_all(y_sent, "sweep", split_axis=0, concat_axis=0, tiled=True)

    rows = GROUPS * SL * PX
    grad_attn, halves, gain_sum = call(
        functools.partial(attend_kernel, predivide),
        (
            struct((GROUPS, SL, PX, C), BF16),
            struct((2, GROUPS, LANES, LANES), BF16),
            struct((1, C), F32),
        ),
        32,
        flops=2_000_000_000,
        moved=6_000_000,
        smem=1,
        scratch=[
            pltpu.VMEM((rows, C), BF16),
            pltpu.VMEM((rows, 3 * HD), BF16),
            pltpu.VMEM((rows, HD), BF16),
            pltpu.VMEM((rows, C), BF16),
            pltpu.VMEM((rows, C), F32),
            pltpu.VMEM((rows, LANES), F32),
            pltpu.VMEM((rows, 3 * HD), BF16),
            pltpu.VMEM((rows, HD), BF16),
            pltpu.VMEM((rows, C), F32),
        ],
    )(core, recv, recv_cot, w_query, w_key, w_value, w_output, gain_row)
    ret = lax.all_to_all(grad_attn, "sweep", split_axis=0, concat_axis=0, tiled=True)
    got = lax.ppermute(halves[1], "azim", pair)

    one_edge = struct((SL, H, C), BF16)
    first_sent, back_first, back_last = call(
        functools.partial(taps_kernel, predivide),
        (struct((GROUPS, LANES + 16, LANES), BF16), one_edge, one_edge),
        16,
        flops=10_000_000,
        moved=3_000_000,
        scratch=[edge, edge, pltpu.VMEM((GROUPS, 8, LANES), F32), pltpu.VMEM((2, SL, H, C), F32)],
    )(latents, left, right, cotangent, ret, gain_sum, halves, got)
    first_recv = lax.all_to_all(first_sent, "sweep", split_axis=0, concat_axis=0, tiled=True)
    back_l = lax.ppermute(back_last, "azim", up)
    back_r = lax.ppermute(back_first, "azim", down)

    grad_latents = call(
        latents_kernel,
        struct((SL, H, WL, C), F32),
        16,
        flops=10_000_000,
        moved=4_000_000,
        scratch=[edge, edge],
    )(latents, cotangent, ret, left, right, back_l, back_r, conv_kernel)
    first_recv, grad_latents = lax.optimization_barrier((first_recv, grad_latents))

    second_sent = call(
        second_kernel, struct((strips, 16, LANES), BF16), 16, moved=1_000_000, smem=1
    )(core, first_recv)
    second_recv = lax.all_to_all(second_sent, "azim", split_axis=0, concat_axis=0, tiled=True)
    third_sent = call(third_kernel, struct((GROUPS, 16, LANES), F32), 16, moved=300_000)(
        second_recv
    )
    third_recv = lax.all_to_all(third_sent, "sweep", split_axis=0, concat_axis=0, tiled=True)
    share = struct((C // strips, HD), F32)
    line = struct((1, C), F32)
    grad_kernel, grad_bias, grad_gain, *shares = call(
        unpack_kernel,
        (struct((9, C), F32), line, line, share, share, share, share),
        16,
        moved=300_000,
    )(third_recv)
    return (
        grad_latents,
        grad_kernel,
        grad_bias.reshape(C),
        grad_gain.reshape(C),
        shares[0],
        shares[1],
        shares[2],
        shares[3],
    )


def solution(mesh):
    image = P("sweep", None, "azim", None)
    share = P("azim", None)
    return jax.shard_map(
        on_device,
        mesh=mesh,
        in_specs=(image, image, P(), P(), P(), P(), P(), P(), P()),
        out_specs=(image, P(), P(), P(), share, share, share, share),
        check_vma=False,
    )
```

```python
import functools
import math

import jax
import jax.numpy as jnp
from jax import lax
from jax.experimental import pallas as pl
from jax.experimental.pallas import tpu as pltpu
from jax.sharding import PartitionSpec as P

DH = 64
EPS = 1e-06
F32 = jnp.float32
BF16 = jnp.bfloat16
MASKED = -1e30

SL, H, WL, C = 2, 8, 32, 512
GROUPS = 16
PX = 16
HD = 256
LANES = 128
PARTS = C // LANES


def params(mib):
    return pltpu.CompilerParams(vmem_limit_bytes=mib * 1024 * 1024)


def call(kernel, outs, mib, flops=0, moved=0, scratch=(), smem=0, hbm=()):
    vmem = pl.BlockSpec(memory_space=pltpu.VMEM)

    def run(*args):
        specs = [pl.BlockSpec(memory_space=pltpu.SMEM)] * smem + [vmem] * (len(args) - smem)
        for at in hbm:
            specs[at] = pl.BlockSpec(memory_space=pltpu.HBM)
        return pl.pallas_call(
            kernel,
            out_shape=outs,
            in_specs=specs,
            out_specs=jax.tree.map(lambda _: vmem, outs),
            scratch_shapes=list(scratch),
            compiler_params=params(mib),
            cost_estimate=pl.CostEstimate(
                flops=flops, bytes_accessed=moved, transcendentals=0
            ),
        )(*args)

    return run


def struct(shape, dtype):
    return jax.ShapeDtypeStruct(shape, dtype)


def silu(value):
    return value / (1.0 + jnp.exp(-value))


def nt(left, right):
    return lax.dot_general(left, right, (((1,), (1,)), ((), ())), preferred_element_type=F32)


def tn(left, right):
    return lax.dot_general(left, right, (((0,), (0,)), ((), ())), preferred_element_type=F32)


def nn(left, right):
    return lax.dot_general(left, right, (((1,), (0,)), ((), ())), preferred_element_type=F32)


def lanes_of(part):
    return pl.ds(pl.multiple_of(part * LANES, LANES), LANES)


def row_index(rows):
    return lax.broadcasted_iota(jnp.int32, (rows, LANES), 0)


def row_shifts(value):
    at = lax.broadcasted_iota(jnp.int32, value.shape, 0)
    below = jnp.where(at == 0, 0.0, pltpu.roll(value, 1, 0))
    above = jnp.where(at == H - 1, 0.0, pltpu.roll(value, H - 1, 0))
    return below, value, above


def start_kernel(lat_far, cot_far, packed, first, last, lat, cot, edges, sems):
    copies = [
        pltpu.make_async_copy(lat_far, lat, sems.at[0]),
        pltpu.make_async_copy(cot_far, cot, sems.at[1]),
    ]
    for copy in copies:
        copy.start()
    for which, ref in enumerate((lat, cot)):
        copies[which].wait()
        for s in range(SL):
            for h in range(H):
                edges[0, which, s, h : h + 1, :] = ref[s, h, :PX, :].astype(F32)[:1]
                edges[1, which, s, h : h + 1, :] = ref[s, h, PX:, :].astype(F32)[PX - 1 :]
    first[...] = edges[0].astype(BF16)
    last[...] = edges[1].astype(BF16)
    for s in range(SL):
        for h in range(H):
            packed[2 * h, s] = cot[s, h, :PX, :]
            packed[2 * h + 1, s] = cot[s, h, PX:, :]


def forward_kernel(lat, left, right, taps, bias, out, edge_l, edge_r):
    for s in range(SL):
        shifted = row_shifts(silu(left[0, s].astype(F32)))
        edge_l[s] = sum(taps[3 * a : 3 * a + 1, :] * shifted[a] for a in range(3))
        shifted = row_shifts(silu(right[0, s].astype(F32)))
        edge_r[s] = sum(taps[3 * a + 2 : 3 * a + 3, :] * shifted[a] for a in range(3))
    rows = row_index(WL)

    @pl.loop(0, SL * PARTS)
    def _(step):
        s = step // PARTS
        here = lanes_of(step % PARTS)
        tap = [taps[t : t + 1, here] for t in range(9)]
        base = bias[:, here]
        values = [lat[s, h, :, here].astype(F32) for h in range(H)]
        acts = [silu(v) for v in values]
        for h in range(H):
            cols = []
            for b in range(3):
                terms = [
                    tap[3 * a + b] * acts[h + a - 1] for a in range(3) if 0 <= h + a - 1 < H
                ]
                cols.append(functools.reduce(jnp.add, terms))
            from_left = jnp.where(
                rows == 0, edge_l[s, h : h + 1, here], pltpu.roll(cols[0], 1, 0)
            )
            from_right = jnp.where(
                rows == WL - 1, edge_r[s, h : h + 1, here], pltpu.roll(cols[2], WL - 1, 0)
            )
            y = (values[h] + (cols[1] + from_left + from_right) + base).astype(BF16)
            out[2 * h, s, :, here] = y[:PX]
            out[2 * h + 1, s, :, here] = y[PX:]


def pair_up(first, second):
    low = lax.broadcasted_iota(jnp.int32, first.shape, 1) < 4
    return (
        jnp.where(low, first, pltpu.roll(second, 4, 1)),
        jnp.where(low, pltpu.roll(first, 4, 1), second),
    )


def attend_kernel(
    predivide, core, recv, recv_cot, w_query, w_key, w_value, w_output, gain,
    out, halves, gain_sum,
    normed, stacked, attended, cot, y_rows, inv_rows, qkv, gatt, gnorm,
):
    rows_each = GROUPS * 8
    scale = 1.0 / math.sqrt(DH)
    for tile in range(2):
        y_two = [
            recv[:, s].astype(F32)[:, 8 * tile : 8 * tile + 8, :] for s in range(SL)
        ]
        cot_two = [
            recv_cot[:, s].astype(F32)[:, 8 * tile : 8 * tile + 8, :] for s in range(SL)
        ]
        for half, (y, c) in enumerate(zip(pair_up(*y_two), pair_up(*cot_two))):
            at = pl.ds((2 * tile + half) * rows_each, rows_each)
            y = y.reshape(rows_each, C)
            inverse = lax.rsqrt(jnp.sum(y * y, axis=-1, keepdims=True) * (1.0 / C) + EPS)
            y_rows[at, :] = y
            inv_rows[at, :] = jnp.broadcast_to(inverse, (rows_each, LANES))
            normed[at, :] = (y * inverse * gain[...]).astype(BF16)
            cot[at, :] = c.reshape(rows_each, C).astype(BF16)
    for index, weight in enumerate((w_query, w_key, w_value)):
        qkv[:, index * HD : (index + 1) * HD] = nn(normed[...], weight[...]).astype(BF16)
    gatt[...] = nn(cot[...], w_output[...]).astype(BF16)

    square = (rows_each, rows_each)
    same = (lax.broadcasted_iota(jnp.int32, square, 0) % 4) == (
        lax.broadcasted_iota(jnp.int32, square, 1) % 4
    )
    lane = lax.broadcasted_iota(jnp.int32, (rows_each, LANES), 1)

    def split(value):
        zero = jnp.zeros_like(value)
        return jnp.concatenate(
            [jnp.where(lane < DH, value, zero), jnp.where(lane >= DH, value, zero)], axis=0
        )

    for group in range(4):
        at = pl.ds(group * rows_each, rows_each)
        for pair in range(2):
            def part(index):
                return qkv[at, pl.ds(index * HD + pair * LANES, LANES)]

            lanes = pl.ds(pair * LANES, LANES)
            query, key, value = part(0), part(1), part(2)
            grad_att = gatt[at, lanes]
            key2, value2 = split(key), split(value)
            scores = nt(query, key2)
            grad_probs = nt(grad_att, value2)
            lows, grads = [], []
            for head in range(2):
                cut = slice(head * rows_each, (head + 1) * rows_each)
                score = jnp.where(same, scores[:, cut] * scale, MASKED)
                expon = jnp.exp(score - jnp.max(score, axis=-1, keepdims=True))
                probs = expon * (1.0 / jnp.sum(expon, axis=-1, keepdims=True))
                gp = grad_probs[:, cut]
                weighted = probs * gp
                total = jnp.sum(weighted, axis=-1, keepdims=True)
                lows.append(probs.astype(BF16))
                grads.append(((weighted - probs * total) * scale).astype(BF16))
            attended[at, lanes] = nn(jnp.concatenate(lows, axis=1), value2).astype(BF16)
            grad_q = nn(jnp.concatenate(grads, axis=1), key2)
            grad_k = tn(jnp.concatenate(grads, axis=0), split(query))
            grad_v = tn(jnp.concatenate(lows, axis=0), split(grad_att))
            for index, grad in enumerate((grad_q, grad_k, grad_v)):
                stacked[at, pl.ds(index * HD + pair * LANES, LANES)] = grad.astype(BF16)

    gnorm[...] = (
        nt(stacked[:, :HD], w_query[...])
        + nt(stacked[:, HD : 2 * HD], w_key[...])
        + nt(stacked[:, 2 * HD :], w_value[...])
    )
    total = jnp.zeros((8, C), F32)
    for tile in range(2):
        results = []
        for half in range(2):
            at = pl.ds((2 * tile + half) * rows_each, rows_each)
            y = y_rows[at, :]
            inverse = inv_rows[at, :][:, :1]
            grad = gnorm[at, :]
            total = total + jnp.sum((grad * y * inverse).reshape(GROUPS, 8, C), axis=0)
            gained = grad * gain[...]
            mean = jnp.sum(gained * y, axis=-1, keepdims=True) * (1.0 / C)
            result = inverse * (gained - y * (mean * inverse * inverse))
            results.append(result.reshape(GROUPS, 8, C))
        for s, whole in enumerate(pair_up(*results)):
            out[:, s, 8 * tile : 8 * tile + 8, :] = whole.astype(BF16)
    gain_sum[...] = jnp.sum(total, axis=0, keepdims=True)

    mine = core[0]
    for m in range(4):
        if m < 3:
            whole = tn(normed[...], stacked[:, m * HD : (m + 1) * HD])
        else:
            whole = tn(cot[...], attended[...])
        tiles = (whole * predivide).reshape(16, 2, 2, 8, HD)
        for which in range(2):
            slot = (mine + which) % 2
            for high in range(2):
                for side in range(2):
                    piece = tiles[:, which, high, :, side * LANES : (side + 1) * LANES]
                    halves[slot, 4 * m + 2 * high + side] = piece.reshape(LANES, LANES).astype(BF16)


def taps_kernel(
    predivide, lat, left, right, cot, ret, gain_sum, kept, got,
    out, edge_l, edge_r, tiles,
):
    tiles[...] = jnp.zeros_like(tiles)
    for s in range(SL):
        edge_l[s] = silu(left[0, s].astype(F32))
        edge_r[s] = silu(right[0, s].astype(F32))
    rows = row_index(WL)

    @pl.loop(0, PARTS)
    def _(part):
        here = lanes_of(part)
        sums = [jnp.zeros((8, LANES), F32) for _ in range(10)]
        for s in range(SL):
            grads, cols = [], []
            for h in range(H):
                back = jnp.concatenate(
                    [ret[2 * h, s, :, here].astype(F32), ret[2 * h + 1, s, :, here].astype(F32)],
                    axis=0,
                )
                grads.append(cot[s, h, :, here].astype(F32) + back)
                act = silu(lat[s, h, :, here].astype(F32))
                cols.append(
                    (
                        jnp.where(rows == 0, edge_l[s, h : h + 1, here], pltpu.roll(act, 1, 0)),
                        act,
                        jnp.where(
                            rows == WL - 1, edge_r[s, h : h + 1, here], pltpu.roll(act, WL - 1, 0)
                        ),
                    )
                )
            for h in range(H):
                for a in range(3):
                    if 0 <= h + a - 1 < H:
                        for b in range(3):
                            term = (grads[h] * cols[h + a - 1][b]).reshape(4, 8, LANES)
                            sums[3 * a + b] = sums[3 * a + b] + jnp.sum(term, axis=0)
                sums[9] = sums[9] + jnp.sum(grads[h].reshape(4, 8, LANES), axis=0)
        for r in range(10):
            tiles[4 * part + r // 3, pl.ds(r % 3, 1), :] = jnp.sum(sums[r], axis=0, keepdims=True)
        tiles[4 * part + 3, pl.ds(1, 1), :] = gain_sum[:, here]

    whole = tiles[...] * predivide
    high = whole.astype(BF16).astype(F32)
    out[:, LANES:, :] = jnp.concatenate([high, whole - high], axis=1).astype(BF16)
    out[:, :LANES, :] = (kept[0].astype(F32) + got[...].astype(F32)).astype(BF16)


def edges_kernel(after, ret, first, last, edges):
    del after
    for s in range(SL):
        for h in range(H):
            edges[0, s, h : h + 1, :] = ret[2 * h, s].astype(F32)[:1]
            edges[1, s, h : h + 1, :] = ret[2 * h + 1, s].astype(F32)[PX - 1 :]
    first[...] = edges[0].astype(BF16)
    last[...] = edges[1].astype(BF16)


def latents_kernel(lat, cot, ret, left, right, back_l, back_r, taps, out, edge_l, edge_r):
    for s in range(SL):
        below, here, above = row_shifts(left[1, s].astype(F32) + back_l[s].astype(F32))
        edge_l[s] = taps[2:3, :] * above + taps[5:6, :] * here + taps[8:9, :] * below
        below, here, above = row_shifts(right[1, s].astype(F32) + back_r[s].astype(F32))
        edge_r[s] = taps[0:1, :] * above + taps[3:4, :] * here + taps[6:7, :] * below
    rows = row_index(WL)

    @pl.loop(0, SL * PARTS)
    def _(step):
        s = step // PARTS
        here = lanes_of(step % PARTS)
        tap = [taps[t : t + 1, here] for t in range(9)]
        grads = []
        for h in range(H):
            back = jnp.concatenate(
                [ret[2 * h, s, :, here].astype(F32), ret[2 * h + 1, s, :, here].astype(F32)],
                axis=0,
            )
            grads.append(cot[s, h, :, here].astype(F32) + back)
        for h in range(H):
            cols = []
            for b in range(3):
                terms = [
                    tap[3 * a + b] * grads[h - a + 1] for a in range(3) if 0 <= h - a + 1 < H
                ]
                cols.append(functools.reduce(jnp.add, terms))
            from_left = jnp.where(
                rows == 0, edge_l[s, h : h + 1, here], pltpu.roll(cols[2], 1, 0)
            )
            from_right = jnp.where(
                rows == WL - 1, edge_r[s, h : h + 1, here], pltpu.roll(cols[0], WL - 1, 0)
            )
            total = cols[1] + from_left + from_right
            value = lat[s, h, :, here].astype(F32)
            sig = 1.0 / (1.0 + jnp.exp(-value))
            out[s, h, :, here] = grads[h] + total * (sig * (1.0 + value * (1.0 - sig)))


def second_kernel(core, recv, out):
    total = jnp.sum(recv[...].astype(F32), axis=0)
    weights = total[:LANES].reshape(16, 8, LANES)
    taps = total[LANES : LANES + 8] + total[LANES + 8 :]
    high = taps.astype(BF16).astype(F32)
    low = taps - high
    at = lax.broadcasted_iota(jnp.int32, (8, LANES), 0)
    both = jnp.where(at < 4, high, pltpu.roll(low, 4, 0))
    for which in range(2):
        own = jnp.where(core[0] == which, 1.0, 0.0)
        for z in range(16):
            out[2 * z + which] = jnp.concatenate([weights[z] * own, both], axis=0).astype(BF16)


def third_kernel(recv, out):
    total = jnp.sum(recv[...].astype(F32), axis=0)
    both = total[8:]
    taps = both + pltpu.roll(both, 4, 0)
    result = jnp.concatenate([total[:8], taps], axis=0)
    for s in range(GROUPS):
        out[s] = result


def unpack_kernel(recv, kernel_out, bias_out, gain_out, *outs):
    for part in range(PARTS):
        here = slice(part * LANES, (part + 1) * LANES)
        for r in range(11):
            row = recv[4 * part + r // 3, 8 + r % 3 : 9 + r % 3, :]
            if r < 9:
                kernel_out[r : r + 1, here] = row
            elif r == 9:
                bias_out[:, here] = row
            else:
                gain_out[:, here] = row
    for m in range(4):
        for high in range(2):
            for side in range(2):
                outs[m][8 * high : 8 * high + 8, side * LANES : (side + 1) * LANES] = recv[
                    4 * m + 2 * high + side, :8, :
                ]


def on_device(
    latents, cotangent, conv_kernel, conv_bias, norm_gain, w_query, w_key, w_value, w_output
):
    strips = lax.axis_size("azim")
    groups = lax.axis_size("sweep")
    up = [(i, (i + 1) % strips) for i in range(strips)]
    down = [(j, i) for i, j in up]
    pair = [(i, i ^ 1) for i in range(strips)]
    core = (lax.axis_index("azim") % 2).astype(jnp.int32).reshape(1)
    predivide = 1.0 / math.sqrt(SL * groups * H * WL * strips)
    bias_row = conv_bias.reshape(1, C)
    gain_row = norm_gain.reshape(1, C)
    edge = pltpu.VMEM((SL, H, C), F32)

    both_edges = struct((2, SL, H, C), BF16)
    cot_sent, first, last = call(
        start_kernel,
        (struct((GROUPS, SL, PX, C), BF16), both_edges, both_edges),
        56,
        moved=1_500_000,
        hbm=(0, 1),
        scratch=[
            pltpu.VMEM((SL, H, WL, C), BF16),
            pltpu.VMEM((SL, H, WL, C), BF16),
            pltpu.VMEM((2, 2, SL, H, C), F32),
            pltpu.SemaphoreType.DMA((2,)),
        ],
    )(latents, cotangent)
    left = lax.ppermute(last, "azim", up)
    right = lax.ppermute(first, "azim", down)
    recv_cot = lax.all_to_all(cot_sent, "sweep", split_axis=0, concat_axis=0, tiled=True)

    rows = GROUPS * SL * PX
    y_sent = call(
        forward_kernel,
        struct((GROUPS, SL, PX, C), BF16),
        16,
        flops=10_000_000,
        moved=1_000_000,
        scratch=[edge, edge],
    )(latents, left, right, conv_kernel, bias_row)
    recv = lax.all_to_all(y_sent, "sweep", split_axis=0, concat_axis=0, tiled=True)

    grad_attn, halves, gain_sum = call(
        functools.partial(attend_kernel, predivide),
        (
            struct((GROUPS, SL, PX, C), BF16),
            struct((2, GROUPS, LANES, LANES), BF16),
            struct((1, C), F32),
        ),
        32,
        flops=2_000_000_000,
        moved=6_000_000,
        smem=1,
        scratch=[
            pltpu.VMEM((rows, C), BF16),
            pltpu.VMEM((rows, 3 * HD), BF16),
            pltpu.VMEM((rows, HD), BF16),
            pltpu.VMEM((rows, C), BF16),
            pltpu.VMEM((rows, C), F32),
            pltpu.VMEM((rows, LANES), F32),
            pltpu.VMEM((rows, 3 * HD), BF16),
            pltpu.VMEM((rows, HD), BF16),
            pltpu.VMEM((rows, C), F32),
        ],
    )(core, recv, recv_cot, w_query, w_key, w_value, w_output, gain_row)
    ret = lax.all_to_all(grad_attn, "sweep", split_axis=0, concat_axis=0, tiled=True)
    got = lax.ppermute(halves[1], "azim", pair)

    first_sent = call(
        functools.partial(taps_kernel, predivide),
        struct((GROUPS, LANES + 16, LANES), BF16),
        16,
        flops=10_000_000,
        moved=3_000_000,
        scratch=[edge, edge, pltpu.VMEM((GROUPS, 8, LANES), F32)],
    )(latents, left, right, cotangent, ret, gain_sum, halves, got)
    first_recv = lax.all_to_all(first_sent, "sweep", split_axis=0, concat_axis=0, tiled=True)
    one_edge = struct((SL, H, C), BF16)
    back_first, back_last = call(
        edges_kernel,
        (one_edge, one_edge),
        16,
        moved=100_000,
        hbm=(0,),
        scratch=[pltpu.VMEM((2, SL, H, C), F32)],
    )(first_sent, ret)
    back_l = lax.ppermute(back_last, "azim", up)
    back_r = lax.ppermute(back_first, "azim", down)
    first_recv, back_l, back_r = lax.optimization_barrier((first_recv, back_l, back_r))

    grad_latents = call(
        latents_kernel,
        struct((SL, H, WL, C), F32),
        16,
        flops=10_000_000,
        moved=4_000_000,
        scratch=[edge, edge],
    )(latents, cotangent, ret, left, right, back_l, back_r, conv_kernel)

    second_sent = call(
        second_kernel, struct((strips, 16, LANES), BF16), 16, moved=1_000_000, smem=1
    )(core, first_recv)
    second_recv = lax.all_to_all(second_sent, "azim", split_axis=0, concat_axis=0, tiled=True)
    second_recv, grad_latents = lax.optimization_barrier((second_recv, grad_latents))
    third_sent = call(third_kernel, struct((GROUPS, 16, LANES), F32), 16, moved=300_000)(
        second_recv
    )
    third_recv = lax.all_to_all(third_sent, "sweep", split_axis=0, concat_axis=0, tiled=True)
    share = struct((C // strips, HD), F32)
    line = struct((1, C), F32)
    grad_kernel, grad_bias, grad_gain, *shares = call(
        unpack_kernel,
        (struct((9, C), F32), line, line, share, share, share, share),
        16,
        moved=300_000,
    )(third_recv)
    return (
        grad_latents,
        grad_kernel,
        grad_bias.reshape(C),
        grad_gain.reshape(C),
        shares[0],
        shares[1],
        shares[2],
        shares[3],
    )


def solution(mesh):
    image = P("sweep", None, "azim", None)
    share = P("azim", None)
    return jax.shard_map(
        on_device,
        mesh=mesh,
        in_specs=(image, image, P(), P(), P(), P(), P(), P(), P()),
        out_specs=(image, P(), P(), P(), share, share, share, share),
        check_vma=False,
    )
```

```python
import functools
import math

import jax
import jax.numpy as jnp
from jax import lax
from jax.experimental import pallas as pl
from jax.experimental.pallas import tpu as pltpu
from jax.sharding import PartitionSpec as P

DH = 64
EPS = 1e-06
F32 = jnp.float32
BF16 = jnp.bfloat16
MASKED = -1e30

SL, H, WL, C = 2, 8, 32, 512
GROUPS = 16
PX = 16
HD = 256
LANES = 128
PARTS = C // LANES
ROWS = 64


def params(mib):
    return pltpu.CompilerParams(vmem_limit_bytes=mib * 1024 * 1024)


def call(kernel, outs, mib, flops=0, moved=0, scratch=(), smem=0, hbm=()):
    vmem = pl.BlockSpec(memory_space=pltpu.VMEM)

    def run(*args):
        specs = [pl.BlockSpec(memory_space=pltpu.SMEM)] * smem + [vmem] * (len(args) - smem)
        for at in hbm:
            specs[at] = pl.BlockSpec(memory_space=pltpu.HBM)
        return pl.pallas_call(
            kernel,
            out_shape=outs,
            in_specs=specs,
            out_specs=jax.tree.map(lambda _: vmem, outs),
            scratch_shapes=list(scratch),
            compiler_params=params(mib),
            cost_estimate=pl.CostEstimate(
                flops=flops, bytes_accessed=moved, transcendentals=0
            ),
        )(*args)

    return run


def struct(shape, dtype):
    return jax.ShapeDtypeStruct(shape, dtype)


def silu(value):
    return value / (1.0 + jnp.exp(-value))


def nt(left, right):
    return lax.dot_general(left, right, (((1,), (1,)), ((), ())), preferred_element_type=F32)


def tn(left, right):
    return lax.dot_general(left, right, (((0,), (0,)), ((), ())), preferred_element_type=F32)


def nn(left, right):
    return lax.dot_general(left, right, (((1,), (0,)), ((), ())), preferred_element_type=F32)


def lanes_of(part):
    return pl.ds(pl.multiple_of(part * LANES, LANES), LANES)


def row_index(rows):
    return lax.broadcasted_iota(jnp.int32, (rows, LANES), 0)


def row_shifts(value):
    at = lax.broadcasted_iota(jnp.int32, value.shape, 0)
    below = jnp.where(at == 0, 0.0, pltpu.roll(value, 1, 0))
    above = jnp.where(at == H - 1, 0.0, pltpu.roll(value, H - 1, 0))
    return below, value, above


def core_of(spot):
    return spot[0] % 2


def side_of(spot):
    return (spot[0] // 2) % 2


def to_partners(spot, first, last):
    even = core_of(spot) == 0
    return jnp.where(even, last, first), jnp.where(even, first, last)


def from_partners(spot, other_core, other_chip):
    even = core_of(spot) == 0
    return jnp.where(even, other_chip, other_core), jnp.where(even, other_core, other_chip)


def start_kernel(spot, lat, to_core, to_chip, edges):
    for s in range(SL):
        for h in range(H):
            edges[0, s, h : h + 1, :] = lat[s, h, :PX, :].astype(F32)[:1]
            edges[1, s, h : h + 1, :] = lat[s, h, PX:, :].astype(F32)[PX - 1 :]
    one, two = to_partners(spot, edges[0], edges[1])
    to_core[...] = one.astype(BF16)
    to_chip[...] = two.astype(BF16)


def forward_kernel(spot, lat, cot, other_core, other_chip, taps, bias, out, edge_l, edge_r):
    for s in range(SL):
        left, right = from_partners(spot, other_core[s].astype(F32), other_chip[s].astype(F32))
        shifted = row_shifts(silu(left))
        edge_l[s] = sum(taps[3 * a : 3 * a + 1, :] * shifted[a] for a in range(3))
        shifted = row_shifts(silu(right))
        edge_r[s] = sum(taps[3 * a + 2 : 3 * a + 3, :] * shifted[a] for a in range(3))
    rows = row_index(WL)

    @pl.loop(0, SL * PARTS)
    def _(step):
        s = step // PARTS
        here = lanes_of(step % PARTS)
        tap = [taps[t : t + 1, here] for t in range(9)]
        base = bias[:, here]
        values = [lat[s, h, :, here].astype(F32) for h in range(H)]
        acts = [silu(v) for v in values]
        for h in range(H):
            cols = []
            for b in range(3):
                terms = [
                    tap[3 * a + b] * acts[h + a - 1] for a in range(3) if 0 <= h + a - 1 < H
                ]
                cols.append(functools.reduce(jnp.add, terms))
            from_left = jnp.where(
                rows == 0, edge_l[s, h : h + 1, here], pltpu.roll(cols[0], 1, 0)
            )
            from_right = jnp.where(
                rows == WL - 1, edge_r[s, h : h + 1, here], pltpu.roll(cols[2], WL - 1, 0)
            )
            y = (values[h] + (cols[1] + from_left + from_right) + base).astype(BF16)
            out[2 * h, 0, s, :, here] = y[:PX]
            out[2 * h + 1, 0, s, :, here] = y[PX:]
            moved = cot[s, h, :, here]
            out[2 * h, 1, s, :, here] = moved[:PX]
            out[2 * h + 1, 1, s, :, here] = moved[PX:]


def pair_up(first, second):
    low = lax.broadcasted_iota(jnp.int32, first.shape, 1) < 4
    return (
        jnp.where(low, first, pltpu.roll(second, 4, 1)),
        jnp.where(low, pltpu.roll(first, 4, 1), second),
    )


def attend_kernel(
    predivide, spot, recv, w_query, w_key, w_value, w_output, gain,
    out, halves, gain_sum,
    normed, stacked, attended, cot, y_rows, inv_rows, qkv, gatt, gnorm,
):
    rows_each = GROUPS * 8
    scale = 1.0 / math.sqrt(DH)
    for tile in range(2):
        y_two = [
            recv[:, 0, s].astype(F32)[:, 8 * tile : 8 * tile + 8, :] for s in range(SL)
        ]
        cot_two = [
            recv[:, 1, s].astype(F32)[:, 8 * tile : 8 * tile + 8, :] for s in range(SL)
        ]
        for half, (y, c) in enumerate(zip(pair_up(*y_two), pair_up(*cot_two))):
            at = pl.ds((2 * tile + half) * rows_each, rows_each)
            y = y.reshape(rows_each, C)
            inverse = lax.rsqrt(jnp.sum(y * y, axis=-1, keepdims=True) * (1.0 / C) + EPS)
            y_rows[at, :] = y
            inv_rows[at, :] = jnp.broadcast_to(inverse, (rows_each, LANES))
            normed[at, :] = (y * inverse * gain[...]).astype(BF16)
            cot[at, :] = c.reshape(rows_each, C).astype(BF16)
    for index, weight in enumerate((w_query, w_key, w_value)):
        qkv[:, index * HD : (index + 1) * HD] = nn(normed[...], weight[...]).astype(BF16)
    gatt[...] = nn(cot[...], w_output[...]).astype(BF16)

    square = (rows_each, rows_each)
    same = (lax.broadcasted_iota(jnp.int32, square, 0) % 4) == (
        lax.broadcasted_iota(jnp.int32, square, 1) % 4
    )
    lane = lax.broadcasted_iota(jnp.int32, (rows_each, LANES), 1)

    def split(value):
        zero = jnp.zeros_like(value)
        return jnp.concatenate(
            [jnp.where(lane < DH, value, zero), jnp.where(lane >= DH, value, zero)], axis=0
        )

    for group in range(4):
        at = pl.ds(group * rows_each, rows_each)
        for pair in range(2):
            def part(index):
                return qkv[at, pl.ds(index * HD + pair * LANES, LANES)]

            lanes = pl.ds(pair * LANES, LANES)
            query, key, value = part(0), part(1), part(2)
            grad_att = gatt[at, lanes]
            key2, value2 = split(key), split(value)
            scores = nt(query, key2)
            grad_probs = nt(grad_att, value2)
            lows, grads = [], []
            for head in range(2):
                cut = slice(head * rows_each, (head + 1) * rows_each)
                score = jnp.where(same, scores[:, cut] * scale, MASKED)
                expon = jnp.exp(score - jnp.max(score, axis=-1, keepdims=True))
                probs = expon * (1.0 / jnp.sum(expon, axis=-1, keepdims=True))
                gp = grad_probs[:, cut]
                weighted = probs * gp
                total = jnp.sum(weighted, axis=-1, keepdims=True)
                lows.append(probs.astype(BF16))
                grads.append(((weighted - probs * total) * scale).astype(BF16))
            attended[at, lanes] = nn(jnp.concatenate(lows, axis=1), value2).astype(BF16)
            grad_q = nn(jnp.concatenate(grads, axis=1), key2)
            grad_k = tn(jnp.concatenate(grads, axis=0), split(query))
            grad_v = tn(jnp.concatenate(lows, axis=0), split(grad_att))
            for index, grad in enumerate((grad_q, grad_k, grad_v)):
                stacked[at, pl.ds(index * HD + pair * LANES, LANES)] = grad.astype(BF16)

    gnorm[...] = (
        nt(stacked[:, :HD], w_query[...])
        + nt(stacked[:, HD : 2 * HD], w_key[...])
        + nt(stacked[:, 2 * HD :], w_value[...])
    )
    total = jnp.zeros((8, C), F32)
    for tile in range(2):
        results = []
        for half in range(2):
            at = pl.ds((2 * tile + half) * rows_each, rows_each)
            y = y_rows[at, :]
            inverse = inv_rows[at, :][:, :1]
            grad = gnorm[at, :]
            total = total + jnp.sum((grad * y * inverse).reshape(GROUPS, 8, C), axis=0)
            gained = grad * gain[...]
            mean = jnp.sum(gained * y, axis=-1, keepdims=True) * (1.0 / C)
            result = inverse * (gained - y * (mean * inverse * inverse))
            results.append(result.reshape(GROUPS, 8, C))
        for s, whole in enumerate(pair_up(*results)):
            out[:, s, 8 * tile : 8 * tile + 8, :] = whole.astype(BF16)
    gain_sum[...] = jnp.sum(total, axis=0, keepdims=True)

    for m in range(4):
        if m < 3:
            whole = tn(normed[...], stacked[:, m * HD : (m + 1) * HD])
        else:
            whole = tn(cot[...], attended[...])
        tiles = (whole * predivide).reshape(8, 2, 2, 2, 8, HD)
        for z in range(2):
            for core in range(2):
                away_core, away_z = (core_of(spot) + core) % 2, (side_of(spot) + z) % 2
                for high in range(2):
                    for side in range(2):
                        piece = tiles[:, z, core, high, :, side * LANES : (side + 1) * LANES]
                        halves[away_core, away_z, 4 * m + 2 * high + side] = piece.reshape(
                            ROWS, LANES
                        ).astype(BF16)


def add_cores_kernel(kept, got, keep, send):
    keep[...] = (kept[0, 0].astype(F32) + got[0].astype(F32)).astype(BF16)
    send[...] = (kept[0, 1].astype(F32) + got[1].astype(F32)).astype(BF16)


def add_chips_kernel(kept, got, out):
    out[:, :ROWS, :] = (kept[...].astype(F32) + got[...].astype(F32)).astype(BF16)
    out[:, ROWS:, :] = jnp.zeros((GROUPS, 16, LANES), BF16)


def taps_kernel(
    predivide, spot, lat, other_core, other_chip, cot, ret, gain_sum, sums_in,
    out, edge_l, edge_r, tiles, packed, sem,
):
    del sums_in
    tiles[...] = jnp.zeros_like(tiles)
    for s in range(SL):
        left, right = from_partners(spot, other_core[s].astype(F32), other_chip[s].astype(F32))
        edge_l[s] = silu(left)
        edge_r[s] = silu(right)
    rows = row_index(WL)

    @pl.loop(0, PARTS)
    def _(part):
        here = lanes_of(part)
        sums = [jnp.zeros((8, LANES), F32) for _ in range(10)]
        for s in range(SL):
            grads, cols = [], []
            for h in range(H):
                back = jnp.concatenate(
                    [ret[2 * h, s, :, here].astype(F32), ret[2 * h + 1, s, :, here].astype(F32)],
                    axis=0,
                )
                grads.append(cot[s, h, :, here].astype(F32) + back)
                act = silu(lat[s, h, :, here].astype(F32))
                cols.append(
                    (
                        jnp.where(rows == 0, edge_l[s, h : h + 1, here], pltpu.roll(act, 1, 0)),
                        act,
                        jnp.where(
                            rows == WL - 1, edge_r[s, h : h + 1, here], pltpu.roll(act, WL - 1, 0)
                        ),
                    )
                )
            for h in range(H):
                for a in range(3):
                    if 0 <= h + a - 1 < H:
                        for b in range(3):
                            term = (grads[h] * cols[h + a - 1][b]).reshape(4, 8, LANES)
                            sums[3 * a + b] = sums[3 * a + b] + jnp.sum(term, axis=0)
                sums[9] = sums[9] + jnp.sum(grads[h].reshape(4, 8, LANES), axis=0)
        for r in range(10):
            tiles[4 * part + r // 3, pl.ds(r % 3, 1), :] = jnp.sum(sums[r], axis=0, keepdims=True)
        tiles[4 * part + 3, pl.ds(1, 1), :] = gain_sum[:, here]

    whole = tiles[...] * predivide
    high = whole.astype(BF16).astype(F32)
    packed[...] = jnp.concatenate([high, whole - high], axis=1).astype(BF16)
    copy = pltpu.make_async_copy(packed, out.at[:, pl.ds(ROWS, 16), :], sem)
    copy.start()
    copy.wait()


def edges_kernel(spot, after, cot, ret, to_core, to_chip, edges):
    del after
    for s in range(SL):
        for h in range(H):
            at = pl.ds(h, 1)
            edges[0, 0, s, at, :] = cot[s, h, :PX, :].astype(F32)[:1]
            edges[1, 0, s, at, :] = cot[s, h, PX:, :].astype(F32)[PX - 1 :]
            edges[0, 1, s, at, :] = ret[2 * h, s].astype(F32)[:1]
            edges[1, 1, s, at, :] = ret[2 * h + 1, s].astype(F32)[PX - 1 :]
    one, two = to_partners(spot, edges[0], edges[1])
    to_core[...] = one.astype(BF16)
    to_chip[...] = two.astype(BF16)


def latents_kernel(spot, lat, cot, ret, other_core, other_chip, taps, out, edge_l, edge_r):
    for s in range(SL):
        left, right = from_partners(
            spot,
            other_core[0, s].astype(F32) + other_core[1, s].astype(F32),
            other_chip[0, s].astype(F32) + other_chip[1, s].astype(F32),
        )
        below, here, above = row_shifts(left)
        edge_l[s] = taps[2:3, :] * above + taps[5:6, :] * here + taps[8:9, :] * below
        below, here, above = row_shifts(right)
        edge_r[s] = taps[0:1, :] * above + taps[3:4, :] * here + taps[6:7, :] * below
    rows = row_index(WL)

    @pl.loop(0, SL * PARTS)
    def _(step):
        s = step // PARTS
        here = lanes_of(step % PARTS)
        tap = [taps[t : t + 1, here] for t in range(9)]
        grads = []
        for h in range(H):
            back = jnp.concatenate(
                [ret[2 * h, s, :, here].astype(F32), ret[2 * h + 1, s, :, here].astype(F32)],
                axis=0,
            )
            grads.append(cot[s, h, :, here].astype(F32) + back)
        for h in range(H):
            cols = []
            for b in range(3):
                terms = [
                    tap[3 * a + b] * grads[h - a + 1] for a in range(3) if 0 <= h - a + 1 < H
                ]
                cols.append(functools.reduce(jnp.add, terms))
            from_left = jnp.where(
                rows == 0, edge_l[s, h : h + 1, here], pltpu.roll(cols[2], 1, 0)
            )
            from_right = jnp.where(
                rows == WL - 1, edge_r[s, h : h + 1, here], pltpu.roll(cols[0], WL - 1, 0)
            )
            total = cols[1] + from_left + from_right
            value = lat[s, h, :, here].astype(F32)
            sig = 1.0 / (1.0 + jnp.exp(-value))
            out[s, h, :, here] = grads[h] + total * (sig * (1.0 + value * (1.0 - sig)))


def second_kernel(spot, recv, out):
    total = jnp.sum(recv[...].astype(F32), axis=0)
    weights = total[:ROWS].reshape(8, 8, LANES)
    taps = total[ROWS : ROWS + 8] + total[ROWS + 8 :]
    high = taps.astype(BF16).astype(F32)
    low = taps - high
    at = lax.broadcasted_iota(jnp.int32, (8, LANES), 0)
    both = jnp.where(at < 4, high, pltpu.roll(low, 4, 0))
    for z in range(2):
        for core in range(2):
            own = jnp.where(jnp.logical_and(core_of(spot) == core, side_of(spot) == z), 1.0, 0.0)
            for block in range(8):
                out[4 * block + 2 * z + core] = jnp.concatenate(
                    [weights[block] * own, both], axis=0
                ).astype(BF16)


def third_kernel(recv, out):
    total = jnp.sum(recv[...].astype(F32), axis=0)
    both = total[8:]
    taps = both + pltpu.roll(both, 4, 0)
    result = jnp.concatenate([total[:8], taps], axis=0)
    for s in range(GROUPS):
        out[s] = result


def unpack_kernel(recv, kernel_out, bias_out, gain_out, *outs):
    for part in range(PARTS):
        here = slice(part * LANES, (part + 1) * LANES)
        for r in range(11):
            row = recv[4 * part + r // 3, 8 + r % 3 : 9 + r % 3, :]
            if r < 9:
                kernel_out[r : r + 1, here] = row
            elif r == 9:
                bias_out[:, here] = row
            else:
                gain_out[:, here] = row
    for m in range(4):
        for high in range(2):
            for side in range(2):
                outs[m][8 * high : 8 * high + 8, side * LANES : (side + 1) * LANES] = recv[
                    4 * m + 2 * high + side, :8, :
                ]


def on_device(
    latents, cotangent, conv_kernel, conv_bias, norm_gain, w_query, w_key, w_value, w_output
):
    strips = lax.axis_size("azim")
    groups = lax.axis_size("sweep")
    cores = [(i, i ^ 1) for i in range(strips)]
    chips = [(i, (i + 1 if i % 2 else i - 1) % strips) for i in range(strips)]
    sides = [(i, i ^ 2) for i in range(strips)]
    strip = lax.axis_index("azim")
    spot = strip.astype(jnp.int32).reshape(1)
    predivide = 1.0 / math.sqrt(SL * groups * H * WL * strips)
    bias_row = conv_bias.reshape(1, C)
    gain_row = norm_gain.reshape(1, C)
    edge = pltpu.VMEM((SL, H, C), F32)

    one_edge = struct((SL, H, C), BF16)
    to_core, to_chip = call(
        start_kernel,
        (one_edge, one_edge),
        16,
        moved=600_000,
        smem=1,
        scratch=[pltpu.VMEM((2, SL, H, C), F32)],
    )(spot, latents)
    other_chip = lax.ppermute(to_chip, "azim", chips)
    other_core = lax.ppermute(to_core, "azim", cores)

    sent = call(
        forward_kernel,
        struct((GROUPS, 2, SL, PX, C), BF16),
        16,
        flops=10_000_000,
        moved=2_000_000,
        smem=1,
        scratch=[edge, edge],
    )(spot, latents, cotangent, other_core, other_chip, conv_kernel, bias_row)
    recv = lax.all_to_all(sent, "sweep", split_axis=0, concat_axis=0, tiled=True)

    rows = GROUPS * SL * PX
    grad_attn, halves, gain_sum = call(
        functools.partial(attend_kernel, predivide),
        (
            struct((GROUPS, SL, PX, C), BF16),
            struct((2, 2, GROUPS, ROWS, LANES), BF16),
            struct((1, C), F32),
        ),
        32,
        flops=2_000_000_000,
        moved=6_000_000,
        smem=1,
        scratch=[
            pltpu.VMEM((rows, C), BF16),
            pltpu.VMEM((rows, 3 * HD), BF16),
            pltpu.VMEM((rows, HD), BF16),
            pltpu.VMEM((rows, C), BF16),
            pltpu.VMEM((rows, C), F32),
            pltpu.VMEM((rows, LANES), F32),
            pltpu.VMEM((rows, 3 * HD), BF16),
            pltpu.VMEM((rows, HD), BF16),
            pltpu.VMEM((rows, C), F32),
        ],
    )(spot, recv, w_query, w_key, w_value, w_output, gain_row)
    ret = lax.all_to_all(grad_attn, "sweep", split_axis=0, concat_axis=0, tiled=True)
    from_core = lax.ppermute(halves[1], "azim", cores)
    piece = struct((GROUPS, ROWS, LANES), BF16)
    keep, send = call(add_cores_kernel, (piece, piece), 16, moved=2_000_000)(halves, from_core)
    from_chip = lax.ppermute(send, "azim", sides)
    payload = struct((GROUPS, ROWS + 16, LANES), BF16)
    sums = call(add_chips_kernel, payload, 16, moved=1_000_000)(keep, from_chip)

    vmem = pl.BlockSpec(memory_space=pltpu.VMEM)
    anywhere = pl.BlockSpec(memory_space=pltpu.HBM)
    first_sent = pl.pallas_call(
        functools.partial(taps_kernel, predivide),
        out_shape=payload,
        in_specs=[pl.BlockSpec(memory_space=pltpu.SMEM)] + [vmem] * 6 + [anywhere],
        out_specs=anywhere,
        input_output_aliases={7: 0},
        scratch_shapes=[
            edge,
            edge,
            pltpu.VMEM((GROUPS, 8, LANES), F32),
            pltpu.VMEM((GROUPS, 16, LANES), BF16),
            pltpu.SemaphoreType.DMA,
        ],
        compiler_params=params(16),
        cost_estimate=pl.CostEstimate(
            flops=10_000_000, bytes_accessed=2_000_000, transcendentals=0
        ),
    )(spot, latents, other_core, other_chip, cotangent, ret, gain_sum, sums)
    first_recv = lax.all_to_all(first_sent, "sweep", split_axis=0, concat_axis=0, tiled=True)
    both_edges = struct((2, SL, H, C), BF16)
    back_core, back_chip = call(
        edges_kernel,
        (both_edges, both_edges),
        16,
        moved=100_000,
        smem=1,
        hbm=(1,),
        scratch=[pltpu.VMEM((2, 2, SL, H, C), F32)],
    )(spot, first_sent, cotangent, ret)
    back_chip = lax.ppermute(back_chip, "azim", chips)
    back_core = lax.ppermute(back_core, "azim", cores)
    first_recv, back_chip, back_core = lax.optimization_barrier(
        (first_recv, back_chip, back_core)
    )

    grad_latents = call(
        latents_kernel,
        struct((SL, H, WL, C), F32),
        16,
        flops=10_000_000,
        moved=4_000_000,
        smem=1,
        scratch=[edge, edge],
    )(spot, latents, cotangent, ret, back_core, back_chip, conv_kernel)

    second_sent = call(
        second_kernel, struct((strips, 16, LANES), BF16), 16, moved=1_000_000, smem=1
    )(spot, first_recv)
    second_recv = lax.all_to_all(second_sent, "azim", split_axis=0, concat_axis=0, tiled=True)
    second_recv, grad_latents = lax.optimization_barrier((second_recv, grad_latents))
    third_sent = call(third_kernel, struct((GROUPS, 16, LANES), F32), 16, moved=300_000)(
        second_recv
    )
    third_recv = lax.all_to_all(third_sent, "sweep", split_axis=0, concat_axis=0, tiled=True)
    share = struct((C // strips, HD), F32)
    line = struct((1, C), F32)
    grad_kernel, grad_bias, grad_gain, *shares = call(
        unpack_kernel,
        (struct((9, C), F32), line, line, share, share, share, share),
        16,
        moved=300_000,
    )(third_recv)
    return (
        grad_latents,
        grad_kernel,
        grad_bias.reshape(C),
        grad_gain.reshape(C),
        shares[0],
        shares[1],
        shares[2],
        shares[3],
    )


def solution(mesh):
    image = P("sweep", None, "azim", None)
    share = P("azim", None)
    return jax.shard_map(
        on_device,
        mesh=mesh,
        in_specs=(image, image, P(), P(), P(), P(), P(), P(), P()),
        out_specs=(image, P(), P(), P(), share, share, share, share),
        check_vma=False,
    )
```

```python
import functools
import math

import jax
import jax.numpy as jnp
from jax import lax
from jax.experimental import pallas as pl
from jax.experimental.pallas import tpu as pltpu
from jax.sharding import PartitionSpec as P

DH = 64
EPS = 1e-06
F32 = jnp.float32
BF16 = jnp.bfloat16
MASKED = -1e30

SL, H, WL, C = 2, 8, 32, 512
GROUPS = 16
PX = 16
HD = 256
LANES = 128
PARTS = C // LANES
ROWS = 64


def params(mib):
    return pltpu.CompilerParams(vmem_limit_bytes=mib * 1024 * 1024)


def call(kernel, outs, mib, flops=0, moved=0, scratch=(), smem=0, hbm=()):
    vmem = pl.BlockSpec(memory_space=pltpu.VMEM)

    def run(*args):
        specs = [pl.BlockSpec(memory_space=pltpu.SMEM)] * smem + [vmem] * (len(args) - smem)
        for at in hbm:
            specs[at] = pl.BlockSpec(memory_space=pltpu.HBM)
        return pl.pallas_call(
            kernel,
            out_shape=outs,
            in_specs=specs,
            out_specs=jax.tree.map(lambda _: vmem, outs),
            scratch_shapes=list(scratch),
            compiler_params=params(mib),
            cost_estimate=pl.CostEstimate(
                flops=flops, bytes_accessed=moved, transcendentals=0
            ),
        )(*args)

    return run


def struct(shape, dtype):
    return jax.ShapeDtypeStruct(shape, dtype)


def silu(value):
    return value / (1.0 + jnp.exp(-value))


def nt(left, right):
    return lax.dot_general(left, right, (((1,), (1,)), ((), ())), preferred_element_type=F32)


def tn(left, right):
    return lax.dot_general(left, right, (((0,), (0,)), ((), ())), preferred_element_type=F32)


def nn(left, right):
    return lax.dot_general(left, right, (((1,), (0,)), ((), ())), preferred_element_type=F32)


def lanes_of(part):
    return pl.ds(pl.multiple_of(part * LANES, LANES), LANES)


def row_index(rows):
    return lax.broadcasted_iota(jnp.int32, (rows, LANES), 0)


def row_shifts(value):
    at = lax.broadcasted_iota(jnp.int32, value.shape, 0)
    below = jnp.where(at == 0, 0.0, pltpu.roll(value, 1, 0))
    above = jnp.where(at == H - 1, 0.0, pltpu.roll(value, H - 1, 0))
    return below, value, above


def core_of(spot):
    return spot[0] % 2


def side_of(spot):
    return (spot[0] // 2) % 2


def partner_column(spot, for_core, first, last):
    even = core_of(spot) == 0
    return jnp.where(even, last, first) if for_core else jnp.where(even, first, last)


def from_partners(spot, other_core, other_chip):
    even = core_of(spot) == 0
    return jnp.where(even, other_chip, other_core), jnp.where(even, other_core, other_chip)


def edge_columns(lat, edges):
    for s in range(SL):
        for h in range(H):
            edges[0, s, h : h + 1, :] = lat[s, h, :PX, :].astype(F32)[:1]
            edges[1, s, h : h + 1, :] = lat[s, h, PX:, :].astype(F32)[PX - 1 :]


def chip_edge_kernel(spot, lat, out, edges):
    edge_columns(lat, edges)
    out[...] = partner_column(spot, False, edges[0], edges[1]).astype(BF16)


def core_edge_kernel(spot, after, lat, taps, bias, out, table, edges):
    del after
    edge_columns(lat, edges)
    out[...] = partner_column(spot, True, edges[0], edges[1]).astype(BF16)
    table[:9, :] = taps[...]
    table[9:10, :] = bias[...]
    table[10:, :] = jnp.zeros((6, C), F32)


def forward_kernel(spot, lat, cot, other_core, other_chip, taps, out, edge_l, edge_r):
    for s in range(SL):
        left, right = from_partners(spot, other_core[s].astype(F32), other_chip[s].astype(F32))
        shifted = row_shifts(silu(left))
        edge_l[s] = sum(taps[3 * a : 3 * a + 1, :] * shifted[a] for a in range(3))
        shifted = row_shifts(silu(right))
        edge_r[s] = sum(taps[3 * a + 2 : 3 * a + 3, :] * shifted[a] for a in range(3))
    rows = row_index(WL)

    @pl.loop(0, SL * PARTS)
    def _(step):
        s = step // PARTS
        here = lanes_of(step % PARTS)
        tap = [taps[t : t + 1, here] for t in range(9)]
        base = taps[9:10, here]
        values = [lat[s, h, :, here].astype(F32) for h in range(H)]
        acts = [silu(v) for v in values]
        for h in range(H):
            cols = []
            for b in range(3):
                terms = [
                    tap[3 * a + b] * acts[h + a - 1] for a in range(3) if 0 <= h + a - 1 < H
                ]
                cols.append(functools.reduce(jnp.add, terms))
            from_left = jnp.where(
                rows == 0, edge_l[s, h : h + 1, here], pltpu.roll(cols[0], 1, 0)
            )
            from_right = jnp.where(
                rows == WL - 1, edge_r[s, h : h + 1, here], pltpu.roll(cols[2], WL - 1, 0)
            )
            y = (values[h] + (cols[1] + from_left + from_right) + base).astype(BF16)
            out[2 * h, 0, s, :, here] = y[:PX]
            out[2 * h + 1, 0, s, :, here] = y[PX:]
            moved = cot[s, h, :, here]
            out[2 * h, 1, s, :, here] = moved[:PX]
            out[2 * h + 1, 1, s, :, here] = moved[PX:]


def pair_up(first, second):
    low = lax.broadcasted_iota(jnp.int32, first.shape, 1) < 4
    return (
        jnp.where(low, first, pltpu.roll(second, 4, 1)),
        jnp.where(low, pltpu.roll(first, 4, 1), second),
    )


def attend_kernel(
    predivide, spot, recv, w_query, w_key, w_value, w_output, gain,
    out, halves, gain_sum,
    normed, stacked, attended, cot, y_rows, inv_rows, qkv, gatt, gnorm,
):
    rows_each = GROUPS * 8
    scale = 1.0 / math.sqrt(DH)
    for tile in range(2):
        y_two = [
            recv[:, 0, s].astype(F32)[:, 8 * tile : 8 * tile + 8, :] for s in range(SL)
        ]
        cot_two = [
            recv[:, 1, s].astype(F32)[:, 8 * tile : 8 * tile + 8, :] for s in range(SL)
        ]
        for half, (y, c) in enumerate(zip(pair_up(*y_two), pair_up(*cot_two))):
            at = pl.ds((2 * tile + half) * rows_each, rows_each)
            y = y.reshape(rows_each, C)
            inverse = lax.rsqrt(jnp.sum(y * y, axis=-1, keepdims=True) * (1.0 / C) + EPS)
            y_rows[at, :] = y
            inv_rows[at, :] = jnp.broadcast_to(inverse, (rows_each, LANES))
            normed[at, :] = (y * inverse * gain[...]).astype(BF16)
            cot[at, :] = c.reshape(rows_each, C).astype(BF16)
    for index, weight in enumerate((w_query, w_key, w_value)):
        qkv[:, index * HD : (index + 1) * HD] = nn(normed[...], weight[...]).astype(BF16)
    gatt[...] = nn(cot[...], w_output[...]).astype(BF16)

    square = (rows_each, rows_each)
    same = (lax.broadcasted_iota(jnp.int32, square, 0) % 4) == (
        lax.broadcasted_iota(jnp.int32, square, 1) % 4
    )
    lane = lax.broadcasted_iota(jnp.int32, (rows_each, LANES), 1)

    def split(value):
        zero = jnp.zeros_like(value)
        return jnp.concatenate(
            [jnp.where(lane < DH, value, zero), jnp.where(lane >= DH, value, zero)], axis=0
        )

    for group in range(4):
        at = pl.ds(group * rows_each, rows_each)
        for pair in range(2):
            def part(index):
                return qkv[at, pl.ds(index * HD + pair * LANES, LANES)]

            lanes = pl.ds(pair * LANES, LANES)
            query, key, value = part(0), part(1), part(2)
            grad_att = gatt[at, lanes]
            key2, value2 = split(key), split(value)
            scores = nt(query, key2)
            grad_probs = nt(grad_att, value2)
            lows, grads = [], []
            for head in range(2):
                cut = slice(head * rows_each, (head + 1) * rows_each)
                score = jnp.where(same, scores[:, cut] * scale, MASKED)
                expon = jnp.exp(score - jnp.max(score, axis=-1, keepdims=True))
                probs = expon * (1.0 / jnp.sum(expon, axis=-1, keepdims=True))
                gp = grad_probs[:, cut]
                weighted = probs * gp
                total = jnp.sum(weighted, axis=-1, keepdims=True)
                lows.append(probs.astype(BF16))
                grads.append(((weighted - probs * total) * scale).astype(BF16))
            attended[at, lanes] = nn(jnp.concatenate(lows, axis=1), value2).astype(BF16)
            grad_q = nn(jnp.concatenate(grads, axis=1), key2)
            grad_k = tn(jnp.concatenate(grads, axis=0), split(query))
            grad_v = tn(jnp.concatenate(lows, axis=0), split(grad_att))
            for index, grad in enumerate((grad_q, grad_k, grad_v)):
                stacked[at, pl.ds(index * HD + pair * LANES, LANES)] = grad.astype(BF16)

    gnorm[...] = (
        nt(stacked[:, :HD], w_query[...])
        + nt(stacked[:, HD : 2 * HD], w_key[...])
        + nt(stacked[:, 2 * HD :], w_value[...])
    )
    total = jnp.zeros((8, C), F32)
    for tile in range(2):
        results = []
        for half in range(2):
            at = pl.ds((2 * tile + half) * rows_each, rows_each)
            y = y_rows[at, :]
            inverse = inv_rows[at, :][:, :1]
            grad = gnorm[at, :]
            total = total + jnp.sum((grad * y * inverse).reshape(GROUPS, 8, C), axis=0)
            gained = grad * gain[...]
            mean = jnp.sum(gained * y, axis=-1, keepdims=True) * (1.0 / C)
            result = inverse * (gained - y * (mean * inverse * inverse))
            results.append(result.reshape(GROUPS, 8, C))
        for s, whole in enumerate(pair_up(*results)):
            out[:, s, 8 * tile : 8 * tile + 8, :] = whole.astype(BF16)
    gain_sum[...] = jnp.sum(total, axis=0, keepdims=True)

    for m in range(4):
        if m < 3:
            whole = tn(normed[...], stacked[:, m * HD : (m + 1) * HD])
        else:
            whole = tn(cot[...], attended[...])
        tiles = (whole * predivide).reshape(8, 2, 2, 2, 8, HD)
        for z in range(2):
            for core in range(2):
                away_core, away_z = (core_of(spot) + core) % 2, (side_of(spot) + z) % 2
                for high in range(2):
                    for side in range(2):
                        piece = tiles[:, z, core, high, :, side * LANES : (side + 1) * LANES]
                        halves[away_core, away_z, 4 * m + 2 * high + side] = piece.reshape(
                            ROWS, LANES
                        ).astype(BF16)


def add_cores_kernel(kept, got, keep, send):
    keep[...] = (kept[0, 0].astype(F32) + got[0].astype(F32)).astype(BF16)
    send[...] = (kept[0, 1].astype(F32) + got[1].astype(F32)).astype(BF16)


def add_chips_kernel(kept, got, out):
    out[:, :ROWS, :] = (kept[...].astype(F32) + got[...].astype(F32)).astype(BF16)
    out[:, ROWS:, :] = jnp.zeros((GROUPS, 16, LANES), BF16)


def taps_kernel(
    predivide, spot, lat, other_core, other_chip, cot, ret, gain_sum, sums_in,
    out, edge_l, edge_r, tiles, packed, sem,
):
    del sums_in
    tiles[...] = jnp.zeros_like(tiles)
    for s in range(SL):
        left, right = from_partners(spot, other_core[s].astype(F32), other_chip[s].astype(F32))
        edge_l[s] = silu(left)
        edge_r[s] = silu(right)
    rows = row_index(WL)

    @pl.loop(0, PARTS)
    def _(part):
        here = lanes_of(part)
        sums = [jnp.zeros((8, LANES), F32) for _ in range(10)]
        for s in range(SL):
            grads, cols = [], []
            for h in range(H):
                back = jnp.concatenate(
                    [ret[2 * h, s, :, here].astype(F32), ret[2 * h + 1, s, :, here].astype(F32)],
                    axis=0,
                )
                grads.append(cot[s, h, :, here].astype(F32) + back)
                act = silu(lat[s, h, :, here].astype(F32))
                cols.append(
                    (
                        jnp.where(rows == 0, edge_l[s, h : h + 1, here], pltpu.roll(act, 1, 0)),
                        act,
                        jnp.where(
                            rows == WL - 1, edge_r[s, h : h + 1, here], pltpu.roll(act, WL - 1, 0)
                        ),
                    )
                )
            for h in range(H):
                for a in range(3):
                    if 0 <= h + a - 1 < H:
                        for b in range(3):
                            term = (grads[h] * cols[h + a - 1][b]).reshape(4, 8, LANES)
                            sums[3 * a + b] = sums[3 * a + b] + jnp.sum(term, axis=0)
                sums[9] = sums[9] + jnp.sum(grads[h].reshape(4, 8, LANES), axis=0)
        for r in range(10):
            tiles[4 * part + r // 3, pl.ds(r % 3, 1), :] = jnp.sum(sums[r], axis=0, keepdims=True)
        tiles[4 * part + 3, pl.ds(1, 1), :] = gain_sum[:, here]

    whole = tiles[...] * predivide
    high = whole.astype(BF16).astype(F32)
    packed[...] = jnp.concatenate([high, whole - high], axis=1).astype(BF16)
    copy = pltpu.make_async_copy(packed, out.at[:, pl.ds(ROWS, 16), :], sem)
    copy.start()
    copy.wait()


def back_edges_kernel(for_core, spot, after, cot, ret, out, edges):
    del after
    for s in range(SL):
        for h in range(H):
            at = pl.ds(h, 1)
            edges[0, 0, s, at, :] = cot[s, h, :PX, :].astype(F32)[:1]
            edges[1, 0, s, at, :] = cot[s, h, PX:, :].astype(F32)[PX - 1 :]
            edges[0, 1, s, at, :] = ret[2 * h, s].astype(F32)[:1]
            edges[1, 1, s, at, :] = ret[2 * h + 1, s].astype(F32)[PX - 1 :]
    out[...] = partner_column(spot, for_core, edges[0], edges[1]).astype(BF16)


def latents_kernel(spot, after, lat, cot, ret, other_core, other_chip, taps, out, edge_l, edge_r):
    del after
    for s in range(SL):
        left, right = from_partners(
            spot,
            other_core[0, s].astype(F32) + other_core[1, s].astype(F32),
            other_chip[0, s].astype(F32) + other_chip[1, s].astype(F32),
        )
        below, here, above = row_shifts(left)
        edge_l[s] = taps[2:3, :] * above + taps[5:6, :] * here + taps[8:9, :] * below
        below, here, above = row_shifts(right)
        edge_r[s] = taps[0:1, :] * above + taps[3:4, :] * here + taps[6:7, :] * below
    rows = row_index(WL)

    @pl.loop(0, SL * PARTS)
    def _(step):
        s = step // PARTS
        here = lanes_of(step % PARTS)
        tap = [taps[t : t + 1, here] for t in range(9)]
        grads = []
        for h in range(H):
            back = jnp.concatenate(
                [ret[2 * h, s, :, here].astype(F32), ret[2 * h + 1, s, :, here].astype(F32)],
                axis=0,
            )
            grads.append(cot[s, h, :, here].astype(F32) + back)
        for h in range(H):
            cols = []
            for b in range(3):
                terms = [
                    tap[3 * a + b] * grads[h - a + 1] for a in range(3) if 0 <= h - a + 1 < H
                ]
                cols.append(functools.reduce(jnp.add, terms))
            from_left = jnp.where(
                rows == 0, edge_l[s, h : h + 1, here], pltpu.roll(cols[2], 1, 0)
            )
            from_right = jnp.where(
                rows == WL - 1, edge_r[s, h : h + 1, here], pltpu.roll(cols[0], WL - 1, 0)
            )
            total = cols[1] + from_left + from_right
            value = lat[s, h, :, here].astype(F32)
            sig = 1.0 / (1.0 + jnp.exp(-value))
            out[s, h, :, here] = grads[h] + total * (sig * (1.0 + value * (1.0 - sig)))


def second_kernel(spot, recv, out):
    total = jnp.sum(recv[...].astype(F32), axis=0)
    weights = total[:ROWS].reshape(8, 8, LANES)
    taps = total[ROWS : ROWS + 8] + total[ROWS + 8 :]
    high = taps.astype(BF16).astype(F32)
    low = taps - high
    at = lax.broadcasted_iota(jnp.int32, (8, LANES), 0)
    both = jnp.where(at < 4, high, pltpu.roll(low, 4, 0))
    for z in range(2):
        for core in range(2):
            own = jnp.where(jnp.logical_and(core_of(spot) == core, side_of(spot) == z), 1.0, 0.0)
            for block in range(8):
                out[4 * block + 2 * z + core] = jnp.concatenate(
                    [weights[block] * own, both], axis=0
                ).astype(BF16)


def third_kernel(recv, out):
    total = jnp.sum(recv[...].astype(F32), axis=0)
    both = total[8:]
    taps = both + pltpu.roll(both, 4, 0)
    result = jnp.concatenate([total[:8], taps], axis=0)
    for s in range(GROUPS):
        out[s] = result


def unpack_kernel(recv, kernel_out, bias_out, gain_out, *outs):
    for part in range(PARTS):
        here = slice(part * LANES, (part + 1) * LANES)
        for r in range(11):
            row = recv[4 * part + r // 3, 8 + r % 3 : 9 + r % 3, :]
            if r < 9:
                kernel_out[r : r + 1, here] = row
            elif r == 9:
                bias_out[:, here] = row
            else:
                gain_out[:, here] = row
    for m in range(4):
        for high in range(2):
            for side in range(2):
                outs[m][8 * high : 8 * high + 8, side * LANES : (side + 1) * LANES] = recv[
                    4 * m + 2 * high + side, :8, :
                ]


def on_device(
    latents, cotangent, conv_kernel, conv_bias, norm_gain, w_query, w_key, w_value, w_output
):
    strips = lax.axis_size("azim")
    groups = lax.axis_size("sweep")
    cores = [(i, i ^ 1) for i in range(strips)]
    chips = [(i, (i + 1 if i % 2 else i - 1) % strips) for i in range(strips)]
    sides = [(i, i ^ 2) for i in range(strips)]
    strip = lax.axis_index("azim")
    spot = strip.astype(jnp.int32).reshape(1)
    predivide = 1.0 / math.sqrt(SL * groups * H * WL * strips)
    bias_row = conv_bias.reshape(1, C)
    gain_row = norm_gain.reshape(1, C)
    edge = pltpu.VMEM((SL, H, C), F32)

    one_edge = struct((SL, H, C), BF16)
    column = [pltpu.VMEM((2, SL, H, C), F32)]
    to_chip = call(chip_edge_kernel, one_edge, 16, moved=600_000, smem=1, scratch=column)(
        spot, latents
    )
    other_chip = lax.ppermute(to_chip, "azim", chips)
    to_core, table = call(
        core_edge_kernel,
        (one_edge, struct((16, C), F32)),
        16,
        moved=600_000,
        smem=1,
        hbm=(1,),
        scratch=column,
    )(spot, to_chip, latents, conv_kernel, bias_row)
    other_core = lax.ppermute(to_core, "azim", cores)

    sent = call(
        forward_kernel,
        struct((GROUPS, 2, SL, PX, C), BF16),
        16,
        flops=10_000_000,
        moved=2_000_000,
        smem=1,
        scratch=[edge, edge],
    )(spot, latents, cotangent, other_core, other_chip, table)
    recv = lax.all_to_all(sent, "sweep", split_axis=0, concat_axis=0, tiled=True)

    rows = GROUPS * SL * PX
    grad_attn, halves, gain_sum = call(
        functools.partial(attend_kernel, predivide),
        (
            struct((GROUPS, SL, PX, C), BF16),
            struct((2, 2, GROUPS, ROWS, LANES), BF16),
            struct((1, C), F32),
        ),
        32,
        flops=2_000_000_000,
        moved=6_000_000,
        smem=1,
        scratch=[
            pltpu.VMEM((rows, C), BF16),
            pltpu.VMEM((rows, 3 * HD), BF16),
            pltpu.VMEM((rows, HD), BF16),
            pltpu.VMEM((rows, C), BF16),
            pltpu.VMEM((rows, C), F32),
            pltpu.VMEM((rows, LANES), F32),
            pltpu.VMEM((rows, 3 * HD), BF16),
            pltpu.VMEM((rows, HD), BF16),
            pltpu.VMEM((rows, C), F32),
        ],
    )(spot, recv, w_query, w_key, w_value, w_output, gain_row)
    ret = lax.all_to_all(grad_attn, "sweep", split_axis=0, concat_axis=0, tiled=True)
    from_core = lax.ppermute(halves[1], "azim", cores)
    piece = struct((GROUPS, ROWS, LANES), BF16)
    keep, send = call(add_cores_kernel, (piece, piece), 16, moved=2_000_000)(halves, from_core)
    from_chip = lax.ppermute(send, "azim", sides)
    payload = struct((GROUPS, ROWS + 16, LANES), BF16)
    sums = call(add_chips_kernel, payload, 16, moved=1_000_000)(keep, from_chip)

    vmem = pl.BlockSpec(memory_space=pltpu.VMEM)
    anywhere = pl.BlockSpec(memory_space=pltpu.HBM)
    first_sent = pl.pallas_call(
        functools.partial(taps_kernel, predivide),
        out_shape=payload,
        in_specs=[pl.BlockSpec(memory_space=pltpu.SMEM)] + [vmem] * 6 + [anywhere],
        out_specs=anywhere,
        input_output_aliases={7: 0},
        scratch_shapes=[
            edge,
            edge,
            pltpu.VMEM((GROUPS, 8, LANES), F32),
            pltpu.VMEM((GROUPS, 16, LANES), BF16),
            pltpu.SemaphoreType.DMA,
        ],
        compiler_params=params(16),
        cost_estimate=pl.CostEstimate(
            flops=10_000_000, bytes_accessed=2_000_000, transcendentals=0
        ),
    )(spot, latents, other_core, other_chip, cotangent, ret, gain_sum, sums)
    first_recv = lax.all_to_all(first_sent, "sweep", split_axis=0, concat_axis=0, tiled=True)
    both_edges = struct((2, SL, H, C), BF16)
    second_sent = call(
        second_kernel, struct((strips, 16, LANES), BF16), 16, moved=1_000_000, smem=1
    )(spot, first_recv)
    second_recv = lax.all_to_all(second_sent, "azim", split_axis=0, concat_axis=0, tiled=True)

    def back_edges(for_core, after):
        return call(
            functools.partial(back_edges_kernel, for_core),
            both_edges,
            16,
            moved=100_000,
            smem=1,
            hbm=(1,),
            scratch=[pltpu.VMEM((2, 2, SL, H, C), F32)],
        )(spot, after, cotangent, ret)

    to_chip = back_edges(False, second_sent)
    back_chip = lax.ppermute(to_chip, "azim", chips)
    back_core = lax.ppermute(back_edges(True, to_chip), "azim", cores)

    grad_latents = call(
        latents_kernel,
        struct((SL, H, WL, C), F32),
        16,
        flops=10_000_000,
        moved=4_000_000,
        smem=1,
        hbm=(1,),
        scratch=[edge, edge],
    )(spot, second_sent, latents, cotangent, ret, back_core, back_chip, table)

    second_recv, grad_latents = lax.optimization_barrier((second_recv, grad_latents))
    third_sent = call(third_kernel, struct((GROUPS, 16, LANES), F32), 16, moved=300_000)(
        second_recv
    )
    third_recv = lax.all_to_all(third_sent, "sweep", split_axis=0, concat_axis=0, tiled=True)
    share = struct((C // strips, HD), F32)
    line = struct((1, C), F32)
    grad_kernel, grad_bias, grad_gain, *shares = call(
        unpack_kernel,
        (struct((9, C), F32), line, line, share, share, share, share),
        16,
        moved=300_000,
    )(third_recv)
    return (
        grad_latents,
        grad_kernel,
        grad_bias.reshape(C),
        grad_gain.reshape(C),
        shares[0],
        shares[1],
        shares[2],
        shares[3],
    )


def solution(mesh):
    image = P("sweep", None, "azim", None)
    share = P("azim", None)
    return jax.shard_map(
        on_device,
        mesh=mesh,
        in_specs=(image, image, P(), P(), P(), P(), P(), P(), P()),
        out_specs=(image, P(), P(), P(), share, share, share, share),
        check_vma=False,
    )
```

```python
import functools
import math

import jax
import jax.numpy as jnp
from jax import lax
from jax.experimental import pallas as pl
from jax.experimental.pallas import tpu as pltpu
from jax.sharding import PartitionSpec as P

DH = 64
EPS = 1e-06
F32 = jnp.float32
BF16 = jnp.bfloat16
MASKED = -1e30

SL, H, WL, C = 2, 8, 32, 512
GROUPS = 16
PX = 16
HD = 256
LANES = 128
PARTS = C // LANES
ROWS = 64


def params(mib):
    return pltpu.CompilerParams(vmem_limit_bytes=mib * 1024 * 1024)


def call(kernel, outs, mib, flops=0, moved=0, scratch=(), smem=0, hbm=()):
    vmem = pl.BlockSpec(memory_space=pltpu.VMEM)

    def run(*args):
        specs = [pl.BlockSpec(memory_space=pltpu.SMEM)] * smem + [vmem] * (len(args) - smem)
        for at in hbm:
            specs[at] = pl.BlockSpec(memory_space=pltpu.HBM)
        return pl.pallas_call(
            kernel,
            out_shape=outs,
            in_specs=specs,
            out_specs=jax.tree.map(lambda _: vmem, outs),
            scratch_shapes=list(scratch),
            compiler_params=params(mib),
            cost_estimate=pl.CostEstimate(
                flops=flops, bytes_accessed=moved, transcendentals=0
            ),
        )(*args)

    return run


def struct(shape, dtype):
    return jax.ShapeDtypeStruct(shape, dtype)


def silu(value):
    return value / (1.0 + jnp.exp(-value))


def nt(left, right):
    return lax.dot_general(left, right, (((1,), (1,)), ((), ())), preferred_element_type=F32)


def tn(left, right):
    return lax.dot_general(left, right, (((0,), (0,)), ((), ())), preferred_element_type=F32)


def nn(left, right):
    return lax.dot_general(left, right, (((1,), (0,)), ((), ())), preferred_element_type=F32)


def lanes_of(part):
    return pl.ds(pl.multiple_of(part * LANES, LANES), LANES)


def row_index(rows):
    return lax.broadcasted_iota(jnp.int32, (rows, LANES), 0)


def row_shifts(value):
    at = lax.broadcasted_iota(jnp.int32, value.shape, 0)
    below = jnp.where(at == 0, 0.0, pltpu.roll(value, 1, 0))
    above = jnp.where(at == H - 1, 0.0, pltpu.roll(value, H - 1, 0))
    return below, value, above


def core_of(spot):
    return spot[0] % 2


def side_of(spot):
    return (spot[0] // 2) % 2


def partner_column(spot, for_core, first, last):
    even = core_of(spot) == 0
    return jnp.where(even, last, first) if for_core else jnp.where(even, first, last)


def from_partners(spot, other_core, other_chip):
    even = core_of(spot) == 0
    return jnp.where(even, other_chip, other_core), jnp.where(even, other_core, other_chip)


def edge_columns(lat, edges):
    for s in range(SL):
        for h in range(H):
            edges[0, s, h : h + 1, :] = lat[s, h, :PX, :].astype(F32)[:1]
            edges[1, s, h : h + 1, :] = lat[s, h, PX:, :].astype(F32)[PX - 1 :]


def pack_kernel(cot, out):
    for s in range(SL):
        for h in range(H):
            out[2 * h, s] = cot[s, h, :PX, :]
            out[2 * h + 1, s] = cot[s, h, PX:, :]


def chip_edge_kernel(spot, after, lat, out, edges):
    del after
    edge_columns(lat, edges)
    out[...] = partner_column(spot, False, edges[0], edges[1]).astype(BF16)


def core_edge_kernel(spot, after, lat, taps, bias, out, table, edges):
    del after
    edge_columns(lat, edges)
    out[...] = partner_column(spot, True, edges[0], edges[1]).astype(BF16)
    table[:9, :] = taps[...]
    table[9:10, :] = bias[...]
    table[10:, :] = jnp.zeros((6, C), F32)


def forward_kernel(spot, lat, other_core, other_chip, taps, out, edge_l, edge_r):
    for s in range(SL):
        left, right = from_partners(spot, other_core[s].astype(F32), other_chip[s].astype(F32))
        shifted = row_shifts(silu(left))
        edge_l[s] = sum(taps[3 * a : 3 * a + 1, :] * shifted[a] for a in range(3))
        shifted = row_shifts(silu(right))
        edge_r[s] = sum(taps[3 * a + 2 : 3 * a + 3, :] * shifted[a] for a in range(3))
    rows = row_index(WL)

    @pl.loop(0, SL * PARTS)
    def _(step):
        s = step // PARTS
        here = lanes_of(step % PARTS)
        tap = [taps[t : t + 1, here] for t in range(9)]
        base = taps[9:10, here]
        values = [lat[s, h, :, here].astype(F32) for h in range(H)]
        acts = [silu(v) for v in values]
        for h in range(H):
            cols = []
            for b in range(3):
                terms = [
                    tap[3 * a + b] * acts[h + a - 1] for a in range(3) if 0 <= h + a - 1 < H
                ]
                cols.append(functools.reduce(jnp.add, terms))
            from_left = jnp.where(
                rows == 0, edge_l[s, h : h + 1, here], pltpu.roll(cols[0], 1, 0)
            )
            from_right = jnp.where(
                rows == WL - 1, edge_r[s, h : h + 1, here], pltpu.roll(cols[2], WL - 1, 0)
            )
            y = (values[h] + (cols[1] + from_left + from_right) + base).astype(BF16)
            out[2 * h, s, :, here] = y[:PX]
            out[2 * h + 1, s, :, here] = y[PX:]


def pair_up(first, second):
    low = lax.broadcasted_iota(jnp.int32, first.shape, 1) < 4
    return (
        jnp.where(low, first, pltpu.roll(second, 4, 1)),
        jnp.where(low, pltpu.roll(first, 4, 1), second),
    )


def attend_kernel(
    predivide, spot, recv, recv_cot, w_query, w_key, w_value, w_output, gain,
    out, halves, gain_sum,
    normed, stacked, attended, cot, y_rows, inv_rows, qkv, gatt, gnorm,
):
    rows_each = GROUPS * 8
    scale = 1.0 / math.sqrt(DH)
    for tile in range(2):
        y_two = [
            recv[:, s].astype(F32)[:, 8 * tile : 8 * tile + 8, :] for s in range(SL)
        ]
        cot_two = [
            recv_cot[:, s].astype(F32)[:, 8 * tile : 8 * tile + 8, :] for s in range(SL)
        ]
        for half, (y, c) in enumerate(zip(pair_up(*y_two), pair_up(*cot_two))):
            at = pl.ds((2 * tile + half) * rows_each, rows_each)
            y = y.reshape(rows_each, C)
            inverse = lax.rsqrt(jnp.sum(y * y, axis=-1, keepdims=True) * (1.0 / C) + EPS)
            y_rows[at, :] = y
            inv_rows[at, :] = jnp.broadcast_to(inverse, (rows_each, LANES))
            normed[at, :] = (y * inverse * gain[...]).astype(BF16)
            cot[at, :] = c.reshape(rows_each, C).astype(BF16)
    for index, weight in enumerate((w_query, w_key, w_value)):
        qkv[:, index * HD : (index + 1) * HD] = nn(normed[...], weight[...]).astype(BF16)
    gatt[...] = nn(cot[...], w_output[...]).astype(BF16)

    square = (rows_each, rows_each)
    same = (lax.broadcasted_iota(jnp.int32, square, 0) % 4) == (
        lax.broadcasted_iota(jnp.int32, square, 1) % 4
    )
    lane = lax.broadcasted_iota(jnp.int32, (rows_each, LANES), 1)

    def split(value):
        zero = jnp.zeros_like(value)
        return jnp.concatenate(
            [jnp.where(lane < DH, value, zero), jnp.where(lane >= DH, value, zero)], axis=0
        )

    for group in range(4):
        at = pl.ds(group * rows_each, rows_each)
        for pair in range(2):
            def part(index):
                return qkv[at, pl.ds(index * HD + pair * LANES, LANES)]

            lanes = pl.ds(pair * LANES, LANES)
            query, key, value = part(0), part(1), part(2)
            grad_att = gatt[at, lanes]
            key2, value2 = split(key), split(value)
            scores = nt(query, key2)
            grad_probs = nt(grad_att, value2)
            lows, grads = [], []
            for head in range(2):
                cut = slice(head * rows_each, (head + 1) * rows_each)
                score = jnp.where(same, scores[:, cut] * scale, MASKED)
                expon = jnp.exp(score - jnp.max(score, axis=-1, keepdims=True))
                probs = expon * (1.0 / jnp.sum(expon, axis=-1, keepdims=True))
                gp = grad_probs[:, cut]
                weighted = probs * gp
                total = jnp.sum(weighted, axis=-1, keepdims=True)
                lows.append(probs.astype(BF16))
                grads.append(((weighted - probs * total) * scale).astype(BF16))
            attended[at, lanes] = nn(jnp.concatenate(lows, axis=1), value2).astype(BF16)
            grad_q = nn(jnp.concatenate(grads, axis=1), key2)
            grad_k = tn(jnp.concatenate(grads, axis=0), split(query))
            grad_v = tn(jnp.concatenate(lows, axis=0), split(grad_att))
            for index, grad in enumerate((grad_q, grad_k, grad_v)):
                stacked[at, pl.ds(index * HD + pair * LANES, LANES)] = grad.astype(BF16)

    gnorm[...] = (
        nt(stacked[:, :HD], w_query[...])
        + nt(stacked[:, HD : 2 * HD], w_key[...])
        + nt(stacked[:, 2 * HD :], w_value[...])
    )
    total = jnp.zeros((8, C), F32)
    for tile in range(2):
        results = []
        for half in range(2):
            at = pl.ds((2 * tile + half) * rows_each, rows_each)
            y = y_rows[at, :]
            inverse = inv_rows[at, :][:, :1]
            grad = gnorm[at, :]
            total = total + jnp.sum((grad * y * inverse).reshape(GROUPS, 8, C), axis=0)
            gained = grad * gain[...]
            mean = jnp.sum(gained * y, axis=-1, keepdims=True) * (1.0 / C)
            result = inverse * (gained - y * (mean * inverse * inverse))
            results.append(result.reshape(GROUPS, 8, C))
        for s, whole in enumerate(pair_up(*results)):
            out[:, s, 8 * tile : 8 * tile + 8, :] = whole.astype(BF16)
    gain_sum[...] = jnp.sum(total, axis=0, keepdims=True)

    for m in range(4):
        if m < 3:
            whole = tn(normed[...], stacked[:, m * HD : (m + 1) * HD])
        else:
            whole = tn(cot[...], attended[...])
        tiles = (whole * predivide).reshape(8, 2, 2, 2, 8, HD)
        for z in range(2):
            for core in range(2):
                away_core, away_z = (core_of(spot) + core) % 2, (side_of(spot) + z) % 2
                for high in range(2):
                    for side in range(2):
                        piece = tiles[:, z, core, high, :, side * LANES : (side + 1) * LANES]
                        halves[away_core, away_z, 4 * m + 2 * high + side] = piece.reshape(
                            ROWS, LANES
                        ).astype(BF16)


def add_cores_kernel(kept, got, keep, send):
    keep[...] = (kept[0, 0].astype(F32) + got[0].astype(F32)).astype(BF16)
    send[...] = (kept[0, 1].astype(F32) + got[1].astype(F32)).astype(BF16)


def add_chips_kernel(kept, got, out):
    out[:, :ROWS, :] = (kept[...].astype(F32) + got[...].astype(F32)).astype(BF16)
    out[:, ROWS:, :] = jnp.zeros((GROUPS, 16, LANES), BF16)


def taps_kernel(
    predivide, spot, lat, other_core, other_chip, cot, ret, gain_sum, sums_in,
    out, edge_l, edge_r, tiles, packed, sem,
):
    del sums_in
    tiles[...] = jnp.zeros_like(tiles)
    for s in range(SL):
        left, right = from_partners(spot, other_core[s].astype(F32), other_chip[s].astype(F32))
        edge_l[s] = silu(left)
        edge_r[s] = silu(right)
    rows = row_index(WL)

    @pl.loop(0, PARTS)
    def _(part):
        here = lanes_of(part)
        sums = [jnp.zeros((8, LANES), F32) for _ in range(10)]
        for s in range(SL):
            grads, cols = [], []
            for h in range(H):
                back = jnp.concatenate(
                    [ret[2 * h, s, :, here].astype(F32), ret[2 * h + 1, s, :, here].astype(F32)],
                    axis=0,
                )
                grads.append(cot[s, h, :, here].astype(F32) + back)
                act = silu(lat[s, h, :, here].astype(F32))
                cols.append(
                    (
                        jnp.where(rows == 0, edge_l[s, h : h + 1, here], pltpu.roll(act, 1, 0)),
                        act,
                        jnp.where(
                            rows == WL - 1, edge_r[s, h : h + 1, here], pltpu.roll(act, WL - 1, 0)
                        ),
                    )
                )
            for h in range(H):
                for a in range(3):
                    if 0 <= h + a - 1 < H:
                        for b in range(3):
                            term = (grads[h] * cols[h + a - 1][b]).reshape(4, 8, LANES)
                            sums[3 * a + b] = sums[3 * a + b] + jnp.sum(term, axis=0)
                sums[9] = sums[9] + jnp.sum(grads[h].reshape(4, 8, LANES), axis=0)
        for r in range(10):
            tiles[4 * part + r // 3, pl.ds(r % 3, 1), :] = jnp.sum(sums[r], axis=0, keepdims=True)
        tiles[4 * part + 3, pl.ds(1, 1), :] = gain_sum[:, here]

    whole = tiles[...] * predivide
    high = whole.astype(BF16).astype(F32)
    packed[...] = jnp.concatenate([high, whole - high], axis=1).astype(BF16)
    copy = pltpu.make_async_copy(packed, out.at[:, pl.ds(ROWS, 16), :], sem)
    copy.start()
    copy.wait()


def back_edges_kernel(for_core, spot, after, cot, ret, out, edges):
    del after
    for s in range(SL):
        for h in range(H):
            at = pl.ds(h, 1)
            edges[0, 0, s, at, :] = cot[s, h, :PX, :].astype(F32)[:1]
            edges[1, 0, s, at, :] = cot[s, h, PX:, :].astype(F32)[PX - 1 :]
            edges[0, 1, s, at, :] = ret[2 * h, s].astype(F32)[:1]
            edges[1, 1, s, at, :] = ret[2 * h + 1, s].astype(F32)[PX - 1 :]
    out[...] = partner_column(spot, for_core, edges[0], edges[1]).astype(BF16)


def latents_kernel(spot, after, lat, cot, ret, other_core, other_chip, taps, out, edge_l, edge_r):
    del after
    for s in range(SL):
        left, right = from_partners(
            spot,
            other_core[0, s].astype(F32) + other_core[1, s].astype(F32),
            other_chip[0, s].astype(F32) + other_chip[1, s].astype(F32),
        )
        below, here, above = row_shifts(left)
        edge_l[s] = taps[2:3, :] * above + taps[5:6, :] * here + taps[8:9, :] * below
        below, here, above = row_shifts(right)
        edge_r[s] = taps[0:1, :] * above + taps[3:4, :] * here + taps[6:7, :] * below
    rows = row_index(WL)

    @pl.loop(0, SL * PARTS)
    def _(step):
        s = step // PARTS
        here = lanes_of(step % PARTS)
        tap = [taps[t : t + 1, here] for t in range(9)]
        grads = []
        for h in range(H):
            back = jnp.concatenate(
                [ret[2 * h, s, :, here].astype(F32), ret[2 * h + 1, s, :, here].astype(F32)],
                axis=0,
            )
            grads.append(cot[s, h, :, here].astype(F32) + back)
        for h in range(H):
            cols = []
            for b in range(3):
                terms = [
                    tap[3 * a + b] * grads[h - a + 1] for a in range(3) if 0 <= h - a + 1 < H
                ]
                cols.append(functools.reduce(jnp.add, terms))
            from_left = jnp.where(
                rows == 0, edge_l[s, h : h + 1, here], pltpu.roll(cols[2], 1, 0)
            )
            from_right = jnp.where(
                rows == WL - 1, edge_r[s, h : h + 1, here], pltpu.roll(cols[0], WL - 1, 0)
            )
            total = cols[1] + from_left + from_right
            value = lat[s, h, :, here].astype(F32)
            sig = 1.0 / (1.0 + jnp.exp(-value))
            out[s, h, :, here] = grads[h] + total * (sig * (1.0 + value * (1.0 - sig)))


def second_kernel(spot, recv, after_chip, after_core, out):
    del after_chip, after_core
    total = jnp.sum(recv[...].astype(F32), axis=0)
    weights = total[:ROWS].reshape(8, 8, LANES)
    taps = total[ROWS : ROWS + 8] + total[ROWS + 8 :]
    high = taps.astype(BF16).astype(F32)
    low = taps - high
    at = lax.broadcasted_iota(jnp.int32, (8, LANES), 0)
    both = jnp.where(at < 4, high, pltpu.roll(low, 4, 0))
    for z in range(2):
        for core in range(2):
            own = jnp.where(jnp.logical_and(core_of(spot) == core, side_of(spot) == z), 1.0, 0.0)
            for block in range(8):
                out[4 * block + 2 * z + core] = jnp.concatenate(
                    [weights[block] * own, both], axis=0
                ).astype(BF16)


def third_kernel(recv, out):
    total = jnp.sum(recv[...].astype(F32), axis=0)
    both = total[8:]
    taps = both + pltpu.roll(both, 4, 0)
    result = jnp.concatenate([total[:8], taps], axis=0)
    for s in range(GROUPS):
        out[s] = result


def unpack_kernel(recv, kernel_out, bias_out, gain_out, *outs):
    for part in range(PARTS):
        here = slice(part * LANES, (part + 1) * LANES)
        for r in range(11):
            row = recv[4 * part + r // 3, 8 + r % 3 : 9 + r % 3, :]
            if r < 9:
                kernel_out[r : r + 1, here] = row
            elif r == 9:
                bias_out[:, here] = row
            else:
                gain_out[:, here] = row
    for m in range(4):
        for high in range(2):
            for side in range(2):
                outs[m][8 * high : 8 * high + 8, side * LANES : (side + 1) * LANES] = recv[
                    4 * m + 2 * high + side, :8, :
                ]


def on_device(
    latents, cotangent, conv_kernel, conv_bias, norm_gain, w_query, w_key, w_value, w_output
):
    strips = lax.axis_size("azim")
    groups = lax.axis_size("sweep")
    cores = [(i, i ^ 1) for i in range(strips)]
    chips = [(i, (i + 1 if i % 2 else i - 1) % strips) for i in range(strips)]
    sides = [(i, i ^ 2) for i in range(strips)]
    strip = lax.axis_index("azim")
    spot = strip.astype(jnp.int32).reshape(1)
    predivide = 1.0 / math.sqrt(SL * groups * H * WL * strips)
    bias_row = conv_bias.reshape(1, C)
    gain_row = norm_gain.reshape(1, C)
    edge = pltpu.VMEM((SL, H, C), F32)

    one_edge = struct((SL, H, C), BF16)
    column = [pltpu.VMEM((2, SL, H, C), F32)]
    packed = struct((GROUPS, SL, PX, C), BF16)
    cot_sent = call(pack_kernel, packed, 16, moved=1_000_000)(cotangent)
    recv_cot = lax.all_to_all(cot_sent, "sweep", split_axis=0, concat_axis=0, tiled=True)
    to_chip = call(
        chip_edge_kernel, one_edge, 16, moved=600_000, smem=1, hbm=(1,), scratch=column
    )(spot, cot_sent, latents)
    other_chip = lax.ppermute(to_chip, "azim", chips)
    to_core, table = call(
        core_edge_kernel,
        (one_edge, struct((16, C), F32)),
        16,
        moved=600_000,
        smem=1,
        hbm=(1,),
        scratch=column,
    )(spot, to_chip, latents, conv_kernel, bias_row)
    other_core = lax.ppermute(to_core, "azim", cores)

    sent = call(
        forward_kernel,
        packed,
        16,
        flops=10_000_000,
        moved=1_000_000,
        smem=1,
        scratch=[edge, edge],
    )(spot, latents, other_core, other_chip, table)
    recv = lax.all_to_all(sent, "sweep", split_axis=0, concat_axis=0, tiled=True)

    rows = GROUPS * SL * PX
    grad_attn, halves, gain_sum = call(
        functools.partial(attend_kernel, predivide),
        (
            struct((GROUPS, SL, PX, C), BF16),
            struct((2, 2, GROUPS, ROWS, LANES), BF16),
            struct((1, C), F32),
        ),
        32,
        flops=2_000_000_000,
        moved=6_000_000,
        smem=1,
        scratch=[
            pltpu.VMEM((rows, C), BF16),
            pltpu.VMEM((rows, 3 * HD), BF16),
            pltpu.VMEM((rows, HD), BF16),
            pltpu.VMEM((rows, C), BF16),
            pltpu.VMEM((rows, C), F32),
            pltpu.VMEM((rows, LANES), F32),
            pltpu.VMEM((rows, 3 * HD), BF16),
            pltpu.VMEM((rows, HD), BF16),
            pltpu.VMEM((rows, C), F32),
        ],
    )(spot, recv, recv_cot, w_query, w_key, w_value, w_output, gain_row)
    ret = lax.all_to_all(grad_attn, "sweep", split_axis=0, concat_axis=0, tiled=True)
    from_core = lax.ppermute(halves[1], "azim", cores)
    piece = struct((GROUPS, ROWS, LANES), BF16)
    keep, send = call(add_cores_kernel, (piece, piece), 16, moved=2_000_000)(halves, from_core)
    from_chip = lax.ppermute(send, "azim", sides)
    payload = struct((GROUPS, ROWS + 16, LANES), BF16)
    sums = call(add_chips_kernel, payload, 16, moved=1_000_000)(keep, from_chip)

    vmem = pl.BlockSpec(memory_space=pltpu.VMEM)
    anywhere = pl.BlockSpec(memory_space=pltpu.HBM)
    first_sent = pl.pallas_call(
        functools.partial(taps_kernel, predivide),
        out_shape=payload,
        in_specs=[pl.BlockSpec(memory_space=pltpu.SMEM)] + [vmem] * 6 + [anywhere],
        out_specs=anywhere,
        input_output_aliases={7: 0},
        scratch_shapes=[
            edge,
            edge,
            pltpu.VMEM((GROUPS, 8, LANES), F32),
            pltpu.VMEM((GROUPS, 16, LANES), BF16),
            pltpu.SemaphoreType.DMA,
        ],
        compiler_params=params(16),
        cost_estimate=pl.CostEstimate(
            flops=10_000_000, bytes_accessed=2_000_000, transcendentals=0
        ),
    )(spot, latents, other_core, other_chip, cotangent, ret, gain_sum, sums)
    first_recv = lax.all_to_all(first_sent, "sweep", split_axis=0, concat_axis=0, tiled=True)
    both_edges = struct((2, SL, H, C), BF16)

    def back_edges(for_core, after):
        return call(
            functools.partial(back_edges_kernel, for_core),
            both_edges,
            16,
            moved=100_000,
            smem=1,
            hbm=(1,),
            scratch=[pltpu.VMEM((2, 2, SL, H, C), F32)],
        )(spot, after, cotangent, ret)

    to_chip = back_edges(False, first_sent)
    back_chip = lax.ppermute(to_chip, "azim", chips)
    to_core = back_edges(True, to_chip)
    back_core = lax.ppermute(to_core, "azim", cores)

    second_sent = call(
        second_kernel, struct((strips, 16, LANES), BF16), 16, moved=1_000_000, smem=1, hbm=(2, 3)
    )(spot, first_recv, back_chip, back_core)
    second_recv = lax.all_to_all(second_sent, "azim", split_axis=0, concat_axis=0, tiled=True)

    third_sent = call(third_kernel, struct((GROUPS, 16, LANES), F32), 16, moved=300_000)(
        second_recv
    )
    third_recv = lax.all_to_all(third_sent, "sweep", split_axis=0, concat_axis=0, tiled=True)

    grad_latents = call(
        latents_kernel,
        struct((SL, H, WL, C), F32),
        16,
        flops=10_000_000,
        moved=4_000_000,
        smem=1,
        hbm=(1,),
        scratch=[edge, edge],
    )(spot, third_sent, latents, cotangent, ret, back_core, back_chip, table)

    share = struct((C // strips, HD), F32)
    line = struct((1, C), F32)
    grad_kernel, grad_bias, grad_gain, *shares = call(
        unpack_kernel,
        (struct((9, C), F32), line, line, share, share, share, share),
        16,
        moved=300_000,
    )(third_recv)
    return (
        grad_latents,
        grad_kernel,
        grad_bias.reshape(C),
        grad_gain.reshape(C),
        shares[0],
        shares[1],
        shares[2],
        shares[3],
    )


def solution(mesh):
    image = P("sweep", None, "azim", None)
    share = P("azim", None)
    return jax.shard_map(
        on_device,
        mesh=mesh,
        in_specs=(image, image, P(), P(), P(), P(), P(), P(), P()),
        out_specs=(image, P(), P(), P(), share, share, share, share),
        check_vma=False,
    )
```

```python
import functools
import math

import jax
import jax.numpy as jnp
from jax import lax
from jax.experimental import pallas as pl
from jax.experimental.pallas import tpu as pltpu
from jax.sharding import PartitionSpec as P

DH = 64
EPS = 1e-06
F32 = jnp.float32
BF16 = jnp.bfloat16
MASKED = -1e30

SL, H, WL, C = 2, 8, 32, 512
GROUPS = 16
PX = 16
HD = 256
LANES = 128
PARTS = C // LANES
ROWS = 64


def params(mib):
    return pltpu.CompilerParams(vmem_limit_bytes=mib * 1024 * 1024)


def call(kernel, outs, mib, flops=0, moved=0, scratch=(), smem=0, hbm=()):
    vmem = pl.BlockSpec(memory_space=pltpu.VMEM)

    def run(*args):
        specs = [pl.BlockSpec(memory_space=pltpu.SMEM)] * smem + [vmem] * (len(args) - smem)
        for at in hbm:
            specs[at] = pl.BlockSpec(memory_space=pltpu.HBM)
        return pl.pallas_call(
            kernel,
            out_shape=outs,
            in_specs=specs,
            out_specs=jax.tree.map(lambda _: vmem, outs),
            scratch_shapes=list(scratch),
            compiler_params=params(mib),
            cost_estimate=pl.CostEstimate(
                flops=flops, bytes_accessed=moved, transcendentals=0
            ),
        )(*args)

    return run


def struct(shape, dtype):
    return jax.ShapeDtypeStruct(shape, dtype)


def silu(value):
    return value / (1.0 + jnp.exp(-value))


def nt(left, right):
    return lax.dot_general(left, right, (((1,), (1,)), ((), ())), preferred_element_type=F32)


def tn(left, right):
    return lax.dot_general(left, right, (((0,), (0,)), ((), ())), preferred_element_type=F32)


def nn(left, right):
    return lax.dot_general(left, right, (((1,), (0,)), ((), ())), preferred_element_type=F32)


def lanes_of(part):
    return pl.ds(pl.multiple_of(part * LANES, LANES), LANES)


def row_index(rows):
    return lax.broadcasted_iota(jnp.int32, (rows, LANES), 0)


def row_shifts(value):
    at = lax.broadcasted_iota(jnp.int32, value.shape, 0)
    below = jnp.where(at == 0, 0.0, pltpu.roll(value, 1, 0))
    above = jnp.where(at == H - 1, 0.0, pltpu.roll(value, H - 1, 0))
    return below, value, above


def core_of(spot):
    return spot[0] % 2


def side_of(spot):
    return (spot[0] // 2) % 2


def partner_column(spot, for_core, first, last):
    even = core_of(spot) == 0
    return jnp.where(even, last, first) if for_core else jnp.where(even, first, last)


def from_partners(spot, other_core, other_chip):
    even = core_of(spot) == 0
    return jnp.where(even, other_chip, other_core), jnp.where(even, other_core, other_chip)


def edge_columns(lat, edges):
    for s in range(SL):
        for h in range(H):
            edges[0, s, h : h + 1, :] = lat[s, h, :PX, :].astype(F32)[:1]
            edges[1, s, h : h + 1, :] = lat[s, h, PX:, :].astype(F32)[PX - 1 :]


def pack_kernel(cot, out):
    for s in range(SL):
        for h in range(H):
            out[2 * h, s] = cot[s, h, :PX, :]
            out[2 * h + 1, s] = cot[s, h, PX:, :]


def chip_edge_kernel(spot, after, lat, out, edges):
    del after
    edge_columns(lat, edges)
    out[...] = partner_column(spot, False, edges[0], edges[1]).astype(BF16)


def core_edge_kernel(spot, after, lat, taps, bias, out, table, edges):
    del after
    edge_columns(lat, edges)
    out[...] = partner_column(spot, True, edges[0], edges[1]).astype(BF16)
    table[:9, :] = taps[...]
    table[9:10, :] = bias[...]
    table[10:, :] = jnp.zeros((6, C), F32)


def forward_kernel(spot, lat, other_core, other_chip, taps, out, edge_l, edge_r):
    for s in range(SL):
        left, right = from_partners(spot, other_core[s].astype(F32), other_chip[s].astype(F32))
        shifted = row_shifts(silu(left))
        edge_l[s] = sum(taps[3 * a : 3 * a + 1, :] * shifted[a] for a in range(3))
        shifted = row_shifts(silu(right))
        edge_r[s] = sum(taps[3 * a + 2 : 3 * a + 3, :] * shifted[a] for a in range(3))
    rows = row_index(WL)

    @pl.loop(0, SL * PARTS)
    def _(step):
        s = step // PARTS
        here = lanes_of(step % PARTS)
        tap = [taps[t : t + 1, here] for t in range(9)]
        base = taps[9:10, here]
        values = [lat[s, h, :, here].astype(F32) for h in range(H)]
        acts = [silu(v) for v in values]
        for h in range(H):
            cols = []
            for b in range(3):
                terms = [
                    tap[3 * a + b] * acts[h + a - 1] for a in range(3) if 0 <= h + a - 1 < H
                ]
                cols.append(functools.reduce(jnp.add, terms))
            from_left = jnp.where(
                rows == 0, edge_l[s, h : h + 1, here], pltpu.roll(cols[0], 1, 0)
            )
            from_right = jnp.where(
                rows == WL - 1, edge_r[s, h : h + 1, here], pltpu.roll(cols[2], WL - 1, 0)
            )
            y = (values[h] + (cols[1] + from_left + from_right) + base).astype(BF16)
            out[2 * h, s, :, here] = y[:PX]
            out[2 * h + 1, s, :, here] = y[PX:]


def pair_up(first, second):
    low = lax.broadcasted_iota(jnp.int32, first.shape, 1) < 4
    return (
        jnp.where(low, first, pltpu.roll(second, 4, 1)),
        jnp.where(low, pltpu.roll(first, 4, 1), second),
    )


def attend_kernel(
    predivide, spot, recv, recv_cot, w_query, w_key, w_value, w_output, gain,
    out, halves, gain_sum,
    normed, stacked, attended, cot, y_rows, inv_rows, qkv, gatt, gnorm,
):
    rows_each = GROUPS * 8
    scale = 1.0 / math.sqrt(DH)
    for tile in range(2):
        y_two = [
            recv[:, s].astype(F32)[:, 8 * tile : 8 * tile + 8, :] for s in range(SL)
        ]
        cot_two = [
            recv_cot[:, s].astype(F32)[:, 8 * tile : 8 * tile + 8, :] for s in range(SL)
        ]
        for half, (y, c) in enumerate(zip(pair_up(*y_two), pair_up(*cot_two))):
            at = pl.ds((2 * tile + half) * rows_each, rows_each)
            y = y.reshape(rows_each, C)
            inverse = lax.rsqrt(jnp.sum(y * y, axis=-1, keepdims=True) * (1.0 / C) + EPS)
            y_rows[at, :] = y
            inv_rows[at, :] = jnp.broadcast_to(inverse, (rows_each, LANES))
            normed[at, :] = (y * inverse * gain[...]).astype(BF16)
            cot[at, :] = c.reshape(rows_each, C).astype(BF16)
    for index, weight in enumerate((w_query, w_key, w_value)):
        qkv[:, index * HD : (index + 1) * HD] = nn(normed[...], weight[...]).astype(BF16)
    gatt[...] = nn(cot[...], w_output[...]).astype(BF16)

    square = (rows_each, rows_each)
    same = (lax.broadcasted_iota(jnp.int32, square, 0) % 4) == (
        lax.broadcasted_iota(jnp.int32, square, 1) % 4
    )
    lane = lax.broadcasted_iota(jnp.int32, (rows_each, LANES), 1)

    def split(value):
        zero = jnp.zeros_like(value)
        return jnp.concatenate(
            [jnp.where(lane < DH, value, zero), jnp.where(lane >= DH, value, zero)], axis=0
        )

    for group in range(4):
        at = pl.ds(group * rows_each, rows_each)
        for pair in range(2):
            def part(index):
                return qkv[at, pl.ds(index * HD + pair * LANES, LANES)]

            lanes = pl.ds(pair * LANES, LANES)
            query, key, value = part(0), part(1), part(2)
            grad_att = gatt[at, lanes]
            key2, value2 = split(key), split(value)
            scores = nt(query, key2)
            grad_probs = nt(grad_att, value2)
            lows, grads = [], []
            for head in range(2):
                cut = slice(head * rows_each, (head + 1) * rows_each)
                score = jnp.where(same, scores[:, cut] * scale, MASKED)
                expon = jnp.exp(score - jnp.max(score, axis=-1, keepdims=True))
                probs = expon * (1.0 / jnp.sum(expon, axis=-1, keepdims=True))
                gp = grad_probs[:, cut]
                weighted = probs * gp
                total = jnp.sum(weighted, axis=-1, keepdims=True)
                lows.append(probs.astype(BF16))
                grads.append(((weighted - probs * total) * scale).astype(BF16))
            attended[at, lanes] = nn(jnp.concatenate(lows, axis=1), value2).astype(BF16)
            grad_q = nn(jnp.concatenate(grads, axis=1), key2)
            grad_k = tn(jnp.concatenate(grads, axis=0), split(query))
            grad_v = tn(jnp.concatenate(lows, axis=0), split(grad_att))
            for index, grad in enumerate((grad_q, grad_k, grad_v)):
                stacked[at, pl.ds(index * HD + pair * LANES, LANES)] = grad.astype(BF16)

    gnorm[...] = (
        nt(stacked[:, :HD], w_query[...])
        + nt(stacked[:, HD : 2 * HD], w_key[...])
        + nt(stacked[:, 2 * HD :], w_value[...])
    )
    total = jnp.zeros((8, C), F32)
    for tile in range(2):
        results = []
        for half in range(2):
            at = pl.ds((2 * tile + half) * rows_each, rows_each)
            y = y_rows[at, :]
            inverse = inv_rows[at, :][:, :1]
            grad = gnorm[at, :]
            total = total + jnp.sum((grad * y * inverse).reshape(GROUPS, 8, C), axis=0)
            gained = grad * gain[...]
            mean = jnp.sum(gained * y, axis=-1, keepdims=True) * (1.0 / C)
            result = inverse * (gained - y * (mean * inverse * inverse))
            results.append(result.reshape(GROUPS, 8, C))
        for s, whole in enumerate(pair_up(*results)):
            out[:, s, 8 * tile : 8 * tile + 8, :] = whole.astype(BF16)
    gain_sum[...] = jnp.sum(total, axis=0, keepdims=True)

    for m in range(4):
        if m < 3:
            whole = tn(normed[...], stacked[:, m * HD : (m + 1) * HD])
        else:
            whole = tn(cot[...], attended[...])
        tiles = (whole * predivide).reshape(8, 2, 2, 2, 8, HD)
        for z in range(2):
            for core in range(2):
                away_core, away_z = (core_of(spot) + core) % 2, (side_of(spot) + z) % 2
                for high in range(2):
                    for side in range(2):
                        piece = tiles[:, z, core, high, :, side * LANES : (side + 1) * LANES]
                        halves[away_core, away_z, 4 * m + 2 * high + side] = piece.reshape(
                            ROWS, LANES
                        ).astype(BF16)


def add_cores_kernel(kept, got, keep, send):
    keep[...] = (kept[0, 0].astype(F32) + got[0].astype(F32)).astype(BF16)
    send[...] = (kept[0, 1].astype(F32) + got[1].astype(F32)).astype(BF16)


def add_chips_kernel(kept, got, out):
    out[:, :ROWS, :] = (kept[...].astype(F32) + got[...].astype(F32)).astype(BF16)
    out[:, ROWS:, :] = jnp.zeros((GROUPS, 16, LANES), BF16)


def taps_kernel(
    predivide, spot, lat, other_core, other_chip, cot, ret, gain_sum, sums_in,
    out, edge_l, edge_r, tiles, packed, sem,
):
    del sums_in
    tiles[...] = jnp.zeros_like(tiles)
    for s in range(SL):
        left, right = from_partners(spot, other_core[s].astype(F32), other_chip[s].astype(F32))
        edge_l[s] = silu(left)
        edge_r[s] = silu(right)
    rows = row_index(WL)

    @pl.loop(0, PARTS)
    def _(part):
        here = lanes_of(part)
        sums = [jnp.zeros((8, LANES), F32) for _ in range(10)]
        for s in range(SL):
            grads, cols = [], []
            for h in range(H):
                back = jnp.concatenate(
                    [ret[2 * h, s, :, here].astype(F32), ret[2 * h + 1, s, :, here].astype(F32)],
                    axis=0,
                )
                grads.append(cot[s, h, :, here].astype(F32) + back)
                act = silu(lat[s, h, :, here].astype(F32))
                cols.append(
                    (
                        jnp.where(rows == 0, edge_l[s, h : h + 1, here], pltpu.roll(act, 1, 0)),
                        act,
                        jnp.where(
                            rows == WL - 1, edge_r[s, h : h + 1, here], pltpu.roll(act, WL - 1, 0)
                        ),
                    )
                )
            for h in range(H):
                for a in range(3):
                    if 0 <= h + a - 1 < H:
                        for b in range(3):
                            term = (grads[h] * cols[h + a - 1][b]).reshape(4, 8, LANES)
                            sums[3 * a + b] = sums[3 * a + b] + jnp.sum(term, axis=0)
                sums[9] = sums[9] + jnp.sum(grads[h].reshape(4, 8, LANES), axis=0)
        for r in range(10):
            tiles[4 * part + r // 3, pl.ds(r % 3, 1), :] = jnp.sum(sums[r], axis=0, keepdims=True)
        tiles[4 * part + 3, pl.ds(1, 1), :] = gain_sum[:, here]

    whole = tiles[...] * predivide
    high = whole.astype(BF16).astype(F32)
    packed[...] = jnp.concatenate([high, whole - high], axis=1).astype(BF16)
    copy = pltpu.make_async_copy(packed, out.at[:, pl.ds(ROWS, 16), :], sem)
    copy.start()
    copy.wait()


def back_edges_kernel(for_core, spot, after, cot, ret, out, edges):
    del after
    for s in range(SL):
        for h in range(H):
            at = pl.ds(h, 1)
            edges[0, 0, s, at, :] = cot[s, h, :PX, :].astype(F32)[:1]
            edges[1, 0, s, at, :] = cot[s, h, PX:, :].astype(F32)[PX - 1 :]
            edges[0, 1, s, at, :] = ret[2 * h, s].astype(F32)[:1]
            edges[1, 1, s, at, :] = ret[2 * h + 1, s].astype(F32)[PX - 1 :]
    out[...] = partner_column(spot, for_core, edges[0], edges[1]).astype(BF16)


def latents_kernel(spot, after, lat, cot, ret, other_core, other_chip, taps, out, edge_l, edge_r):
    del after
    for s in range(SL):
        left, right = from_partners(
            spot,
            other_core[0, s].astype(F32) + other_core[1, s].astype(F32),
            other_chip[0, s].astype(F32) + other_chip[1, s].astype(F32),
        )
        below, here, above = row_shifts(left)
        edge_l[s] = taps[2:3, :] * above + taps[5:6, :] * here + taps[8:9, :] * below
        below, here, above = row_shifts(right)
        edge_r[s] = taps[0:1, :] * above + taps[3:4, :] * here + taps[6:7, :] * below
    rows = row_index(WL)

    @pl.loop(0, SL * PARTS)
    def _(step):
        s = step // PARTS
        here = lanes_of(step % PARTS)
        tap = [taps[t : t + 1, here] for t in range(9)]
        grads = []
        for h in range(H):
            back = jnp.concatenate(
                [ret[2 * h, s, :, here].astype(F32), ret[2 * h + 1, s, :, here].astype(F32)],
                axis=0,
            )
            grads.append(cot[s, h, :, here].astype(F32) + back)
        for h in range(H):
            cols = []
            for b in range(3):
                terms = [
                    tap[3 * a + b] * grads[h - a + 1] for a in range(3) if 0 <= h - a + 1 < H
                ]
                cols.append(functools.reduce(jnp.add, terms))
            from_left = jnp.where(
                rows == 0, edge_l[s, h : h + 1, here], pltpu.roll(cols[2], 1, 0)
            )
            from_right = jnp.where(
                rows == WL - 1, edge_r[s, h : h + 1, here], pltpu.roll(cols[0], WL - 1, 0)
            )
            total = cols[1] + from_left + from_right
            value = lat[s, h, :, here].astype(F32)
            sig = 1.0 / (1.0 + jnp.exp(-value))
            out[s, h, :, here] = grads[h] + total * (sig * (1.0 + value * (1.0 - sig)))


def second_kernel(spot, recv, after_chip, after_core, out):
    del after_chip, after_core
    total = jnp.sum(recv[...].astype(F32), axis=0)
    weights = total[:ROWS].reshape(8, 8, LANES)
    taps = total[ROWS : ROWS + 8] + total[ROWS + 8 :]
    high = taps.astype(BF16).astype(F32)
    low = taps - high
    at = lax.broadcasted_iota(jnp.int32, (8, LANES), 0)
    both = jnp.where(at < 4, high, pltpu.roll(low, 4, 0))
    for z in range(2):
        for core in range(2):
            own = jnp.where(jnp.logical_and(core_of(spot) == core, side_of(spot) == z), 1.0, 0.0)
            for block in range(8):
                out[4 * block + 2 * z + core] = jnp.concatenate(
                    [weights[block] * own, both], axis=0
                ).astype(BF16)


def third_kernel(recv, out):
    total = jnp.sum(recv[...].astype(F32), axis=0)
    both = total[8:]
    taps = both + pltpu.roll(both, 4, 0)
    result = jnp.concatenate([total[:8], taps], axis=0)
    for s in range(GROUPS):
        out[s] = result


def unpack_kernel(recv, kernel_out, bias_out, gain_out, *outs):
    for part in range(PARTS):
        here = slice(part * LANES, (part + 1) * LANES)
        for r in range(11):
            row = recv[4 * part + r // 3, 8 + r % 3 : 9 + r % 3, :]
            if r < 9:
                kernel_out[r : r + 1, here] = row
            elif r == 9:
                bias_out[:, here] = row
            else:
                gain_out[:, here] = row
    for m in range(4):
        for high in range(2):
            for side in range(2):
                outs[m][8 * high : 8 * high + 8, side * LANES : (side + 1) * LANES] = recv[
                    4 * m + 2 * high + side, :8, :
                ]


def on_device(
    latents, cotangent, conv_kernel, conv_bias, norm_gain, w_query, w_key, w_value, w_output
):
    strips = lax.axis_size("azim")
    groups = lax.axis_size("sweep")
    cores = [(i, i ^ 1) for i in range(strips)]
    chips = [(i, (i + 1 if i % 2 else i - 1) % strips) for i in range(strips)]
    sides = [(i, i ^ 2) for i in range(strips)]
    strip = lax.axis_index("azim")
    spot = strip.astype(jnp.int32).reshape(1)
    predivide = 1.0 / math.sqrt(SL * groups * H * WL * strips)
    bias_row = conv_bias.reshape(1, C)
    gain_row = norm_gain.reshape(1, C)
    edge = pltpu.VMEM((SL, H, C), F32)

    one_edge = struct((SL, H, C), BF16)
    column = [pltpu.VMEM((2, SL, H, C), F32)]
    packed = struct((GROUPS, SL, PX, C), BF16)
    cot_sent = call(pack_kernel, packed, 16, moved=1_000_000)(cotangent)
    recv_cot = lax.all_to_all(cot_sent, "sweep", split_axis=0, concat_axis=0, tiled=True)
    to_chip = call(
        chip_edge_kernel, one_edge, 16, moved=600_000, smem=1, hbm=(1,), scratch=column
    )(spot, cot_sent, latents)
    other_chip = lax.ppermute(to_chip, "azim", chips)
    to_core, table = call(
        core_edge_kernel,
        (one_edge, struct((16, C), F32)),
        16,
        moved=600_000,
        smem=1,
        hbm=(1,),
        scratch=column,
    )(spot, to_chip, latents, conv_kernel, bias_row)
    other_core = lax.ppermute(to_core, "azim", cores)

    sent = call(
        forward_kernel,
        packed,
        16,
        flops=10_000_000,
        moved=1_000_000,
        smem=1,
        scratch=[edge, edge],
    )(spot, latents, other_core, other_chip, table)
    recv = lax.all_to_all(sent, "sweep", split_axis=0, concat_axis=0, tiled=True)

    rows = GROUPS * SL * PX
    grad_attn, halves, gain_sum = call(
        functools.partial(attend_kernel, predivide),
        (
            struct((GROUPS, SL, PX, C), BF16),
            struct((2, 2, GROUPS, ROWS, LANES), BF16),
            struct((1, C), F32),
        ),
        32,
        flops=2_000_000_000,
        moved=6_000_000,
        smem=1,
        scratch=[
            pltpu.VMEM((rows, C), BF16),
            pltpu.VMEM((rows, 3 * HD), BF16),
            pltpu.VMEM((rows, HD), BF16),
            pltpu.VMEM((rows, C), BF16),
            pltpu.VMEM((rows, C), F32),
            pltpu.VMEM((rows, LANES), F32),
            pltpu.VMEM((rows, 3 * HD), BF16),
            pltpu.VMEM((rows, HD), BF16),
            pltpu.VMEM((rows, C), F32),
        ],
    )(spot, recv, recv_cot, w_query, w_key, w_value, w_output, gain_row)
    ret = lax.all_to_all(grad_attn, "sweep", split_axis=0, concat_axis=0, tiled=True)
    from_core = lax.ppermute(halves[1], "azim", cores)
    piece = struct((GROUPS, ROWS, LANES), BF16)
    keep, send = call(add_cores_kernel, (piece, piece), 16, moved=2_000_000)(halves, from_core)
    from_chip = lax.ppermute(send, "azim", sides)
    payload = struct((GROUPS, ROWS + 16, LANES), BF16)
    sums = call(add_chips_kernel, payload, 16, moved=1_000_000)(keep, from_chip)

    vmem = pl.BlockSpec(memory_space=pltpu.VMEM)
    anywhere = pl.BlockSpec(memory_space=pltpu.HBM)
    first_sent = pl.pallas_call(
        functools.partial(taps_kernel, predivide),
        out_shape=payload,
        in_specs=[pl.BlockSpec(memory_space=pltpu.SMEM)] + [vmem] * 6 + [anywhere],
        out_specs=anywhere,
        input_output_aliases={7: 0},
        scratch_shapes=[
            edge,
            edge,
            pltpu.VMEM((GROUPS, 8, LANES), F32),
            pltpu.VMEM((GROUPS, 16, LANES), BF16),
            pltpu.SemaphoreType.DMA,
        ],
        compiler_params=params(16),
        cost_estimate=pl.CostEstimate(
            flops=10_000_000, bytes_accessed=2_000_000, transcendentals=0
        ),
    )(spot, latents, other_core, other_chip, cotangent, ret, gain_sum, sums)
    first_recv = lax.all_to_all(first_sent, "sweep", split_axis=0, concat_axis=0, tiled=True)
    both_edges = struct((2, SL, H, C), BF16)

    def back_edges(for_core, after):
        return call(
            functools.partial(back_edges_kernel, for_core),
            both_edges,
            16,
            moved=100_000,
            smem=1,
            hbm=(1,),
            scratch=[pltpu.VMEM((2, 2, SL, H, C), F32)],
        )(spot, after, cotangent, ret)

    to_chip = back_edges(False, first_sent)
    back_chip = lax.ppermute(to_chip, "azim", chips)
    to_core = back_edges(True, to_chip)
    back_core = lax.ppermute(to_core, "azim", cores)

    second_sent = call(
        second_kernel, struct((strips, 16, LANES), BF16), 16, moved=1_000_000, smem=1, hbm=(2, 3)
    )(spot, first_recv, back_chip, back_core)
    second_recv = lax.all_to_all(second_sent, "azim", split_axis=0, concat_axis=0, tiled=True)

    grad_latents = call(
        latents_kernel,
        struct((SL, H, WL, C), F32),
        16,
        flops=10_000_000,
        moved=4_000_000,
        smem=1,
        hbm=(1,),
        scratch=[edge, edge],
    )(spot, second_sent, latents, cotangent, ret, back_core, back_chip, table)
    second_recv, grad_latents = lax.optimization_barrier((second_recv, grad_latents))

    third_sent = call(third_kernel, struct((GROUPS, 16, LANES), F32), 16, moved=300_000)(
        second_recv
    )
    third_recv = lax.all_to_all(third_sent, "sweep", split_axis=0, concat_axis=0, tiled=True)

    share = struct((C // strips, HD), F32)
    line = struct((1, C), F32)
    grad_kernel, grad_bias, grad_gain, *shares = call(
        unpack_kernel,
        (struct((9, C), F32), line, line, share, share, share, share),
        16,
        moved=300_000,
    )(third_recv)
    return (
        grad_latents,
        grad_kernel,
        grad_bias.reshape(C),
        grad_gain.reshape(C),
        shares[0],
        shares[1],
        shares[2],
        shares[3],
    )


def solution(mesh):
    image = P("sweep", None, "azim", None)
    share = P("azim", None)
    return jax.shard_map(
        on_device,
        mesh=mesh,
        in_specs=(image, image, P(), P(), P(), P(), P(), P(), P()),
        out_specs=(image, P(), P(), P(), share, share, share, share),
        check_vma=False,
    )
```

```python
import functools
import math

import jax
import jax.numpy as jnp
from jax import lax
from jax.experimental import pallas as pl
from jax.experimental.pallas import tpu as pltpu
from jax.sharding import PartitionSpec as P

DH = 64
EPS = 1e-06
F32 = jnp.float32
BF16 = jnp.bfloat16
MASKED = -1e30

SL, H, WL, C = 2, 8, 32, 512
GROUPS = 16
PX = 16
HD = 256
LANES = 128
PARTS = C // LANES
ROWS = 64


def params(mib):
    return pltpu.CompilerParams(vmem_limit_bytes=mib * 1024 * 1024)


def call(kernel, outs, mib, flops=0, moved=0, scratch=(), smem=0, hbm=()):
    vmem = pl.BlockSpec(memory_space=pltpu.VMEM)

    def run(*args):
        specs = [pl.BlockSpec(memory_space=pltpu.SMEM)] * smem + [vmem] * (len(args) - smem)
        for at in hbm:
            specs[at] = pl.BlockSpec(memory_space=pltpu.HBM)
        return pl.pallas_call(
            kernel,
            out_shape=outs,
            in_specs=specs,
            out_specs=jax.tree.map(lambda _: vmem, outs),
            scratch_shapes=list(scratch),
            compiler_params=params(mib),
            cost_estimate=pl.CostEstimate(
                flops=flops, bytes_accessed=moved, transcendentals=0
            ),
        )(*args)

    return run


def struct(shape, dtype):
    return jax.ShapeDtypeStruct(shape, dtype)


def silu(value):
    return value / (1.0 + jnp.exp(-value))


def nt(left, right):
    return lax.dot_general(left, right, (((1,), (1,)), ((), ())), preferred_element_type=F32)


def tn(left, right):
    return lax.dot_general(left, right, (((0,), (0,)), ((), ())), preferred_element_type=F32)


def nn(left, right):
    return lax.dot_general(left, right, (((1,), (0,)), ((), ())), preferred_element_type=F32)


def lanes_of(part):
    return pl.ds(pl.multiple_of(part * LANES, LANES), LANES)


def row_index(rows):
    return lax.broadcasted_iota(jnp.int32, (rows, LANES), 0)


def row_shifts(value):
    at = lax.broadcasted_iota(jnp.int32, value.shape, 0)
    below = jnp.where(at == 0, 0.0, pltpu.roll(value, 1, 0))
    above = jnp.where(at == H - 1, 0.0, pltpu.roll(value, H - 1, 0))
    return below, value, above


def core_of(spot):
    return spot[0] % 2


def side_of(spot):
    return (spot[0] // 2) % 2


def partner_column(spot, for_core, first, last):
    even = core_of(spot) == 0
    return jnp.where(even, last, first) if for_core else jnp.where(even, first, last)


def from_partners(spot, other_core, other_chip):
    even = core_of(spot) == 0
    return jnp.where(even, other_chip, other_core), jnp.where(even, other_core, other_chip)


def edge_columns(lat, edges):
    for s in range(SL):
        for h in range(H):
            edges[0, s, h : h + 1, :] = lat[s, h, :PX, :].astype(F32)[:1]
            edges[1, s, h : h + 1, :] = lat[s, h, PX:, :].astype(F32)[PX - 1 :]


def pack_kernel(cot, out):
    for s in range(SL):
        for h in range(H):
            out[2 * h, s] = cot[s, h, :PX, :]
            out[2 * h + 1, s] = cot[s, h, PX:, :]


def chip_edge_kernel(spot, after, lat, out, edges):
    del after
    edge_columns(lat, edges)
    out[...] = partner_column(spot, False, edges[0], edges[1]).astype(BF16)


def core_edge_kernel(spot, after, lat, taps, bias, out, table, edges):
    del after
    edge_columns(lat, edges)
    out[...] = partner_column(spot, True, edges[0], edges[1]).astype(BF16)
    table[:9, :] = taps[...]
    table[9:10, :] = bias[...]
    table[10:, :] = jnp.zeros((6, C), F32)


def forward_kernel(spot, lat, other_core, other_chip, taps, out, edge_l, edge_r):
    for s in range(SL):
        left, right = from_partners(spot, other_core[s].astype(F32), other_chip[s].astype(F32))
        shifted = row_shifts(silu(left))
        edge_l[s] = sum(taps[3 * a : 3 * a + 1, :] * shifted[a] for a in range(3))
        shifted = row_shifts(silu(right))
        edge_r[s] = sum(taps[3 * a + 2 : 3 * a + 3, :] * shifted[a] for a in range(3))
    rows = row_index(WL)

    @pl.loop(0, SL * PARTS)
    def _(step):
        s = step // PARTS
        here = lanes_of(step % PARTS)
        tap = [taps[t : t + 1, here] for t in range(9)]
        base = taps[9:10, here]
        values = [lat[s, h, :, here].astype(F32) for h in range(H)]
        acts = [silu(v) for v in values]
        for h in range(H):
            cols = []
            for b in range(3):
                terms = [
                    tap[3 * a + b] * acts[h + a - 1] for a in range(3) if 0 <= h + a - 1 < H
                ]
                cols.append(functools.reduce(jnp.add, terms))
            from_left = jnp.where(
                rows == 0, edge_l[s, h : h + 1, here], pltpu.roll(cols[0], 1, 0)
            )
            from_right = jnp.where(
                rows == WL - 1, edge_r[s, h : h + 1, here], pltpu.roll(cols[2], WL - 1, 0)
            )
            y = (values[h] + (cols[1] + from_left + from_right) + base).astype(BF16)
            out[2 * h, s, :, here] = y[:PX]
            out[2 * h + 1, s, :, here] = y[PX:]


def pair_up(first, second):
    low = lax.broadcasted_iota(jnp.int32, first.shape, 1) < 4
    return (
        jnp.where(low, first, pltpu.roll(second, 4, 1)),
        jnp.where(low, pltpu.roll(first, 4, 1), second),
    )


def attend_kernel(
    predivide, spot, recv, recv_cot, w_query, w_key, w_value, w_output, gain,
    out, halves, gain_sum,
    normed, stacked, attended, cot, y_rows, inv_rows, qkv, gatt, gnorm,
):
    rows_each = GROUPS * 8
    scale = 1.0 / math.sqrt(DH)
    for tile in range(2):
        y_two = [
            recv[:, s].astype(F32)[:, 8 * tile : 8 * tile + 8, :] for s in range(SL)
        ]
        cot_two = [
            recv_cot[:, s].astype(F32)[:, 8 * tile : 8 * tile + 8, :] for s in range(SL)
        ]
        for half, (y, c) in enumerate(zip(pair_up(*y_two), pair_up(*cot_two))):
            at = pl.ds((2 * tile + half) * rows_each, rows_each)
            y = y.reshape(rows_each, C)
            inverse = lax.rsqrt(jnp.sum(y * y, axis=-1, keepdims=True) * (1.0 / C) + EPS)
            y_rows[at, :] = y
            inv_rows[at, :] = jnp.broadcast_to(inverse, (rows_each, LANES))
            normed[at, :] = (y * inverse * gain[...]).astype(BF16)
            cot[at, :] = c.reshape(rows_each, C).astype(BF16)
    for index, weight in enumerate((w_query, w_key, w_value)):
        qkv[:, index * HD : (index + 1) * HD] = nn(normed[...], weight[...]).astype(BF16)
    gatt[...] = nn(cot[...], w_output[...]).astype(BF16)

    square = (rows_each, rows_each)
    same = (lax.broadcasted_iota(jnp.int32, square, 0) % 4) == (
        lax.broadcasted_iota(jnp.int32, square, 1) % 4
    )
    lane = lax.broadcasted_iota(jnp.int32, (rows_each, LANES), 1)

    def split(value):
        zero = jnp.zeros_like(value)
        return jnp.concatenate(
            [jnp.where(lane < DH, value, zero), jnp.where(lane >= DH, value, zero)], axis=0
        )

    units = [
        (pl.ds(group * rows_each, rows_each), pair * LANES)
        for group in range(4)
        for pair in range(2)
    ]

    def part(unit, index):
        return qkv[unit[0], pl.ds(index * HD + unit[1], LANES)]

    scores = [nt(split(part(unit, 1)), part(unit, 0)) for unit in units]
    grad_probs = [
        nt(split(part(unit, 2)), gatt[unit[0], pl.ds(unit[1], LANES)]) for unit in units
    ]
    results = []
    for score2, grad2 in zip(scores, grad_probs):
        lows, grads = [], []
        for head in range(2):
            cut = slice(head * rows_each, (head + 1) * rows_each)
            score = jnp.where(same, score2[cut] * scale, MASKED)
            expon = jnp.exp(score - jnp.max(score, axis=0, keepdims=True))
            probs = expon * (1.0 / jnp.sum(expon, axis=0, keepdims=True))
            weighted = probs * grad2[cut]
            total = jnp.sum(weighted, axis=0, keepdims=True)
            lows.append(probs.astype(BF16))
            grads.append(((weighted - probs * total) * scale).astype(BF16))
        results.append((lows, grads))
    for unit, (lows, grads) in zip(units, results):
        at, lanes = unit[0], pl.ds(unit[1], LANES)
        attended[at, lanes] = tn(jnp.concatenate(lows, axis=0), split(part(unit, 2))).astype(BF16)
        grad_q = tn(jnp.concatenate(grads, axis=0), split(part(unit, 1)))
        grad_k = nn(jnp.concatenate(grads, axis=1), split(part(unit, 0)))
        grad_v = nn(jnp.concatenate(lows, axis=1), split(gatt[at, lanes]))
        for index, grad in enumerate((grad_q, grad_k, grad_v)):
            stacked[at, pl.ds(index * HD + unit[1], LANES)] = grad.astype(BF16)

    gnorm[...] = (
        nt(stacked[:, :HD], w_query[...])
        + nt(stacked[:, HD : 2 * HD], w_key[...])
        + nt(stacked[:, 2 * HD :], w_value[...])
    )
    total = jnp.zeros((8, C), F32)
    for tile in range(2):
        results = []
        for half in range(2):
            at = pl.ds((2 * tile + half) * rows_each, rows_each)
            y = y_rows[at, :]
            inverse = inv_rows[at, :][:, :1]
            grad = gnorm[at, :]
            total = total + jnp.sum((grad * y * inverse).reshape(GROUPS, 8, C), axis=0)
            gained = grad * gain[...]
            mean = jnp.sum(gained * y, axis=-1, keepdims=True) * (1.0 / C)
            result = inverse * (gained - y * (mean * inverse * inverse))
            results.append(result.reshape(GROUPS, 8, C))
        for s, whole in enumerate(pair_up(*results)):
            out[:, s, 8 * tile : 8 * tile + 8, :] = whole.astype(BF16)
    gain_sum[...] = jnp.sum(total, axis=0, keepdims=True)

    for m in range(4):
        if m < 3:
            whole = tn(normed[...], stacked[:, m * HD : (m + 1) * HD])
        else:
            whole = tn(cot[...], attended[...])
        tiles = (whole * predivide).reshape(8, 2, 2, 2, 8, HD)
        for z in range(2):
            for core in range(2):
                away_core, away_z = (core_of(spot) + core) % 2, (side_of(spot) + z) % 2
                for high in range(2):
                    for side in range(2):
                        piece = tiles[:, z, core, high, :, side * LANES : (side + 1) * LANES]
                        halves[away_core, away_z, 4 * m + 2 * high + side] = piece.reshape(
                            ROWS, LANES
                        ).astype(BF16)


def add_cores_kernel(kept, got, keep, send):
    keep[...] = (kept[0, 0].astype(F32) + got[0].astype(F32)).astype(BF16)
    send[...] = (kept[0, 1].astype(F32) + got[1].astype(F32)).astype(BF16)


def add_chips_kernel(kept, got, out):
    out[:, :ROWS, :] = (kept[...].astype(F32) + got[...].astype(F32)).astype(BF16)
    out[:, ROWS:, :] = jnp.zeros((GROUPS, 16, LANES), BF16)


def taps_kernel(
    predivide, spot, lat, other_core, other_chip, cot, ret, gain_sum, sums_in,
    out, edge_l, edge_r, tiles, packed, sem,
):
    del sums_in
    tiles[...] = jnp.zeros_like(tiles)
    for s in range(SL):
        left, right = from_partners(spot, other_core[s].astype(F32), other_chip[s].astype(F32))
        edge_l[s] = silu(left)
        edge_r[s] = silu(right)
    rows = row_index(WL)

    @pl.loop(0, PARTS)
    def _(part):
        here = lanes_of(part)
        sums = [jnp.zeros((8, LANES), F32) for _ in range(10)]
        for s in range(SL):
            grads, cols = [], []
            for h in range(H):
                back = jnp.concatenate(
                    [ret[2 * h, s, :, here].astype(F32), ret[2 * h + 1, s, :, here].astype(F32)],
                    axis=0,
                )
                grads.append(cot[s, h, :, here].astype(F32) + back)
                act = silu(lat[s, h, :, here].astype(F32))
                cols.append(
                    (
                        jnp.where(rows == 0, edge_l[s, h : h + 1, here], pltpu.roll(act, 1, 0)),
                        act,
                        jnp.where(
                            rows == WL - 1, edge_r[s, h : h + 1, here], pltpu.roll(act, WL - 1, 0)
                        ),
                    )
                )
            for h in range(H):
                for a in range(3):
                    if 0 <= h + a - 1 < H:
                        for b in range(3):
                            term = (grads[h] * cols[h + a - 1][b]).reshape(4, 8, LANES)
                            sums[3 * a + b] = sums[3 * a + b] + jnp.sum(term, axis=0)
                sums[9] = sums[9] + jnp.sum(grads[h].reshape(4, 8, LANES), axis=0)
        for r in range(10):
            tiles[4 * part + r // 3, pl.ds(r % 3, 1), :] = jnp.sum(sums[r], axis=0, keepdims=True)
        tiles[4 * part + 3, pl.ds(1, 1), :] = gain_sum[:, here]

    whole = tiles[...] * predivide
    high = whole.astype(BF16).astype(F32)
    packed[...] = jnp.concatenate([high, whole - high], axis=1).astype(BF16)
    copy = pltpu.make_async_copy(packed, out.at[:, pl.ds(ROWS, 16), :], sem)
    copy.start()
    copy.wait()


def back_edges_kernel(for_core, spot, after, cot, ret, out, edges):
    del after
    for s in range(SL):
        for h in range(H):
            at = pl.ds(h, 1)
            edges[0, 0, s, at, :] = cot[s, h, :PX, :].astype(F32)[:1]
            edges[1, 0, s, at, :] = cot[s, h, PX:, :].astype(F32)[PX - 1 :]
            edges[0, 1, s, at, :] = ret[2 * h, s].astype(F32)[:1]
            edges[1, 1, s, at, :] = ret[2 * h + 1, s].astype(F32)[PX - 1 :]
    out[...] = partner_column(spot, for_core, edges[0], edges[1]).astype(BF16)


def latents_kernel(spot, after, lat, cot, ret, other_core, other_chip, taps, out, edge_l, edge_r):
    del after
    for s in range(SL):
        left, right = from_partners(
            spot,
            other_core[0, s].astype(F32) + other_core[1, s].astype(F32),
            other_chip[0, s].astype(F32) + other_chip[1, s].astype(F32),
        )
        below, here, above = row_shifts(left)
        edge_l[s] = taps[2:3, :] * above + taps[5:6, :] * here + taps[8:9, :] * below
        below, here, above = row_shifts(right)
        edge_r[s] = taps[0:1, :] * above + taps[3:4, :] * here + taps[6:7, :] * below
    rows = row_index(WL)

    @pl.loop(0, SL * PARTS)
    def _(step):
        s = step // PARTS
        here = lanes_of(step % PARTS)
        tap = [taps[t : t + 1, here] for t in range(9)]
        grads = []
        for h in range(H):
            back = jnp.concatenate(
                [ret[2 * h, s, :, here].astype(F32), ret[2 * h + 1, s, :, here].astype(F32)],
                axis=0,
            )
            grads.append(cot[s, h, :, here].astype(F32) + back)
        for h in range(H):
            cols = []
            for b in range(3):
                terms = [
                    tap[3 * a + b] * grads[h - a + 1] for a in range(3) if 0 <= h - a + 1 < H
                ]
                cols.append(functools.reduce(jnp.add, terms))
            from_left = jnp.where(
                rows == 0, edge_l[s, h : h + 1, here], pltpu.roll(cols[2], 1, 0)
            )
            from_right = jnp.where(
                rows == WL - 1, edge_r[s, h : h + 1, here], pltpu.roll(cols[0], WL - 1, 0)
            )
            total = cols[1] + from_left + from_right
            value = lat[s, h, :, here].astype(F32)
            sig = 1.0 / (1.0 + jnp.exp(-value))
            out[s, h, :, here] = grads[h] + total * (sig * (1.0 + value * (1.0 - sig)))


def high_low(value):
    high = value.astype(BF16).astype(F32)
    at = lax.broadcasted_iota(jnp.int32, value.shape, 0)
    return jnp.where(at < 4, high, pltpu.roll(value - high, 4, 0))


def second_kernel(spot, recv, out):
    total = jnp.sum(recv[...].astype(F32), axis=0)
    weights = total[:ROWS].reshape(8, 8, LANES)
    taps = total[ROWS : ROWS + 8] + total[ROWS + 8 :]
    both = high_low(taps)
    for z in range(2):
        for core in range(2):
            own = jnp.where(jnp.logical_and(core_of(spot) == core, side_of(spot) == z), 1.0, 0.0)
            for block in range(8):
                out[4 * block + 2 * z + core] = jnp.concatenate(
                    [weights[block] * own, both], axis=0
                ).astype(BF16)


def third_kernel(recv, out):
    total = jnp.sum(recv[...].astype(F32), axis=0)
    both = total[8:]
    result = jnp.concatenate([total[:8], high_low(both + pltpu.roll(both, 4, 0))], axis=0)
    result = result.astype(BF16)
    for s in range(GROUPS):
        out[s] = result


def unpack_kernel(recv, kernel_out, bias_out, gain_out, *outs):
    for part in range(PARTS):
        here = slice(part * LANES, (part + 1) * LANES)
        for group in range(4):
            both = recv[4 * part + group].astype(F32)[8:]
            taps = both + pltpu.roll(both, 4, 0)
            if group < 3:
                kernel_out[3 * group : 3 * group + 3, here] = taps[:3]
            else:
                bias_out[:, here] = taps[:1]
                gain_out[:, here] = taps[1:2]
    for m in range(4):
        for high in range(2):
            for side in range(2):
                piece = recv[4 * m + 2 * high + side].astype(F32)[:8]
                outs[m][8 * high : 8 * high + 8, side * LANES : (side + 1) * LANES] = piece


def on_device(
    latents, cotangent, conv_kernel, conv_bias, norm_gain, w_query, w_key, w_value, w_output
):
    strips = lax.axis_size("azim")
    groups = lax.axis_size("sweep")
    cores = [(i, i ^ 1) for i in range(strips)]
    chips = [(i, (i + 1 if i % 2 else i - 1) % strips) for i in range(strips)]
    sides = [(i, i ^ 2) for i in range(strips)]
    strip = lax.axis_index("azim")
    spot = strip.astype(jnp.int32).reshape(1)
    predivide = 1.0 / math.sqrt(SL * groups * H * WL * strips)
    bias_row = conv_bias.reshape(1, C)
    gain_row = norm_gain.reshape(1, C)
    edge = pltpu.VMEM((SL, H, C), F32)

    one_edge = struct((SL, H, C), BF16)
    column = [pltpu.VMEM((2, SL, H, C), F32)]
    packed = struct((GROUPS, SL, PX, C), BF16)
    cot_sent = call(pack_kernel, packed, 16, moved=1_000_000)(cotangent)
    recv_cot = lax.all_to_all(cot_sent, "sweep", split_axis=0, concat_axis=0, tiled=True)
    to_chip = call(
        chip_edge_kernel, one_edge, 16, moved=600_000, smem=1, hbm=(1,), scratch=column
    )(spot, cot_sent, latents)
    other_chip = lax.ppermute(to_chip, "azim", chips)
    to_core, table = call(
        core_edge_kernel,
        (one_edge, struct((16, C), F32)),
        16,
        moved=600_000,
        smem=1,
        hbm=(1,),
        scratch=column,
    )(spot, to_chip, latents, conv_kernel, bias_row)
    other_core = lax.ppermute(to_core, "azim", cores)

    sent = call(
        forward_kernel,
        packed,
        16,
        flops=10_000_000,
        moved=1_000_000,
        smem=1,
        scratch=[edge, edge],
    )(spot, latents, other_core, other_chip, table)
    recv = lax.all_to_all(sent, "sweep", split_axis=0, concat_axis=0, tiled=True)

    rows = GROUPS * SL * PX
    grad_attn, halves, gain_sum = call(
        functools.partial(attend_kernel, predivide),
        (
            struct((GROUPS, SL, PX, C), BF16),
            struct((2, 2, GROUPS, ROWS, LANES), BF16),
            struct((1, C), F32),
        ),
        32,
        flops=2_000_000_000,
        moved=6_000_000,
        smem=1,
        scratch=[
            pltpu.VMEM((rows, C), BF16),
            pltpu.VMEM((rows, 3 * HD), BF16),
            pltpu.VMEM((rows, HD), BF16),
            pltpu.VMEM((rows, C), BF16),
            pltpu.VMEM((rows, C), F32),
            pltpu.VMEM((rows, LANES), F32),
            pltpu.VMEM((rows, 3 * HD), BF16),
            pltpu.VMEM((rows, HD), BF16),
            pltpu.VMEM((rows, C), F32),
        ],
    )(spot, recv, recv_cot, w_query, w_key, w_value, w_output, gain_row)
    ret = lax.all_to_all(grad_attn, "sweep", split_axis=0, concat_axis=0, tiled=True)
    from_core = lax.ppermute(halves[1], "azim", cores)
    piece = struct((GROUPS, ROWS, LANES), BF16)
    keep, send = call(add_cores_kernel, (piece, piece), 16, moved=2_000_000)(halves, from_core)
    from_chip = lax.ppermute(send, "azim", sides)
    payload = struct((GROUPS, ROWS + 16, LANES), BF16)
    sums = call(add_chips_kernel, payload, 16, moved=1_000_000)(keep, from_chip)

    vmem = pl.BlockSpec(memory_space=pltpu.VMEM)
    anywhere = pl.BlockSpec(memory_space=pltpu.HBM)
    first_sent = pl.pallas_call(
        functools.partial(taps_kernel, predivide),
        out_shape=payload,
        in_specs=[pl.BlockSpec(memory_space=pltpu.SMEM)] + [vmem] * 6 + [anywhere],
        out_specs=anywhere,
        input_output_aliases={7: 0},
        scratch_shapes=[
            edge,
            edge,
            pltpu.VMEM((GROUPS, 8, LANES), F32),
            pltpu.VMEM((GROUPS, 16, LANES), BF16),
            pltpu.SemaphoreType.DMA,
        ],
        compiler_params=params(16),
        cost_estimate=pl.CostEstimate(
            flops=10_000_000, bytes_accessed=2_000_000, transcendentals=0
        ),
    )(spot, latents, other_core, other_chip, cotangent, ret, gain_sum, sums)
    first_recv = lax.all_to_all(first_sent, "sweep", split_axis=0, concat_axis=0, tiled=True)
    second_sent = call(
        second_kernel, struct((strips, 16, LANES), BF16), 16, moved=1_000_000, smem=1
    )(spot, first_recv)
    second_recv = lax.all_to_all(second_sent, "azim", split_axis=0, concat_axis=0, tiled=True)

    both_edges = struct((2, SL, H, C), BF16)

    def back_edges(for_core, after):
        return call(
            functools.partial(back_edges_kernel, for_core),
            both_edges,
            16,
            moved=100_000,
            smem=1,
            hbm=(1,),
            scratch=[pltpu.VMEM((2, 2, SL, H, C), F32)],
        )(spot, after, cotangent, ret)

    to_chip = back_edges(False, second_sent)
    back_chip = lax.ppermute(to_chip, "azim", chips)
    to_core = back_edges(True, to_chip)
    back_core = lax.ppermute(to_core, "azim", cores)

    grad_latents = call(
        latents_kernel,
        struct((SL, H, WL, C), F32),
        16,
        flops=10_000_000,
        moved=4_000_000,
        smem=1,
        hbm=(1,),
        scratch=[edge, edge],
    )(spot, second_sent, latents, cotangent, ret, back_core, back_chip, table)
    second_recv, grad_latents = lax.optimization_barrier((second_recv, grad_latents))

    third_sent = call(third_kernel, struct((GROUPS, 16, LANES), BF16), 16, moved=300_000)(
        second_recv
    )
    third_recv = lax.all_to_all(third_sent, "sweep", split_axis=0, concat_axis=0, tiled=True)

    share = struct((C // strips, HD), F32)
    line = struct((1, C), F32)
    grad_kernel, grad_bias, grad_gain, *shares = call(
        unpack_kernel,
        (struct((9, C), F32), line, line, share, share, share, share),
        16,
        moved=300_000,
    )(third_recv)
    return (
        grad_latents,
        grad_kernel,
        grad_bias.reshape(C),
        grad_gain.reshape(C),
        shares[0],
        shares[1],
        shares[2],
        shares[3],
    )


def solution(mesh):
    image = P("sweep", None, "azim", None)
    share = P("azim", None)
    return jax.shard_map(
        on_device,
        mesh=mesh,
        in_specs=(image, image, P(), P(), P(), P(), P(), P(), P()),
        out_specs=(image, P(), P(), P(), share, share, share, share),
        check_vma=False,
    )
```

```python
import functools
import math

import jax
import jax.numpy as jnp
from jax import lax
from jax.experimental import pallas as pl
from jax.experimental.pallas import tpu as pltpu
from jax.sharding import PartitionSpec as P

DH = 64
EPS = 1e-06
F32 = jnp.float32
BF16 = jnp.bfloat16
MASKED = -1e30

SL, H, WL, C = 2, 8, 32, 512
GROUPS = 16
PX = 16
HD = 256
LANES = 128
PARTS = C // LANES
ROWS = 64


def params(mib):
    return pltpu.CompilerParams(vmem_limit_bytes=mib * 1024 * 1024)


def call(kernel, outs, mib, flops=0, moved=0, scratch=(), smem=0, hbm=()):
    vmem = pl.BlockSpec(memory_space=pltpu.VMEM)

    def run(*args):
        specs = [pl.BlockSpec(memory_space=pltpu.SMEM)] * smem + [vmem] * (len(args) - smem)
        for at in hbm:
            specs[at] = pl.BlockSpec(memory_space=pltpu.HBM)
        return pl.pallas_call(
            kernel,
            out_shape=outs,
            in_specs=specs,
            out_specs=jax.tree.map(lambda _: vmem, outs),
            scratch_shapes=list(scratch),
            compiler_params=params(mib),
            cost_estimate=pl.CostEstimate(
                flops=flops, bytes_accessed=moved, transcendentals=0
            ),
        )(*args)

    return run


def struct(shape, dtype):
    return jax.ShapeDtypeStruct(shape, dtype)


def silu(value):
    return value / (1.0 + jnp.exp(-value))


def nt(left, right):
    return lax.dot_general(left, right, (((1,), (1,)), ((), ())), preferred_element_type=F32)


def tn(left, right):
    return lax.dot_general(left, right, (((0,), (0,)), ((), ())), preferred_element_type=F32)


def nn(left, right):
    return lax.dot_general(left, right, (((1,), (0,)), ((), ())), preferred_element_type=F32)


def lanes_of(part):
    return pl.ds(pl.multiple_of(part * LANES, LANES), LANES)


def row_index(rows):
    return lax.broadcasted_iota(jnp.int32, (rows, LANES), 0)


def row_shifts(value):
    at = lax.broadcasted_iota(jnp.int32, value.shape, 0)
    below = jnp.where(at == 0, 0.0, pltpu.roll(value, 1, 0))
    above = jnp.where(at == H - 1, 0.0, pltpu.roll(value, H - 1, 0))
    return below, value, above


def core_of(spot):
    return spot[0] % 2


def side_of(spot):
    return (spot[0] // 2) % 2


def partner_column(spot, for_core, first, last):
    even = core_of(spot) == 0
    return jnp.where(even, last, first) if for_core else jnp.where(even, first, last)


def from_partners(spot, other_core, other_chip):
    even = core_of(spot) == 0
    return jnp.where(even, other_chip, other_core), jnp.where(even, other_core, other_chip)


def edge_columns(lat, edges):
    for s in range(SL):
        for h in range(H):
            edges[0, s, h : h + 1, :] = lat[s, h, :PX, :].astype(F32)[:1]
            edges[1, s, h : h + 1, :] = lat[s, h, PX:, :].astype(F32)[PX - 1 :]


def pack_kernel(cot, out, token, sems):
    token[...] = jnp.zeros_like(token)
    copies = []
    for s in range(SL):
        for g in range(GROUPS):
            copies.append(
                pltpu.make_async_copy(
                    cot.at[s, g // 2, pl.ds(PX * (g % 2), PX), :],
                    out.at[g, s],
                    sems.at[s * GROUPS + g],
                )
            )
    for copy in copies:
        copy.start()
    for copy in copies:
        copy.wait()


def chip_edge_kernel(spot, after, lat, out, edges):
    del after
    edge_columns(lat, edges)
    out[...] = partner_column(spot, False, edges[0], edges[1]).astype(BF16)


def core_edge_kernel(spot, after, lat, taps, bias, out, table, edges):
    del after
    edge_columns(lat, edges)
    out[...] = partner_column(spot, True, edges[0], edges[1]).astype(BF16)
    table[:9, :] = taps[...]
    table[9:10, :] = bias[...]
    table[10:, :] = jnp.zeros((6, C), F32)


def forward_kernel(spot, lat, other_core, other_chip, taps, out, edge_l, edge_r):
    for s in range(SL):
        left, right = from_partners(spot, other_core[s].astype(F32), other_chip[s].astype(F32))
        shifted = row_shifts(silu(left))
        edge_l[s] = sum(taps[3 * a : 3 * a + 1, :] * shifted[a] for a in range(3))
        shifted = row_shifts(silu(right))
        edge_r[s] = sum(taps[3 * a + 2 : 3 * a + 3, :] * shifted[a] for a in range(3))
    rows = row_index(WL)

    @pl.loop(0, SL * PARTS)
    def _(step):
        s = step // PARTS
        here = lanes_of(step % PARTS)
        tap = [taps[t : t + 1, here] for t in range(9)]
        base = taps[9:10, here]
        values = [lat[s, h, :, here].astype(F32) for h in range(H)]
        acts = [silu(v) for v in values]
        for h in range(H):
            cols = []
            for b in range(3):
                terms = [
                    tap[3 * a + b] * acts[h + a - 1] for a in range(3) if 0 <= h + a - 1 < H
                ]
                cols.append(functools.reduce(jnp.add, terms))
            from_left = jnp.where(
                rows == 0, edge_l[s, h : h + 1, here], pltpu.roll(cols[0], 1, 0)
            )
            from_right = jnp.where(
                rows == WL - 1, edge_r[s, h : h + 1, here], pltpu.roll(cols[2], WL - 1, 0)
            )
            y = (values[h] + (cols[1] + from_left + from_right) + base).astype(BF16)
            out[2 * h, s, :, here] = y[:PX]
            out[2 * h + 1, s, :, here] = y[PX:]


def pair_up(first, second):
    low = lax.broadcasted_iota(jnp.int32, first.shape, 1) < 4
    return (
        jnp.where(low, first, pltpu.roll(second, 4, 1)),
        jnp.where(low, pltpu.roll(first, 4, 1), second),
    )


def attend_kernel(
    predivide, spot, recv, recv_cot, w_query, w_key, w_value, w_output, gain,
    out, halves, gain_sum,
    normed, stacked, attended, cot, y_rows, inv_rows, qkv, gatt, gnorm,
):
    rows_each = GROUPS * 8
    scale = 1.0 / math.sqrt(DH)
    for tile in range(2):
        y_two = [
            recv[:, s].astype(F32)[:, 8 * tile : 8 * tile + 8, :] for s in range(SL)
        ]
        cot_two = [
            recv_cot[:, s].astype(F32)[:, 8 * tile : 8 * tile + 8, :] for s in range(SL)
        ]
        for half, (y, c) in enumerate(zip(pair_up(*y_two), pair_up(*cot_two))):
            at = pl.ds((2 * tile + half) * rows_each, rows_each)
            y = y.reshape(rows_each, C)
            inverse = lax.rsqrt(jnp.sum(y * y, axis=-1, keepdims=True) * (1.0 / C) + EPS)
            y_rows[at, :] = y
            inv_rows[at, :] = jnp.broadcast_to(inverse, (rows_each, LANES))
            normed[at, :] = (y * inverse * gain[...]).astype(BF16)
            cot[at, :] = c.reshape(rows_each, C).astype(BF16)
    for index, weight in enumerate((w_query, w_key, w_value)):
        qkv[:, index * HD : (index + 1) * HD] = nn(normed[...], weight[...]).astype(BF16)
    gatt[...] = nn(cot[...], w_output[...]).astype(BF16)

    square = (rows_each, rows_each)
    same = (lax.broadcasted_iota(jnp.int32, square, 0) % 4) == (
        lax.broadcasted_iota(jnp.int32, square, 1) % 4
    )
    lane = lax.broadcasted_iota(jnp.int32, (rows_each, LANES), 1)

    def split(value):
        zero = jnp.zeros_like(value)
        return jnp.concatenate(
            [jnp.where(lane < DH, value, zero), jnp.where(lane >= DH, value, zero)], axis=0
        )

    units = [
        (pl.ds(group * rows_each, rows_each), pair * LANES)
        for group in range(4)
        for pair in range(2)
    ]

    def part(unit, index):
        return qkv[unit[0], pl.ds(index * HD + unit[1], LANES)]

    scores = [nt(split(part(unit, 1)), part(unit, 0)) for unit in units]
    grad_probs = [
        nt(split(part(unit, 2)), gatt[unit[0], pl.ds(unit[1], LANES)]) for unit in units
    ]
    results = []
    for score2, grad2 in zip(scores, grad_probs):
        lows, grads = [], []
        for head in range(2):
            cut = slice(head * rows_each, (head + 1) * rows_each)
            score = jnp.where(same, score2[cut] * scale, MASKED)
            expon = jnp.exp(score - jnp.max(score, axis=0, keepdims=True))
            probs = expon * (1.0 / jnp.sum(expon, axis=0, keepdims=True))
            weighted = probs * grad2[cut]
            total = jnp.sum(weighted, axis=0, keepdims=True)
            lows.append(probs.astype(BF16))
            grads.append(((weighted - probs * total) * scale).astype(BF16))
        results.append((lows, grads))
    for unit, (lows, grads) in zip(units, results):
        at, lanes = unit[0], pl.ds(unit[1], LANES)
        attended[at, lanes] = tn(jnp.concatenate(lows, axis=0), split(part(unit, 2))).astype(BF16)
        grad_q = tn(jnp.concatenate(grads, axis=0), split(part(unit, 1)))
        grad_k = nn(jnp.concatenate(grads, axis=1), split(part(unit, 0)))
        grad_v = nn(jnp.concatenate(lows, axis=1), split(gatt[at, lanes]))
        for index, grad in enumerate((grad_q, grad_k, grad_v)):
            stacked[at, pl.ds(index * HD + unit[1], LANES)] = grad.astype(BF16)

    gnorm[...] = (
        nt(stacked[:, :HD], w_query[...])
        + nt(stacked[:, HD : 2 * HD], w_key[...])
        + nt(stacked[:, 2 * HD :], w_value[...])
    )
    total = jnp.zeros((8, C), F32)
    for tile in range(2):
        results = []
        for half in range(2):
            at = pl.ds((2 * tile + half) * rows_each, rows_each)
            y = y_rows[at, :]
            inverse = inv_rows[at, :][:, :1]
            grad = gnorm[at, :]
            total = total + jnp.sum((grad * y * inverse).reshape(GROUPS, 8, C), axis=0)
            gained = grad * gain[...]
            mean = jnp.sum(gained * y, axis=-1, keepdims=True) * (1.0 / C)
            result = inverse * (gained - y * (mean * inverse * inverse))
            results.append(result.reshape(GROUPS, 8, C))
        for s, whole in enumerate(pair_up(*results)):
            out[:, s, 8 * tile : 8 * tile + 8, :] = whole.astype(BF16)
    gain_sum[...] = jnp.sum(total, axis=0, keepdims=True)

    for m in range(4):
        if m < 3:
            whole = tn(normed[...], stacked[:, m * HD : (m + 1) * HD])
        else:
            whole = tn(cot[...], attended[...])
        tiles = (whole * predivide).reshape(8, 2, 2, 2, 8, HD)
        for z in range(2):
            for core in range(2):
                away_core, away_z = (core_of(spot) + core) % 2, (side_of(spot) + z) % 2
                for high in range(2):
                    for side in range(2):
                        piece = tiles[:, z, core, high, :, side * LANES : (side + 1) * LANES]
                        halves[away_core, away_z, 4 * m + 2 * high + side] = piece.reshape(
                            ROWS, LANES
                        ).astype(BF16)


def add_cores_kernel(kept, got, keep, send):
    keep[...] = (kept[0, 0].astype(F32) + got[0].astype(F32)).astype(BF16)
    send[...] = (kept[0, 1].astype(F32) + got[1].astype(F32)).astype(BF16)


def add_chips_kernel(kept, got, out):
    out[:, :ROWS, :] = (kept[...].astype(F32) + got[...].astype(F32)).astype(BF16)
    out[:, ROWS:, :] = jnp.zeros((GROUPS, 16, LANES), BF16)


def taps_kernel(
    predivide, spot, lat, other_core, other_chip, cot, ret, gain_sum, sums_in,
    out, edge_l, edge_r, tiles, packed, sem,
):
    del sums_in
    tiles[...] = jnp.zeros_like(tiles)
    for s in range(SL):
        left, right = from_partners(spot, other_core[s].astype(F32), other_chip[s].astype(F32))
        edge_l[s] = silu(left)
        edge_r[s] = silu(right)
    rows = row_index(WL)

    @pl.loop(0, PARTS)
    def _(part):
        here = lanes_of(part)
        sums = [jnp.zeros((8, LANES), F32) for _ in range(10)]
        for s in range(SL):
            grads, cols = [], []
            for h in range(H):
                back = jnp.concatenate(
                    [ret[2 * h, s, :, here].astype(F32), ret[2 * h + 1, s, :, here].astype(F32)],
                    axis=0,
                )
                grads.append(cot[s, h, :, here].astype(F32) + back)
                act = silu(lat[s, h, :, here].astype(F32))
                cols.append(
                    (
                        jnp.where(rows == 0, edge_l[s, h : h + 1, here], pltpu.roll(act, 1, 0)),
                        act,
                        jnp.where(
                            rows == WL - 1, edge_r[s, h : h + 1, here], pltpu.roll(act, WL - 1, 0)
                        ),
                    )
                )
            for h in range(H):
                for a in range(3):
                    if 0 <= h + a - 1 < H:
                        for b in range(3):
                            term = (grads[h] * cols[h + a - 1][b]).reshape(4, 8, LANES)
                            sums[3 * a + b] = sums[3 * a + b] + jnp.sum(term, axis=0)
                sums[9] = sums[9] + jnp.sum(grads[h].reshape(4, 8, LANES), axis=0)
        for r in range(10):
            tiles[4 * part + r // 3, pl.ds(r % 3, 1), :] = jnp.sum(sums[r], axis=0, keepdims=True)
        tiles[4 * part + 3, pl.ds(1, 1), :] = gain_sum[:, here]

    whole = tiles[...] * predivide
    high = whole.astype(BF16).astype(F32)
    packed[...] = jnp.concatenate([high, whole - high], axis=1).astype(BF16)
    copy = pltpu.make_async_copy(packed, out.at[:, pl.ds(ROWS, 16), :], sem)
    copy.start()
    copy.wait()


def back_edges_kernel(for_core, spot, after, cot, ret, out, edges):
    del after
    for s in range(SL):
        for h in range(H):
            at = pl.ds(h, 1)
            edges[0, 0, s, at, :] = cot[s, h, :PX, :].astype(F32)[:1]
            edges[1, 0, s, at, :] = cot[s, h, PX:, :].astype(F32)[PX - 1 :]
            edges[0, 1, s, at, :] = ret[2 * h, s].astype(F32)[:1]
            edges[1, 1, s, at, :] = ret[2 * h + 1, s].astype(F32)[PX - 1 :]
    out[...] = partner_column(spot, for_core, edges[0], edges[1]).astype(BF16)


def latents_kernel(spot, after, lat, cot, ret, other_core, other_chip, taps, out, edge_l, edge_r):
    del after
    for s in range(SL):
        left, right = from_partners(
            spot,
            other_core[0, s].astype(F32) + other_core[1, s].astype(F32),
            other_chip[0, s].astype(F32) + other_chip[1, s].astype(F32),
        )
        below, here, above = row_shifts(left)
        edge_l[s] = taps[2:3, :] * above + taps[5:6, :] * here + taps[8:9, :] * below
        below, here, above = row_shifts(right)
        edge_r[s] = taps[0:1, :] * above + taps[3:4, :] * here + taps[6:7, :] * below
    rows = row_index(WL)

    @pl.loop(0, SL * PARTS)
    def _(step):
        s = step // PARTS
        here = lanes_of(step % PARTS)
        tap = [taps[t : t + 1, here] for t in range(9)]
        grads = []
        for h in range(H):
            back = jnp.concatenate(
                [ret[2 * h, s, :, here].astype(F32), ret[2 * h + 1, s, :, here].astype(F32)],
                axis=0,
            )
            grads.append(cot[s, h, :, here].astype(F32) + back)
        for h in range(H):
            cols = []
            for b in range(3):
                terms = [
                    tap[3 * a + b] * grads[h - a + 1] for a in range(3) if 0 <= h - a + 1 < H
                ]
                cols.append(functools.reduce(jnp.add, terms))
            from_left = jnp.where(
                rows == 0, edge_l[s, h : h + 1, here], pltpu.roll(cols[2], 1, 0)
            )
            from_right = jnp.where(
                rows == WL - 1, edge_r[s, h : h + 1, here], pltpu.roll(cols[0], WL - 1, 0)
            )
            total = cols[1] + from_left + from_right
            value = lat[s, h, :, here].astype(F32)
            sig = 1.0 / (1.0 + jnp.exp(-value))
            out[s, h, :, here] = grads[h] + total * (sig * (1.0 + value * (1.0 - sig)))


def high_low(value):
    high = value.astype(BF16).astype(F32)
    at = lax.broadcasted_iota(jnp.int32, value.shape, 0)
    return jnp.where(at < 4, high, pltpu.roll(value - high, 4, 0))


def second_kernel(spot, recv, out):
    total = jnp.sum(recv[...].astype(F32), axis=0)
    weights = total[:ROWS].reshape(8, 8, LANES)
    taps = total[ROWS : ROWS + 8] + total[ROWS + 8 :]
    both = high_low(taps)
    for z in range(2):
        for core in range(2):
            own = jnp.where(jnp.logical_and(core_of(spot) == core, side_of(spot) == z), 1.0, 0.0)
            for block in range(8):
                out[4 * block + 2 * z + core] = jnp.concatenate(
                    [weights[block] * own, both], axis=0
                ).astype(BF16)


def third_kernel(recv, out):
    total = jnp.sum(recv[...].astype(F32), axis=0)
    both = total[8:]
    result = jnp.concatenate([total[:8], high_low(both + pltpu.roll(both, 4, 0))], axis=0)
    result = result.astype(BF16)
    for s in range(GROUPS):
        out[s] = result


def unpack_kernel(recv, kernel_out, bias_out, gain_out, *outs):
    for part in range(PARTS):
        here = slice(part * LANES, (part + 1) * LANES)
        for group in range(4):
            both = recv[4 * part + group].astype(F32)[8:]
            taps = both + pltpu.roll(both, 4, 0)
            if group < 3:
                kernel_out[3 * group : 3 * group + 3, here] = taps[:3]
            else:
                bias_out[:, here] = taps[:1]
                gain_out[:, here] = taps[1:2]
    for m in range(4):
        for high in range(2):
            for side in range(2):
                piece = recv[4 * m + 2 * high + side].astype(F32)[:8]
                outs[m][8 * high : 8 * high + 8, side * LANES : (side + 1) * LANES] = piece


def on_device(
    latents, cotangent, conv_kernel, conv_bias, norm_gain, w_query, w_key, w_value, w_output
):
    strips = lax.axis_size("azim")
    groups = lax.axis_size("sweep")
    cores = [(i, i ^ 1) for i in range(strips)]
    chips = [(i, (i + 1 if i % 2 else i - 1) % strips) for i in range(strips)]
    sides = [(i, i ^ 2) for i in range(strips)]
    strip = lax.axis_index("azim")
    spot = strip.astype(jnp.int32).reshape(1)
    predivide = 1.0 / math.sqrt(SL * groups * H * WL * strips)
    bias_row = conv_bias.reshape(1, C)
    gain_row = norm_gain.reshape(1, C)
    edge = pltpu.VMEM((SL, H, C), F32)

    one_edge = struct((SL, H, C), BF16)
    column = [pltpu.VMEM((2, SL, H, C), F32)]
    packed = struct((GROUPS, SL, PX, C), BF16)
    far = pl.BlockSpec(memory_space=pltpu.HBM)
    cot_sent, token = pl.pallas_call(
        pack_kernel,
        out_shape=(packed, struct((8, LANES), F32)),
        in_specs=[far],
        out_specs=(far, pl.BlockSpec(memory_space=pltpu.VMEM)),
        scratch_shapes=[pltpu.SemaphoreType.DMA((SL * GROUPS,))],
        compiler_params=params(56),
        cost_estimate=pl.CostEstimate(flops=0, bytes_accessed=1_000_000, transcendentals=0),
    )(cotangent)
    recv_cot = lax.all_to_all(cot_sent, "sweep", split_axis=0, concat_axis=0, tiled=True)
    to_chip = call(
        chip_edge_kernel, one_edge, 16, moved=600_000, smem=1, hbm=(1,), scratch=column
    )(spot, token, latents)
    other_chip = lax.ppermute(to_chip, "azim", chips)
    to_core, table = call(
        core_edge_kernel,
        (one_edge, struct((16, C), F32)),
        16,
        moved=600_000,
        smem=1,
        hbm=(1,),
        scratch=column,
    )(spot, to_chip, latents, conv_kernel, bias_row)
    other_core = lax.ppermute(to_core, "azim", cores)

    sent = call(
        forward_kernel,
        packed,
        16,
        flops=10_000_000,
        moved=1_000_000,
        smem=1,
        scratch=[edge, edge],
    )(spot, latents, other_core, other_chip, table)
    recv = lax.all_to_all(sent, "sweep", split_axis=0, concat_axis=0, tiled=True)

    rows = GROUPS * SL * PX
    grad_attn, halves, gain_sum = call(
        functools.partial(attend_kernel, predivide),
        (
            struct((GROUPS, SL, PX, C), BF16),
            struct((2, 2, GROUPS, ROWS, LANES), BF16),
            struct((1, C), F32),
        ),
        32,
        flops=2_000_000_000,
        moved=6_000_000,
        smem=1,
        scratch=[
            pltpu.VMEM((rows, C), BF16),
            pltpu.VMEM((rows, 3 * HD), BF16),
            pltpu.VMEM((rows, HD), BF16),
            pltpu.VMEM((rows, C), BF16),
            pltpu.VMEM((rows, C), F32),
            pltpu.VMEM((rows, LANES), F32),
            pltpu.VMEM((rows, 3 * HD), BF16),
            pltpu.VMEM((rows, HD), BF16),
            pltpu.VMEM((rows, C), F32),
        ],
    )(spot, recv, recv_cot, w_query, w_key, w_value, w_output, gain_row)
    ret = lax.all_to_all(grad_attn, "sweep", split_axis=0, concat_axis=0, tiled=True)
    from_core = lax.ppermute(halves[1], "azim", cores)
    piece = struct((GROUPS, ROWS, LANES), BF16)
    keep, send = call(add_cores_kernel, (piece, piece), 16, moved=2_000_000)(halves, from_core)
    from_chip = lax.ppermute(send, "azim", sides)
    payload = struct((GROUPS, ROWS + 16, LANES), BF16)
    sums = call(add_chips_kernel, payload, 16, moved=1_000_000)(keep, from_chip)

    vmem = pl.BlockSpec(memory_space=pltpu.VMEM)
    anywhere = pl.BlockSpec(memory_space=pltpu.HBM)
    first_sent = pl.pallas_call(
        functools.partial(taps_kernel, predivide),
        out_shape=payload,
        in_specs=[pl.BlockSpec(memory_space=pltpu.SMEM)] + [vmem] * 6 + [anywhere],
        out_specs=anywhere,
        input_output_aliases={7: 0},
        scratch_shapes=[
            edge,
            edge,
            pltpu.VMEM((GROUPS, 8, LANES), F32),
            pltpu.VMEM((GROUPS, 16, LANES), BF16),
            pltpu.SemaphoreType.DMA,
        ],
        compiler_params=params(16),
        cost_estimate=pl.CostEstimate(
            flops=10_000_000, bytes_accessed=2_000_000, transcendentals=0
        ),
    )(spot, latents, other_core, other_chip, cotangent, ret, gain_sum, sums)
    first_recv = lax.all_to_all(first_sent, "sweep", split_axis=0, concat_axis=0, tiled=True)
    second_sent = call(
        second_kernel, struct((strips, 16, LANES), BF16), 16, moved=1_000_000, smem=1
    )(spot, first_recv)
    second_recv = lax.all_to_all(second_sent, "azim", split_axis=0, concat_axis=0, tiled=True)

    both_edges = struct((2, SL, H, C), BF16)

    def back_edges(for_core, after):
        return call(
            functools.partial(back_edges_kernel, for_core),
            both_edges,
            16,
            moved=100_000,
            smem=1,
            hbm=(1,),
            scratch=[pltpu.VMEM((2, 2, SL, H, C), F32)],
        )(spot, after, cotangent, ret)

    to_core = back_edges(True, second_sent)
    back_core = lax.ppermute(to_core, "azim", cores)
    to_chip = back_edges(False, to_core)
    back_chip = lax.ppermute(to_chip, "azim", chips)

    grad_latents = call(
        latents_kernel,
        struct((SL, H, WL, C), F32),
        16,
        flops=10_000_000,
        moved=4_000_000,
        smem=1,
        hbm=(1,),
        scratch=[edge, edge],
    )(spot, second_sent, latents, cotangent, ret, back_core, back_chip, table)
    second_recv, grad_latents = lax.optimization_barrier((second_recv, grad_latents))

    third_sent = call(third_kernel, struct((GROUPS, 16, LANES), BF16), 16, moved=300_000)(
        second_recv
    )
    third_recv = lax.all_to_all(third_sent, "sweep", split_axis=0, concat_axis=0, tiled=True)

    share = struct((C // strips, HD), F32)
    line = struct((1, C), F32)
    grad_kernel, grad_bias, grad_gain, *shares = call(
        unpack_kernel,
        (struct((9, C), F32), line, line, share, share, share, share),
        16,
        moved=300_000,
    )(third_recv)
    return (
        grad_latents,
        grad_kernel,
        grad_bias.reshape(C),
        grad_gain.reshape(C),
        shares[0],
        shares[1],
        shares[2],
        shares[3],
    )


def solution(mesh):
    image = P("sweep", None, "azim", None)
    share = P("azim", None)
    return jax.shard_map(
        on_device,
        mesh=mesh,
        in_specs=(image, image, P(), P(), P(), P(), P(), P(), P()),
        out_specs=(image, P(), P(), P(), share, share, share, share),
        check_vma=False,
    )
```

```python
import functools
import math

import jax
import jax.numpy as jnp
from jax import lax
from jax.experimental import pallas as pl
from jax.experimental.pallas import tpu as pltpu
from jax.sharding import PartitionSpec as P

DH = 64
EPS = 1e-06
F32 = jnp.float32
BF16 = jnp.bfloat16
MASKED = -1e30

SL, H, WL, C = 2, 8, 32, 512
GROUPS = 16
PX = 16
HD = 256
LANES = 128
PARTS = C // LANES
ROWS = 64


def params(mib):
    return pltpu.CompilerParams(vmem_limit_bytes=mib * 1024 * 1024)


def call(kernel, outs, mib, flops=0, moved=0, scratch=(), smem=0, hbm=()):
    vmem = pl.BlockSpec(memory_space=pltpu.VMEM)

    def run(*args):
        specs = [pl.BlockSpec(memory_space=pltpu.SMEM)] * smem + [vmem] * (len(args) - smem)
        for at in hbm:
            specs[at] = pl.BlockSpec(memory_space=pltpu.HBM)
        return pl.pallas_call(
            kernel,
            out_shape=outs,
            in_specs=specs,
            out_specs=jax.tree.map(lambda _: vmem, outs),
            scratch_shapes=list(scratch),
            compiler_params=params(mib),
            cost_estimate=pl.CostEstimate(
                flops=flops, bytes_accessed=moved, transcendentals=0
            ),
        )(*args)

    return run


def struct(shape, dtype):
    return jax.ShapeDtypeStruct(shape, dtype)


def silu(value):
    return value / (1.0 + jnp.exp(-value))


def nt(left, right):
    return lax.dot_general(left, right, (((1,), (1,)), ((), ())), preferred_element_type=F32)


def tn(left, right):
    return lax.dot_general(left, right, (((0,), (0,)), ((), ())), preferred_element_type=F32)


def nn(left, right):
    return lax.dot_general(left, right, (((1,), (0,)), ((), ())), preferred_element_type=F32)


def lanes_of(part):
    return pl.ds(pl.multiple_of(part * LANES, LANES), LANES)


def row_index(rows):
    return lax.broadcasted_iota(jnp.int32, (rows, LANES), 0)


def row_shifts(value):
    at = lax.broadcasted_iota(jnp.int32, value.shape, 0)
    below = jnp.where(at == 0, 0.0, pltpu.roll(value, 1, 0))
    above = jnp.where(at == H - 1, 0.0, pltpu.roll(value, H - 1, 0))
    return below, value, above


def core_of(spot):
    return spot[0] % 2


def side_of(spot):
    return (spot[0] // 2) % 2


def partner_column(spot, for_core, first, last):
    even = core_of(spot) == 0
    return jnp.where(even, last, first) if for_core else jnp.where(even, first, last)


def from_partners(spot, other_core, other_chip):
    even = core_of(spot) == 0
    return jnp.where(even, other_chip, other_core), jnp.where(even, other_core, other_chip)


def edge_columns(lat, edges):
    for s in range(SL):
        for h in range(H):
            edges[0, s, h : h + 1, :] = lat[s, h, :PX, :].astype(F32)[:1]
            edges[1, s, h : h + 1, :] = lat[s, h, PX:, :].astype(F32)[PX - 1 :]


def pack_kernel(cot, out):
    for s in range(SL):
        for h in range(H):
            out[2 * h, s] = cot[s, h, :PX, :]
            out[2 * h + 1, s] = cot[s, h, PX:, :]


def chip_edge_kernel(spot, after, lat, out, edges):
    del after
    edge_columns(lat, edges)
    out[...] = partner_column(spot, False, edges[0], edges[1]).astype(BF16)


def core_edge_kernel(spot, after, lat, taps, bias, out, table, edges):
    del after
    edge_columns(lat, edges)
    out[...] = partner_column(spot, True, edges[0], edges[1]).astype(BF16)
    table[:9, :] = taps[...]
    table[9:10, :] = bias[...]
    table[10:, :] = jnp.zeros((6, C), F32)


def forward_kernel(spot, lat, other_core, other_chip, taps, out, edge_l, edge_r):
    for s in range(SL):
        left, right = from_partners(spot, other_core[s].astype(F32), other_chip[s].astype(F32))
        shifted = row_shifts(silu(left))
        edge_l[s] = sum(taps[3 * a : 3 * a + 1, :] * shifted[a] for a in range(3))
        shifted = row_shifts(silu(right))
        edge_r[s] = sum(taps[3 * a + 2 : 3 * a + 3, :] * shifted[a] for a in range(3))
    rows = row_index(WL)

    @pl.loop(0, SL * PARTS)
    def _(step):
        s = step // PARTS
        here = lanes_of(step % PARTS)
        tap = [taps[t : t + 1, here] for t in range(9)]
        base = taps[9:10, here]
        values = [lat[s, h, :, here].astype(F32) for h in range(H)]
        acts = [silu(v) for v in values]
        for h in range(H):
            cols = []
            for b in range(3):
                terms = [
                    tap[3 * a + b] * acts[h + a - 1] for a in range(3) if 0 <= h + a - 1 < H
                ]
                cols.append(functools.reduce(jnp.add, terms))
            from_left = jnp.where(
                rows == 0, edge_l[s, h : h + 1, here], pltpu.roll(cols[0], 1, 0)
            )
            from_right = jnp.where(
                rows == WL - 1, edge_r[s, h : h + 1, here], pltpu.roll(cols[2], WL - 1, 0)
            )
            y = (values[h] + (cols[1] + from_left + from_right) + base).astype(BF16)
            out[2 * h, s, :, here] = y[:PX]
            out[2 * h + 1, s, :, here] = y[PX:]


def pair_up(first, second):
    low = lax.broadcasted_iota(jnp.int32, first.shape, 1) < 4
    return (
        jnp.where(low, first, pltpu.roll(second, 4, 1)),
        jnp.where(low, pltpu.roll(first, 4, 1), second),
    )


def attend_kernel(
    predivide, spot, recv, recv_cot, w_query, w_key, w_value, w_output, gain,
    out, halves, gain_sum,
    normed, stacked, attended, cot, y_rows, inv_rows, qkv, gatt, gnorm,
):
    rows_each = GROUPS * 8
    scale = 1.0 / math.sqrt(DH)
    for tile in range(2):
        y_two = [
            recv[:, s].astype(F32)[:, 8 * tile : 8 * tile + 8, :] for s in range(SL)
        ]
        cot_two = [
            recv_cot[:, s].astype(F32)[:, 8 * tile : 8 * tile + 8, :] for s in range(SL)
        ]
        for half, (y, c) in enumerate(zip(pair_up(*y_two), pair_up(*cot_two))):
            at = pl.ds((2 * tile + half) * rows_each, rows_each)
            y = y.reshape(rows_each, C)
            inverse = lax.rsqrt(jnp.sum(y * y, axis=-1, keepdims=True) * (1.0 / C) + EPS)
            y_rows[at, :] = y
            inv_rows[at, :] = jnp.broadcast_to(inverse, (rows_each, LANES))
            normed[at, :] = (y * inverse * gain[...]).astype(BF16)
            cot[at, :] = c.reshape(rows_each, C).astype(BF16)
    for index, weight in enumerate((w_query, w_key, w_value)):
        qkv[:, index * HD : (index + 1) * HD] = nn(normed[...], weight[...]).astype(BF16)
    gatt[...] = nn(cot[...], w_output[...]).astype(BF16)

    square = (rows_each, rows_each)
    same = (lax.broadcasted_iota(jnp.int32, square, 0) % 4) == (
        lax.broadcasted_iota(jnp.int32, square, 1) % 4
    )
    lane = lax.broadcasted_iota(jnp.int32, (rows_each, LANES), 1)

    def split(value):
        zero = jnp.zeros_like(value)
        return jnp.concatenate(
            [jnp.where(lane < DH, value, zero), jnp.where(lane >= DH, value, zero)], axis=0
        )

    units = [
        (pl.ds(group * rows_each, rows_each), pair * LANES)
        for group in range(4)
        for pair in range(2)
    ]

    def part(unit, index):
        return qkv[unit[0], pl.ds(index * HD + unit[1], LANES)]

    scores = [nt(split(part(unit, 1)), part(unit, 0)) for unit in units]
    grad_probs = [
        nt(split(part(unit, 2)), gatt[unit[0], pl.ds(unit[1], LANES)]) for unit in units
    ]
    results = []
    for score2, grad2 in zip(scores, grad_probs):
        lows, grads = [], []
        for head in range(2):
            cut = slice(head * rows_each, (head + 1) * rows_each)
            score = jnp.where(same, score2[cut] * scale, MASKED)
            expon = jnp.exp(score - jnp.max(score, axis=0, keepdims=True))
            probs = expon * (1.0 / jnp.sum(expon, axis=0, keepdims=True))
            weighted = probs * grad2[cut]
            total = jnp.sum(weighted, axis=0, keepdims=True)
            lows.append(probs.astype(BF16))
            grads.append(((weighted - probs * total) * scale).astype(BF16))
        results.append((lows, grads))
    for unit, (lows, grads) in zip(units, results):
        at, lanes = unit[0], pl.ds(unit[1], LANES)
        attended[at, lanes] = tn(jnp.concatenate(lows, axis=0), split(part(unit, 2))).astype(BF16)
        grad_q = tn(jnp.concatenate(grads, axis=0), split(part(unit, 1)))
        grad_k = nn(jnp.concatenate(grads, axis=1), split(part(unit, 0)))
        grad_v = nn(jnp.concatenate(lows, axis=1), split(gatt[at, lanes]))
        for index, grad in enumerate((grad_q, grad_k, grad_v)):
            stacked[at, pl.ds(index * HD + unit[1], LANES)] = grad.astype(BF16)

    gnorm[...] = (
        nt(stacked[:, :HD], w_query[...])
        + nt(stacked[:, HD : 2 * HD], w_key[...])
        + nt(stacked[:, 2 * HD :], w_value[...])
    )
    total = jnp.zeros((8, C), F32)
    for tile in range(2):
        results = []
        for half in range(2):
            at = pl.ds((2 * tile + half) * rows_each, rows_each)
            y = y_rows[at, :]
            inverse = inv_rows[at, :][:, :1]
            grad = gnorm[at, :]
            total = total + jnp.sum((grad * y * inverse).reshape(GROUPS, 8, C), axis=0)
            gained = grad * gain[...]
            mean = jnp.sum(gained * y, axis=-1, keepdims=True) * (1.0 / C)
            result = inverse * (gained - y * (mean * inverse * inverse))
            results.append(result.reshape(GROUPS, 8, C))
        for s, whole in enumerate(pair_up(*results)):
            out[:, s, 8 * tile : 8 * tile + 8, :] = whole.astype(BF16)
    gain_sum[...] = jnp.sum(total, axis=0, keepdims=True)

    for m in range(4):
        if m < 3:
            whole = tn(normed[...], stacked[:, m * HD : (m + 1) * HD])
        else:
            whole = tn(cot[...], attended[...])
        tiles = (whole * predivide).reshape(8, 2, 2, 2, 8, HD)
        for z in range(2):
            for core in range(2):
                away_core, away_z = (core_of(spot) + core) % 2, (side_of(spot) + z) % 2
                for high in range(2):
                    for side in range(2):
                        piece = tiles[:, z, core, high, :, side * LANES : (side + 1) * LANES]
                        halves[away_core, away_z, 4 * m + 2 * high + side] = piece.reshape(
                            ROWS, LANES
                        ).astype(BF16)


def add_cores_kernel(kept, got, keep, send):
    keep[...] = (kept[0, 0].astype(F32) + got[0].astype(F32)).astype(BF16)
    send[...] = (kept[0, 1].astype(F32) + got[1].astype(F32)).astype(BF16)


def add_chips_kernel(kept, got, out):
    out[:, :ROWS, :] = (kept[...].astype(F32) + got[...].astype(F32)).astype(BF16)
    out[:, ROWS:, :] = jnp.zeros((GROUPS, 16, LANES), BF16)


def taps_kernel(
    predivide, spot, lat, other_core, other_chip, cot, ret, gain_sum, sums_in,
    out, edge_l, edge_r, tiles, packed, sem,
):
    del sums_in
    tiles[...] = jnp.zeros_like(tiles)
    for s in range(SL):
        left, right = from_partners(spot, other_core[s].astype(F32), other_chip[s].astype(F32))
        edge_l[s] = silu(left)
        edge_r[s] = silu(right)
    rows = row_index(WL)

    @pl.loop(0, PARTS)
    def _(part):
        here = lanes_of(part)
        sums = [jnp.zeros((8, LANES), F32) for _ in range(10)]
        for s in range(SL):
            grads, cols = [], []
            for h in range(H):
                back = jnp.concatenate(
                    [ret[2 * h, s, :, here].astype(F32), ret[2 * h + 1, s, :, here].astype(F32)],
                    axis=0,
                )
                grads.append(cot[s, h, :, here].astype(F32) + back)
                act = silu(lat[s, h, :, here].astype(F32))
                cols.append(
                    (
                        jnp.where(rows == 0, edge_l[s, h : h + 1, here], pltpu.roll(act, 1, 0)),
                        act,
                        jnp.where(
                            rows == WL - 1, edge_r[s, h : h + 1, here], pltpu.roll(act, WL - 1, 0)
                        ),
                    )
                )
            for h in range(H):
                for a in range(3):
                    if 0 <= h + a - 1 < H:
                        for b in range(3):
                            term = (grads[h] * cols[h + a - 1][b]).reshape(4, 8, LANES)
                            sums[3 * a + b] = sums[3 * a + b] + jnp.sum(term, axis=0)
                sums[9] = sums[9] + jnp.sum(grads[h].reshape(4, 8, LANES), axis=0)
        for r in range(10):
            tiles[4 * part + r // 3, pl.ds(r % 3, 1), :] = jnp.sum(sums[r], axis=0, keepdims=True)
        tiles[4 * part + 3, pl.ds(1, 1), :] = gain_sum[:, here]

    whole = tiles[...] * predivide
    high = whole.astype(BF16).astype(F32)
    packed[...] = jnp.concatenate([high, whole - high], axis=1).astype(BF16)
    copy = pltpu.make_async_copy(packed, out.at[:, pl.ds(ROWS, 16), :], sem)
    copy.start()
    copy.wait()


def back_edges_kernel(for_core, spot, after, cot, ret, out, edges):
    del after
    for s in range(SL):
        for h in range(H):
            at = pl.ds(h, 1)
            edges[0, 0, s, at, :] = cot[s, h, :PX, :].astype(F32)[:1]
            edges[1, 0, s, at, :] = cot[s, h, PX:, :].astype(F32)[PX - 1 :]
            edges[0, 1, s, at, :] = ret[2 * h, s].astype(F32)[:1]
            edges[1, 1, s, at, :] = ret[2 * h + 1, s].astype(F32)[PX - 1 :]
    out[...] = partner_column(spot, for_core, edges[0], edges[1]).astype(BF16)


def latents_kernel(
    spot, after, lat, cot, ret, other_core, other_chip, taps, out, edge_l, edge_r, near, sems
):
    del after
    for s in range(SL):
        left, right = from_partners(
            spot,
            other_core[0, s].astype(F32) + other_core[1, s].astype(F32),
            other_chip[0, s].astype(F32) + other_chip[1, s].astype(F32),
        )
        below, here, above = row_shifts(left)
        edge_l[s] = taps[2:3, :] * above + taps[5:6, :] * here + taps[8:9, :] * below
        below, here, above = row_shifts(right)
        edge_r[s] = taps[0:1, :] * above + taps[3:4, :] * here + taps[6:7, :] * below
    rows = row_index(WL)

    @pl.loop(0, SL * PARTS)
    def _(step):
        s = step // PARTS
        here = lanes_of(step % PARTS)
        tap = [taps[t : t + 1, here] for t in range(9)]
        grads = []
        for h in range(H):
            back = jnp.concatenate(
                [ret[2 * h, s, :, here].astype(F32), ret[2 * h + 1, s, :, here].astype(F32)],
                axis=0,
            )
            grads.append(cot[s, h, :, here].astype(F32) + back)
        for h in range(H):
            cols = []
            for b in range(3):
                terms = [
                    tap[3 * a + b] * grads[h - a + 1] for a in range(3) if 0 <= h - a + 1 < H
                ]
                cols.append(functools.reduce(jnp.add, terms))
            from_left = jnp.where(
                rows == 0, edge_l[s, h : h + 1, here], pltpu.roll(cols[2], 1, 0)
            )
            from_right = jnp.where(
                rows == WL - 1, edge_r[s, h : h + 1, here], pltpu.roll(cols[0], WL - 1, 0)
            )
            total = cols[1] + from_left + from_right
            value = lat[s, h, :, here].astype(F32)
            sig = 1.0 / (1.0 + jnp.exp(-value))
            near[s, h, :, here] = grads[h] + total * (sig * (1.0 + value * (1.0 - sig)))
        pltpu.make_async_copy(
            near.at[s, :, :, here], out.at[s, :, :, here], sems.at[step]
        ).start()

    for step in range(SL * PARTS):
        s, here = step // PARTS, pl.ds(step % PARTS * LANES, LANES)
        pltpu.make_async_copy(
            near.at[s, :, :, here], out.at[s, :, :, here], sems.at[step]
        ).wait()


def high_low(value):
    high = value.astype(BF16).astype(F32)
    at = lax.broadcasted_iota(jnp.int32, value.shape, 0)
    return jnp.where(at < 4, high, pltpu.roll(value - high, 4, 0))


def second_kernel(spot, recv, out):
    total = jnp.sum(recv[...].astype(F32), axis=0)
    weights = total[:ROWS].reshape(8, 8, LANES)
    taps = total[ROWS : ROWS + 8] + total[ROWS + 8 :]
    both = high_low(taps)
    for z in range(2):
        for core in range(2):
            own = jnp.where(jnp.logical_and(core_of(spot) == core, side_of(spot) == z), 1.0, 0.0)
            for block in range(8):
                out[4 * block + 2 * z + core] = jnp.concatenate(
                    [weights[block] * own, both], axis=0
                ).astype(BF16)


def third_kernel(recv, out):
    total = jnp.sum(recv[...].astype(F32), axis=0)
    both = total[8:]
    result = jnp.concatenate([total[:8], high_low(both + pltpu.roll(both, 4, 0))], axis=0)
    result = result.astype(BF16)
    for s in range(GROUPS):
        out[s] = result


def unpack_kernel(recv, kernel_out, bias_out, gain_out, *outs):
    for part in range(PARTS):
        here = slice(part * LANES, (part + 1) * LANES)
        for group in range(4):
            both = recv[4 * part + group].astype(F32)[8:]
            taps = both + pltpu.roll(both, 4, 0)
            if group < 3:
                kernel_out[3 * group : 3 * group + 3, here] = taps[:3]
            else:
                bias_out[:, here] = taps[:1]
                gain_out[:, here] = taps[1:2]
    for m in range(4):
        for high in range(2):
            for side in range(2):
                piece = recv[4 * m + 2 * high + side].astype(F32)[:8]
                outs[m][8 * high : 8 * high + 8, side * LANES : (side + 1) * LANES] = piece


def on_device(
    latents, cotangent, conv_kernel, conv_bias, norm_gain, w_query, w_key, w_value, w_output
):
    strips = lax.axis_size("azim")
    groups = lax.axis_size("sweep")
    cores = [(i, i ^ 1) for i in range(strips)]
    chips = [(i, (i + 1 if i % 2 else i - 1) % strips) for i in range(strips)]
    sides = [(i, i ^ 2) for i in range(strips)]
    strip = lax.axis_index("azim")
    spot = strip.astype(jnp.int32).reshape(1)
    predivide = 1.0 / math.sqrt(SL * groups * H * WL * strips)
    bias_row = conv_bias.reshape(1, C)
    gain_row = norm_gain.reshape(1, C)
    edge = pltpu.VMEM((SL, H, C), F32)

    one_edge = struct((SL, H, C), BF16)
    column = [pltpu.VMEM((2, SL, H, C), F32)]
    packed = struct((GROUPS, SL, PX, C), BF16)
    cot_sent = call(pack_kernel, packed, 16, moved=1_000_000)(cotangent)
    recv_cot = lax.all_to_all(cot_sent, "sweep", split_axis=0, concat_axis=0, tiled=True)
    to_chip = call(
        chip_edge_kernel, one_edge, 16, moved=600_000, smem=1, hbm=(1,), scratch=column
    )(spot, cot_sent, latents)
    other_chip = lax.ppermute(to_chip, "azim", chips)
    to_core, table = call(
        core_edge_kernel,
        (one_edge, struct((16, C), F32)),
        16,
        moved=600_000,
        smem=1,
        hbm=(1,),
        scratch=column,
    )(spot, to_chip, latents, conv_kernel, bias_row)
    other_core = lax.ppermute(to_core, "azim", cores)

    sent = call(
        forward_kernel,
        packed,
        16,
        flops=10_000_000,
        moved=1_000_000,
        smem=1,
        scratch=[edge, edge],
    )(spot, latents, other_core, other_chip, table)
    recv = lax.all_to_all(sent, "sweep", split_axis=0, concat_axis=0, tiled=True)

    rows = GROUPS * SL * PX
    grad_attn, halves, gain_sum = call(
        functools.partial(attend_kernel, predivide),
        (
            struct((GROUPS, SL, PX, C), BF16),
            struct((2, 2, GROUPS, ROWS, LANES), BF16),
            struct((1, C), F32),
        ),
        32,
        flops=2_000_000_000,
        moved=6_000_000,
        smem=1,
        scratch=[
            pltpu.VMEM((rows, C), BF16),
            pltpu.VMEM((rows, 3 * HD), BF16),
            pltpu.VMEM((rows, HD), BF16),
            pltpu.VMEM((rows, C), BF16),
            pltpu.VMEM((rows, C), F32),
            pltpu.VMEM((rows, LANES), F32),
            pltpu.VMEM((rows, 3 * HD), BF16),
            pltpu.VMEM((rows, HD), BF16),
            pltpu.VMEM((rows, C), F32),
        ],
    )(spot, recv, recv_cot, w_query, w_key, w_value, w_output, gain_row)
    ret = lax.all_to_all(grad_attn, "sweep", split_axis=0, concat_axis=0, tiled=True)
    from_core = lax.ppermute(halves[1], "azim", cores)
    piece = struct((GROUPS, ROWS, LANES), BF16)
    keep, send = call(add_cores_kernel, (piece, piece), 16, moved=2_000_000)(halves, from_core)
    from_chip = lax.ppermute(send, "azim", sides)
    payload = struct((GROUPS, ROWS + 16, LANES), BF16)
    sums = call(add_chips_kernel, payload, 16, moved=1_000_000)(keep, from_chip)

    vmem = pl.BlockSpec(memory_space=pltpu.VMEM)
    anywhere = pl.BlockSpec(memory_space=pltpu.HBM)
    first_sent = pl.pallas_call(
        functools.partial(taps_kernel, predivide),
        out_shape=payload,
        in_specs=[pl.BlockSpec(memory_space=pltpu.SMEM)] + [vmem] * 6 + [anywhere],
        out_specs=anywhere,
        input_output_aliases={7: 0},
        scratch_shapes=[
            edge,
            edge,
            pltpu.VMEM((GROUPS, 8, LANES), F32),
            pltpu.VMEM((GROUPS, 16, LANES), BF16),
            pltpu.SemaphoreType.DMA,
        ],
        compiler_params=params(16),
        cost_estimate=pl.CostEstimate(
            flops=10_000_000, bytes_accessed=2_000_000, transcendentals=0
        ),
    )(spot, latents, other_core, other_chip, cotangent, ret, gain_sum, sums)
    first_recv = lax.all_to_all(first_sent, "sweep", split_axis=0, concat_axis=0, tiled=True)
    second_sent = call(
        second_kernel, struct((strips, 16, LANES), BF16), 16, moved=1_000_000, smem=1
    )(spot, first_recv)
    second_recv = lax.all_to_all(second_sent, "azim", split_axis=0, concat_axis=0, tiled=True)

    both_edges = struct((2, SL, H, C), BF16)

    def back_edges(for_core, after):
        return call(
            functools.partial(back_edges_kernel, for_core),
            both_edges,
            16,
            moved=100_000,
            smem=1,
            hbm=(1,),
            scratch=[pltpu.VMEM((2, 2, SL, H, C), F32)],
        )(spot, after, cotangent, ret)

    to_core = back_edges(True, second_sent)
    back_core = lax.ppermute(to_core, "azim", cores)
    to_chip = back_edges(False, to_core)
    back_chip = lax.ppermute(to_chip, "azim", chips)

    grad_latents = pl.pallas_call(
        latents_kernel,
        out_shape=struct((SL, H, WL, C), F32),
        in_specs=[pl.BlockSpec(memory_space=pltpu.SMEM), anywhere] + [vmem] * 6,
        out_specs=anywhere,
        scratch_shapes=[edge, edge]
        + [pltpu.VMEM((SL, H, WL, C), F32), pltpu.SemaphoreType.DMA((SL * PARTS,))],
        compiler_params=params(16),
        cost_estimate=pl.CostEstimate(
            flops=10_000_000, bytes_accessed=4_000_000, transcendentals=0
        ),
    )(spot, second_sent, latents, cotangent, ret, back_core, back_chip, table)
    second_recv, grad_latents = lax.optimization_barrier((second_recv, grad_latents))

    third_sent = call(third_kernel, struct((GROUPS, 16, LANES), BF16), 16, moved=300_000)(
        second_recv
    )
    third_recv = lax.all_to_all(third_sent, "sweep", split_axis=0, concat_axis=0, tiled=True)

    share = struct((C // strips, HD), F32)
    line = struct((1, C), F32)
    grad_kernel, grad_bias, grad_gain, *shares = call(
        unpack_kernel,
        (struct((9, C), F32), line, line, share, share, share, share),
        16,
        moved=300_000,
    )(third_recv)
    return (
        grad_latents,
        grad_kernel,
        grad_bias.reshape(C),
        grad_gain.reshape(C),
        shares[0],
        shares[1],
        shares[2],
        shares[3],
    )


def solution(mesh):
    image = P("sweep", None, "azim", None)
    share = P("azim", None)
    return jax.shard_map(
        on_device,
        mesh=mesh,
        in_specs=(image, image, P(), P(), P(), P(), P(), P(), P()),
        out_specs=(image, P(), P(), P(), share, share, share, share),
        check_vma=False,
    )
```

```python
import functools
import math

import jax
import jax.numpy as jnp
from jax import lax
from jax.experimental import pallas as pl
from jax.experimental.pallas import tpu as pltpu
from jax.sharding import PartitionSpec as P

DH = 64
EPS = 1e-06
F32 = jnp.float32
BF16 = jnp.bfloat16
MASKED = -1e30

SL, H, WL, C = 2, 8, 32, 512
GROUPS = 16
PX = 16
HD = 256
LANES = 128
PARTS = C // LANES
ROWS = 64


def params(mib):
    return pltpu.CompilerParams(vmem_limit_bytes=mib * 1024 * 1024)


def call(kernel, outs, mib, flops=0, moved=0, scratch=(), smem=0, hbm=()):
    vmem = pl.BlockSpec(memory_space=pltpu.VMEM)

    def run(*args):
        specs = [pl.BlockSpec(memory_space=pltpu.SMEM)] * smem + [vmem] * (len(args) - smem)
        for at in hbm:
            specs[at] = pl.BlockSpec(memory_space=pltpu.HBM)
        return pl.pallas_call(
            kernel,
            out_shape=outs,
            in_specs=specs,
            out_specs=jax.tree.map(lambda _: vmem, outs),
            scratch_shapes=list(scratch),
            compiler_params=params(mib),
            cost_estimate=pl.CostEstimate(
                flops=flops, bytes_accessed=moved, transcendentals=0
            ),
        )(*args)

    return run


def struct(shape, dtype):
    return jax.ShapeDtypeStruct(shape, dtype)


def silu(value):
    return value / (1.0 + jnp.exp(-value))


def nt(left, right):
    return lax.dot_general(left, right, (((1,), (1,)), ((), ())), preferred_element_type=F32)


def tn(left, right):
    return lax.dot_general(left, right, (((0,), (0,)), ((), ())), preferred_element_type=F32)


def nn(left, right):
    return lax.dot_general(left, right, (((1,), (0,)), ((), ())), preferred_element_type=F32)


def lanes_of(part):
    return pl.ds(pl.multiple_of(part * LANES, LANES), LANES)


def row_index(rows):
    return lax.broadcasted_iota(jnp.int32, (rows, LANES), 0)


def row_shifts(value):
    at = lax.broadcasted_iota(jnp.int32, value.shape, 0)
    below = jnp.where(at == 0, 0.0, pltpu.roll(value, 1, 0))
    above = jnp.where(at == H - 1, 0.0, pltpu.roll(value, H - 1, 0))
    return below, value, above


def core_of(spot):
    return spot[0] % 2


def side_of(spot):
    return (spot[0] // 2) % 2


def partner_column(spot, for_core, first, last):
    even = core_of(spot) == 0
    return jnp.where(even, last, first) if for_core else jnp.where(even, first, last)


def from_partners(spot, other_core, other_chip):
    even = core_of(spot) == 0
    return jnp.where(even, other_chip, other_core), jnp.where(even, other_core, other_chip)


def edge_columns(lat, edges):
    for s in range(SL):
        for h in range(H):
            edges[0, s, h : h + 1, :] = lat[s, h, :PX, :].astype(F32)[:1]
            edges[1, s, h : h + 1, :] = lat[s, h, PX:, :].astype(F32)[PX - 1 :]


def pack_kernel(cot, out):
    for h in range(H):
        out[2 * h, 0] = cot[0, h, :PX, :]
        out[2 * h + 1, 0] = cot[0, h, PX:, :]


def chip_edge_kernel(spot, after, lat, out, edges):
    del after
    edge_columns(lat, edges)
    out[...] = partner_column(spot, False, edges[0], edges[1]).astype(BF16)


def core_edge_kernel(spot, after, lat, taps, bias, out, table, edges):
    del after
    edge_columns(lat, edges)
    out[...] = partner_column(spot, True, edges[0], edges[1]).astype(BF16)
    table[:9, :] = taps[...]
    table[9:10, :] = bias[...]
    table[10:, :] = jnp.zeros((6, C), F32)


def forward_kernel(spot, lat, other_core, other_chip, taps, out, edge_l, edge_r):
    for s in range(SL):
        left, right = from_partners(spot, other_core[s].astype(F32), other_chip[s].astype(F32))
        shifted = row_shifts(silu(left))
        edge_l[s] = sum(taps[3 * a : 3 * a + 1, :] * shifted[a] for a in range(3))
        shifted = row_shifts(silu(right))
        edge_r[s] = sum(taps[3 * a + 2 : 3 * a + 3, :] * shifted[a] for a in range(3))
    rows = row_index(WL)

    @pl.loop(0, SL * PARTS)
    def _(step):
        s = step // PARTS
        here = lanes_of(step % PARTS)
        tap = [taps[t : t + 1, here] for t in range(9)]
        base = taps[9:10, here]
        values = [lat[s, h, :, here].astype(F32) for h in range(H)]
        acts = [silu(v) for v in values]
        for h in range(H):
            cols = []
            for b in range(3):
                terms = [
                    tap[3 * a + b] * acts[h + a - 1] for a in range(3) if 0 <= h + a - 1 < H
                ]
                cols.append(functools.reduce(jnp.add, terms))
            from_left = jnp.where(
                rows == 0, edge_l[s, h : h + 1, here], pltpu.roll(cols[0], 1, 0)
            )
            from_right = jnp.where(
                rows == WL - 1, edge_r[s, h : h + 1, here], pltpu.roll(cols[2], WL - 1, 0)
            )
            y = (values[h] + (cols[1] + from_left + from_right) + base).astype(BF16)
            out[2 * h, s, :, here] = y[:PX]
            out[2 * h + 1, s, :, here] = y[PX:]


def pair_up(first, second):
    low = lax.broadcasted_iota(jnp.int32, first.shape, 1) < 4
    return (
        jnp.where(low, first, pltpu.roll(second, 4, 1)),
        jnp.where(low, pltpu.roll(first, 4, 1), second),
    )


def attend_kernel(
    predivide, spot, recv, recv_cot, w_query, w_key, w_value, w_output, gain,
    out, halves, gain_sum,
    normed, stacked, attended, cot, y_rows, inv_rows, qkv, gatt, gnorm,
):
    rows_each = GROUPS * 8
    scale = 1.0 / math.sqrt(DH)
    for tile in range(2):
        y_two = [
            recv[:, s].astype(F32)[:, 8 * tile : 8 * tile + 8, :] for s in range(SL)
        ]
        cot_two = [
            recv_cot[:, s].astype(F32)[:, 8 * tile : 8 * tile + 8, :] for s in range(SL)
        ]
        for half, (y, c) in enumerate(zip(pair_up(*y_two), pair_up(*cot_two))):
            at = pl.ds((2 * tile + half) * rows_each, rows_each)
            y = y.reshape(rows_each, C)
            inverse = lax.rsqrt(jnp.sum(y * y, axis=-1, keepdims=True) * (1.0 / C) + EPS)
            y_rows[at, :] = y
            inv_rows[at, :] = jnp.broadcast_to(inverse, (rows_each, LANES))
            normed[at, :] = (y * inverse * gain[...]).astype(BF16)
            cot[at, :] = c.reshape(rows_each, C).astype(BF16)
    for index, weight in enumerate((w_query, w_key, w_value)):
        qkv[:, index * HD : (index + 1) * HD] = nn(normed[...], weight[...]).astype(BF16)
    gatt[...] = nn(cot[...], w_output[...]).astype(BF16)

    square = (rows_each, rows_each)
    same = (lax.broadcasted_iota(jnp.int32, square, 0) % 4) == (
        lax.broadcasted_iota(jnp.int32, square, 1) % 4
    )
    lane = lax.broadcasted_iota(jnp.int32, (rows_each, LANES), 1)

    def split(value):
        zero = jnp.zeros_like(value)
        return jnp.concatenate(
            [jnp.where(lane < DH, value, zero), jnp.where(lane >= DH, value, zero)], axis=0
        )

    units = [
        (pl.ds(group * rows_each, rows_each), pair * LANES)
        for group in range(4)
        for pair in range(2)
    ]

    def part(unit, index):
        return qkv[unit[0], pl.ds(index * HD + unit[1], LANES)]

    scores = [nt(split(part(unit, 1)), part(unit, 0)) for unit in units]
    grad_probs = [
        nt(split(part(unit, 2)), gatt[unit[0], pl.ds(unit[1], LANES)]) for unit in units
    ]
    results = []
    for score2, grad2 in zip(scores, grad_probs):
        lows, grads = [], []
        for head in range(2):
            cut = slice(head * rows_each, (head + 1) * rows_each)
            score = jnp.where(same, score2[cut] * scale, MASKED)
            expon = jnp.exp(score - jnp.max(score, axis=0, keepdims=True))
            probs = expon * (1.0 / jnp.sum(expon, axis=0, keepdims=True))
            weighted = probs * grad2[cut]
            total = jnp.sum(weighted, axis=0, keepdims=True)
            lows.append(probs.astype(BF16))
            grads.append(((weighted - probs * total) * scale).astype(BF16))
        results.append((lows, grads))
    for unit, (lows, grads) in zip(units, results):
        at, lanes = unit[0], pl.ds(unit[1], LANES)
        attended[at, lanes] = tn(jnp.concatenate(lows, axis=0), split(part(unit, 2))).astype(BF16)
        grad_q = tn(jnp.concatenate(grads, axis=0), split(part(unit, 1)))
        grad_k = nn(jnp.concatenate(grads, axis=1), split(part(unit, 0)))
        grad_v = nn(jnp.concatenate(lows, axis=1), split(gatt[at, lanes]))
        for index, grad in enumerate((grad_q, grad_k, grad_v)):
            stacked[at, pl.ds(index * HD + unit[1], LANES)] = grad.astype(BF16)

    gnorm[...] = (
        nt(stacked[:, :HD], w_query[...])
        + nt(stacked[:, HD : 2 * HD], w_key[...])
        + nt(stacked[:, 2 * HD :], w_value[...])
    )
    total = jnp.zeros((8, C), F32)
    for tile in range(2):
        results = []
        for half in range(2):
            at = pl.ds((2 * tile + half) * rows_each, rows_each)
            y = y_rows[at, :]
            inverse = inv_rows[at, :][:, :1]
            grad = gnorm[at, :]
            total = total + jnp.sum((grad * y * inverse).reshape(GROUPS, 8, C), axis=0)
            gained = grad * gain[...]
            mean = jnp.sum(gained * y, axis=-1, keepdims=True) * (1.0 / C)
            result = inverse * (gained - y * (mean * inverse * inverse))
            results.append(result.reshape(GROUPS, 8, C))
        for s, whole in enumerate(pair_up(*results)):
            out[:, s, 8 * tile : 8 * tile + 8, :] = whole.astype(BF16)
    gain_sum[...] = jnp.sum(total, axis=0, keepdims=True)

    for m in range(4):
        if m < 3:
            whole = tn(normed[...], stacked[:, m * HD : (m + 1) * HD])
        else:
            whole = tn(cot[...], attended[...])
        tiles = (whole * predivide).reshape(8, 2, 2, 2, 8, HD)
        for z in range(2):
            for core in range(2):
                away_core, away_z = (core_of(spot) + core) % 2, (side_of(spot) + z) % 2
                for high in range(2):
                    for side in range(2):
                        piece = tiles[:, z, core, high, :, side * LANES : (side + 1) * LANES]
                        halves[away_core, away_z, 4 * m + 2 * high + side] = piece.reshape(
                            ROWS, LANES
                        ).astype(BF16)


def add_cores_kernel(kept, got, keep, send):
    keep[...] = (kept[0, 0].astype(F32) + got[0].astype(F32)).astype(BF16)
    send[...] = (kept[0, 1].astype(F32) + got[1].astype(F32)).astype(BF16)


def add_chips_kernel(kept, got, out):
    out[:, :ROWS, :] = (kept[...].astype(F32) + got[...].astype(F32)).astype(BF16)
    out[:, ROWS:, :] = jnp.zeros((GROUPS, 16, LANES), BF16)


def taps_kernel(
    predivide, spot, lat, other_core, other_chip, cot, ret, gain_sum, sums_in,
    out, edge_l, edge_r, tiles, packed, sem,
):
    del sums_in
    tiles[...] = jnp.zeros_like(tiles)
    for s in range(SL):
        left, right = from_partners(spot, other_core[s].astype(F32), other_chip[s].astype(F32))
        edge_l[s] = silu(left)
        edge_r[s] = silu(right)
    rows = row_index(WL)

    @pl.loop(0, PARTS)
    def _(part):
        here = lanes_of(part)
        sums = [jnp.zeros((8, LANES), F32) for _ in range(10)]
        for s in range(SL):
            grads, cols = [], []
            for h in range(H):
                back = jnp.concatenate(
                    [ret[2 * h, s, :, here].astype(F32), ret[2 * h + 1, s, :, here].astype(F32)],
                    axis=0,
                )
                grads.append(cot[s, h, :, here].astype(F32) + back)
                act = silu(lat[s, h, :, here].astype(F32))
                cols.append(
                    (
                        jnp.where(rows == 0, edge_l[s, h : h + 1, here], pltpu.roll(act, 1, 0)),
                        act,
                        jnp.where(
                            rows == WL - 1, edge_r[s, h : h + 1, here], pltpu.roll(act, WL - 1, 0)
                        ),
                    )
                )
            for h in range(H):
                for a in range(3):
                    if 0 <= h + a - 1 < H:
                        for b in range(3):
                            term = (grads[h] * cols[h + a - 1][b]).reshape(4, 8, LANES)
                            sums[3 * a + b] = sums[3 * a + b] + jnp.sum(term, axis=0)
                sums[9] = sums[9] + jnp.sum(grads[h].reshape(4, 8, LANES), axis=0)
        for r in range(10):
            tiles[4 * part + r // 3, pl.ds(r % 3, 1), :] = jnp.sum(sums[r], axis=0, keepdims=True)
        tiles[4 * part + 3, pl.ds(1, 1), :] = gain_sum[:, here]

    whole = tiles[...] * predivide
    high = whole.astype(BF16).astype(F32)
    packed[...] = jnp.concatenate([high, whole - high], axis=1).astype(BF16)
    copy = pltpu.make_async_copy(packed, out.at[:, pl.ds(ROWS, 16), :], sem)
    copy.start()
    copy.wait()


def back_edges_kernel(for_core, spot, after, cot, ret, out, edges):
    del after
    for s in range(SL):
        for h in range(H):
            at = pl.ds(h, 1)
            edges[0, 0, s, at, :] = cot[s, h, :PX, :].astype(F32)[:1]
            edges[1, 0, s, at, :] = cot[s, h, PX:, :].astype(F32)[PX - 1 :]
            edges[0, 1, s, at, :] = ret[2 * h, s].astype(F32)[:1]
            edges[1, 1, s, at, :] = ret[2 * h + 1, s].astype(F32)[PX - 1 :]
    out[...] = partner_column(spot, for_core, edges[0], edges[1]).astype(BF16)


def latents_kernel(
    spot, after, lat, cot, ret, other_core, other_chip, taps, out, edge_l, edge_r, near, sems
):
    del after
    for s in range(SL):
        left, right = from_partners(
            spot,
            other_core[0, s].astype(F32) + other_core[1, s].astype(F32),
            other_chip[0, s].astype(F32) + other_chip[1, s].astype(F32),
        )
        below, here, above = row_shifts(left)
        edge_l[s] = taps[2:3, :] * above + taps[5:6, :] * here + taps[8:9, :] * below
        below, here, above = row_shifts(right)
        edge_r[s] = taps[0:1, :] * above + taps[3:4, :] * here + taps[6:7, :] * below
    rows = row_index(WL)

    @pl.loop(0, SL * PARTS)
    def _(step):
        s = step // PARTS
        here = lanes_of(step % PARTS)
        tap = [taps[t : t + 1, here] for t in range(9)]
        grads = []
        for h in range(H):
            back = jnp.concatenate(
                [ret[2 * h, s, :, here].astype(F32), ret[2 * h + 1, s, :, here].astype(F32)],
                axis=0,
            )
            grads.append(cot[s, h, :, here].astype(F32) + back)
        for h in range(H):
            cols = []
            for b in range(3):
                terms = [
                    tap[3 * a + b] * grads[h - a + 1] for a in range(3) if 0 <= h - a + 1 < H
                ]
                cols.append(functools.reduce(jnp.add, terms))
            from_left = jnp.where(
                rows == 0, edge_l[s, h : h + 1, here], pltpu.roll(cols[2], 1, 0)
            )
            from_right = jnp.where(
                rows == WL - 1, edge_r[s, h : h + 1, here], pltpu.roll(cols[0], WL - 1, 0)
            )
            total = cols[1] + from_left + from_right
            value = lat[s, h, :, here].astype(F32)
            sig = 1.0 / (1.0 + jnp.exp(-value))
            near[s, h, :, here] = grads[h] + total * (sig * (1.0 + value * (1.0 - sig)))
        pltpu.make_async_copy(
            near.at[s, :, :, here], out.at[s, :, :, here], sems.at[step]
        ).start()

    for step in range(SL * PARTS):
        s, here = step // PARTS, pl.ds(step % PARTS * LANES, LANES)
        pltpu.make_async_copy(
            near.at[s, :, :, here], out.at[s, :, :, here], sems.at[step]
        ).wait()


def high_low(value):
    high = value.astype(BF16).astype(F32)
    at = lax.broadcasted_iota(jnp.int32, value.shape, 0)
    return jnp.where(at < 4, high, pltpu.roll(value - high, 4, 0))


def second_kernel(spot, recv, out):
    total = jnp.sum(recv[...].astype(F32), axis=0)
    weights = total[:ROWS].reshape(8, 8, LANES)
    taps = total[ROWS : ROWS + 8] + total[ROWS + 8 :]
    both = high_low(taps)
    for z in range(2):
        for core in range(2):
            own = jnp.where(jnp.logical_and(core_of(spot) == core, side_of(spot) == z), 1.0, 0.0)
            for block in range(8):
                out[4 * block + 2 * z + core] = jnp.concatenate(
                    [weights[block] * own, both], axis=0
                ).astype(BF16)


def third_kernel(recv, out):
    total = jnp.sum(recv[...].astype(F32), axis=0)
    both = total[8:]
    result = jnp.concatenate([total[:8], high_low(both + pltpu.roll(both, 4, 0))], axis=0)
    result = result.astype(BF16)
    for s in range(GROUPS):
        out[s] = result


def unpack_kernel(recv, kernel_out, bias_out, gain_out, *outs):
    for part in range(PARTS):
        here = slice(part * LANES, (part + 1) * LANES)
        for group in range(4):
            both = recv[4 * part + group].astype(F32)[8:]
            taps = both + pltpu.roll(both, 4, 0)
            if group < 3:
                kernel_out[3 * group : 3 * group + 3, here] = taps[:3]
            else:
                bias_out[:, here] = taps[:1]
                gain_out[:, here] = taps[1:2]
    for m in range(4):
        for high in range(2):
            for side in range(2):
                piece = recv[4 * m + 2 * high + side].astype(F32)[:8]
                outs[m][8 * high : 8 * high + 8, side * LANES : (side + 1) * LANES] = piece


def on_device(
    latents, cotangent, conv_kernel, conv_bias, norm_gain, w_query, w_key, w_value, w_output
):
    strips = lax.axis_size("azim")
    groups = lax.axis_size("sweep")
    cores = [(i, i ^ 1) for i in range(strips)]
    chips = [(i, (i + 1 if i % 2 else i - 1) % strips) for i in range(strips)]
    sides = [(i, i ^ 2) for i in range(strips)]
    strip = lax.axis_index("azim")
    spot = strip.astype(jnp.int32).reshape(1)
    predivide = 1.0 / math.sqrt(SL * groups * H * WL * strips)
    bias_row = conv_bias.reshape(1, C)
    gain_row = norm_gain.reshape(1, C)
    edge = pltpu.VMEM((SL, H, C), F32)

    one_edge = struct((SL, H, C), BF16)
    column = [pltpu.VMEM((2, SL, H, C), F32)]
    packed = struct((GROUPS, SL, PX, C), BF16)
    cot_sent = pl.pallas_call(
        pack_kernel,
        grid=(SL,),
        out_shape=packed,
        in_specs=[pl.BlockSpec((1, H, WL, C), lambda s: (s, 0, 0, 0))],
        out_specs=pl.BlockSpec((GROUPS, 1, PX, C), lambda s: (0, s, 0, 0)),
        compiler_params=params(56),
        cost_estimate=pl.CostEstimate(flops=0, bytes_accessed=1_000_000, transcendentals=0),
    )(cotangent)
    recv_cot = lax.all_to_all(cot_sent, "sweep", split_axis=0, concat_axis=0, tiled=True)
    to_chip = call(
        chip_edge_kernel, one_edge, 16, moved=600_000, smem=1, hbm=(1,), scratch=column
    )(spot, cot_sent, latents)
    other_chip = lax.ppermute(to_chip, "azim", chips)
    to_core, table = call(
        core_edge_kernel,
        (one_edge, struct((16, C), F32)),
        16,
        moved=600_000,
        smem=1,
        hbm=(1,),
        scratch=column,
    )(spot, to_chip, latents, conv_kernel, bias_row)
    other_core = lax.ppermute(to_core, "azim", cores)

    sent = call(
        forward_kernel,
        packed,
        16,
        flops=10_000_000,
        moved=1_000_000,
        smem=1,
        scratch=[edge, edge],
    )(spot, latents, other_core, other_chip, table)
    recv = lax.all_to_all(sent, "sweep", split_axis=0, concat_axis=0, tiled=True)

    rows = GROUPS * SL * PX
    grad_attn, halves, gain_sum = call(
        functools.partial(attend_kernel, predivide),
        (
            struct((GROUPS, SL, PX, C), BF16),
            struct((2, 2, GROUPS, ROWS, LANES), BF16),
            struct((1, C), F32),
        ),
        32,
        flops=2_000_000_000,
        moved=6_000_000,
        smem=1,
        scratch=[
            pltpu.VMEM((rows, C), BF16),
            pltpu.VMEM((rows, 3 * HD), BF16),
            pltpu.VMEM((rows, HD), BF16),
            pltpu.VMEM((rows, C), BF16),
            pltpu.VMEM((rows, C), F32),
            pltpu.VMEM((rows, LANES), F32),
            pltpu.VMEM((rows, 3 * HD), BF16),
            pltpu.VMEM((rows, HD), BF16),
            pltpu.VMEM((rows, C), F32),
        ],
    )(spot, recv, recv_cot, w_query, w_key, w_value, w_output, gain_row)
    ret = lax.all_to_all(grad_attn, "sweep", split_axis=0, concat_axis=0, tiled=True)
    from_core = lax.ppermute(halves[1], "azim", cores)
    piece = struct((GROUPS, ROWS, LANES), BF16)
    keep, send = call(add_cores_kernel, (piece, piece), 16, moved=2_000_000)(halves, from_core)
    from_chip = lax.ppermute(send, "azim", sides)
    payload = struct((GROUPS, ROWS + 16, LANES), BF16)
    sums = call(add_chips_kernel, payload, 16, moved=1_000_000)(keep, from_chip)

    vmem = pl.BlockSpec(memory_space=pltpu.VMEM)
    anywhere = pl.BlockSpec(memory_space=pltpu.HBM)
    first_sent = pl.pallas_call(
        functools.partial(taps_kernel, predivide),
        out_shape=payload,
        in_specs=[pl.BlockSpec(memory_space=pltpu.SMEM)] + [vmem] * 6 + [anywhere],
        out_specs=anywhere,
        input_output_aliases={7: 0},
        scratch_shapes=[
            edge,
            edge,
            pltpu.VMEM((GROUPS, 8, LANES), F32),
            pltpu.VMEM((GROUPS, 16, LANES), BF16),
            pltpu.SemaphoreType.DMA,
        ],
        compiler_params=params(16),
        cost_estimate=pl.CostEstimate(
            flops=10_000_000, bytes_accessed=2_000_000, transcendentals=0
        ),
    )(spot, latents, other_core, other_chip, cotangent, ret, gain_sum, sums)
    first_recv = lax.all_to_all(first_sent, "sweep", split_axis=0, concat_axis=0, tiled=True)
    second_sent = call(
        second_kernel, struct((strips, 16, LANES), BF16), 16, moved=1_000_000, smem=1
    )(spot, first_recv)
    second_recv = lax.all_to_all(second_sent, "azim", split_axis=0, concat_axis=0, tiled=True)

    both_edges = struct((2, SL, H, C), BF16)

    def back_edges(for_core, after):
        return call(
            functools.partial(back_edges_kernel, for_core),
            both_edges,
            16,
            moved=100_000,
            smem=1,
            hbm=(1,),
            scratch=[pltpu.VMEM((2, 2, SL, H, C), F32)],
        )(spot, after, cotangent, ret)

    to_core = back_edges(True, second_sent)
    back_core = lax.ppermute(to_core, "azim", cores)
    to_chip = back_edges(False, to_core)
    back_chip = lax.ppermute(to_chip, "azim", chips)

    grad_latents = pl.pallas_call(
        latents_kernel,
        out_shape=struct((SL, H, WL, C), F32),
        in_specs=[pl.BlockSpec(memory_space=pltpu.SMEM), anywhere] + [vmem] * 6,
        out_specs=anywhere,
        scratch_shapes=[edge, edge]
        + [pltpu.VMEM((SL, H, WL, C), F32), pltpu.SemaphoreType.DMA((SL * PARTS,))],
        compiler_params=params(16),
        cost_estimate=pl.CostEstimate(
            flops=10_000_000, bytes_accessed=4_000_000, transcendentals=0
        ),
    )(spot, second_sent, latents, cotangent, ret, back_core, back_chip, table)
    second_recv, grad_latents = lax.optimization_barrier((second_recv, grad_latents))

    third_sent = call(third_kernel, struct((GROUPS, 16, LANES), BF16), 16, moved=300_000)(
        second_recv
    )
    third_recv = lax.all_to_all(third_sent, "sweep", split_axis=0, concat_axis=0, tiled=True)

    share = struct((C // strips, HD), F32)
    line = struct((1, C), F32)
    grad_kernel, grad_bias, grad_gain, *shares = call(
        unpack_kernel,
        (struct((9, C), F32), line, line, share, share, share, share),
        16,
        moved=300_000,
    )(third_recv)
    return (
        grad_latents,
        grad_kernel,
        grad_bias.reshape(C),
        grad_gain.reshape(C),
        shares[0],
        shares[1],
        shares[2],
        shares[3],
    )


def solution(mesh):
    image = P("sweep", None, "azim", None)
    share = P("azim", None)
    return jax.shard_map(
        on_device,
        mesh=mesh,
        in_specs=(image, image, P(), P(), P(), P(), P(), P(), P()),
        out_specs=(image, P(), P(), P(), share, share, share, share),
        check_vma=False,
    )
```
